32 devices in a mesh: seq: 8 (over y, x, core), blk: 4 (over z).
Axes of the slice: x: 2, y: 2, z: 4, core: 2. Of those that a mesh axis runs over, the one named last changes fastest.
Arguments:
- tokens: float32 [4, 4096, 1024], P('blk', 'seq'), may hold values from -6 to 6
- seq_lengths: int32 [4, 4], P('blk'), may hold values from 64 to 3904, as said below
- ln_gain: float32 [2, 1024], replicated, may hold values from 0.5 to 1.5
- ln_bias: float32 [2, 1024], replicated, may hold values from -1.75 to 1.75
- w_one: bfloat16 [2, 1024, 3072], replicated, may hold values from -0.1875 to 0.1875
- w_two: bfloat16 [2, 1024, 512], replicated, may hold values from -0.1875 to 0.1875
- w_three: bfloat16 [2, 512, 3072], replicated, may hold values from -0.25 to 0.25
- w_four: bfloat16 [2, 3072, 1024], replicated, may hold values from -0.4375 to 0.4375
- readout: float32 [2, 512, 512], replicated, may hold values from -0.25 to 0.25
- log_rate: float32 [2, 512], replicated, as said below
- cotangent: float32 [4, 4096, 1024], P('blk', 'seq'), may hold values from -8 to 8
Outputs:
- result: float32 [4, 4096, 1024], P('blk', 'seq')
- grad_tokens: float32 [4, 4096, 1024], P('blk', 'seq')
- grad_gain: float32 [2, 1024], P(None, 'seq')
- grad_bias: float32 [2, 1024], P(None, 'seq')
- grad_one: float32 [2, 1024, 3072], P(None, None, 'seq')
- grad_two: float32 [2, 1024, 512], P(None, None, 'seq')
- grad_three: float32 [2, 512, 3072], P(None, None, 'seq')
- grad_four: float32 [2, 3072, 1024], P(None, None, 'seq')
- grad_readout: float32 [2, 512, 512], P(None, None, 'seq')
- grad_rate: float32 [2, 512], P(None, 'seq')
The draws below stay inside these ranges and needn't reach their ends.
Inputs may be any that keep to these rules, and one draw needn't show every extreme that they name: `seq_lengths`: row p holds the lengths of the 4 sequences laid end to end in pack p, first to last; every length is a multiple of 64, and a row sums to 4096. `log_rate`: every entry lies between log(0.02 / 4096) and log(1 / 30).
All inputs are finite; a program needn't handle non-finite values.
Results may differ from the reference program's by a relative error of at most 0.0069.
Values sent between devices are 32-bit elements; how exact they have to be, the bound alone decides.
No kernel may reach another device: no remote copies, remote signals or barrier semaphores. Data moves between devices by JAX's collectives and lax.ppermute only.
A program may use at most 448 MiB of HBM per device.

```python
import jax
import jax.numpy as jnp
from jax import lax

D = 1024
GATE = 3072
H = 512
N = 512
LAYERS = 2
BLOCK = 64
PACK = 4096
PACKS = 4


def draw_seq_lengths(key, part):
    key = jax.random.fold_in(key, 5)
    short_key, other_key, order_key = jax.random.split(key, 3)
    blocks = PACK // BLOCK
    short_one = jax.random.randint(short_key, (PACKS,), 1, 4).at[0].set(1)
    short_two = jax.random.randint(other_key, (PACKS,), 1, 4).at[0].set(1)
    single = jnp.ones((PACKS,), jnp.int32)
    longest = blocks - short_one - short_two - single
    length_table = jnp.stack([longest, short_one, single, short_two], axis=1)
    orders = jax.vmap(lambda subkey: jax.random.permutation(subkey, 4))(jax.random.split(order_key, PACKS))
    return (jnp.take_along_axis(length_table, orders, axis=1) * BLOCK).astype(jnp.int32)


def draw_log_rate(key, part):
    key = jax.random.fold_in(key, 9)
    floor_log = jnp.log(0.02 / PACK)
    ceiling_log = jnp.log(1.0 / 30.0)
    return jax.random.uniform(key, (LAYERS, N), jnp.float32, floor_log, ceiling_log)


def with_spikes(array, key, source, target, blocks, factor):
    owner, partner = [(jnp.arange(array.shape[dim]) // (array.shape[dim] // blocks)).reshape([-1 if axis == dim else 1 for axis in range(array.ndim)]) for dim in (source, target)]
    chosen = jax.random.permutation(key, blocks)[partner]
    strong = (owner == chosen) | (owner == (partner + blocks // 2) % blocks)
    return jnp.where(strong, factor * array, array)


def levels(rng, dims, cuts, smallest, top_value):
    gain = 1.0
    for position, shards_of in cuts:
        steps = jax.random.uniform(jax.random.fold_in(jax.random.fold_in(rng, 6), position), (shards_of,), jnp.float32, smallest / len(cuts), top_value / len(cuts))
        gain = gain * jnp.repeat(jnp.exp(steps), dims[position] // shards_of).reshape((-1,) + (1,) * (len(dims) - 1 - position))
    return gain


def centred(rng, extent, scale, bound, cuts=(), held_as=jnp.bfloat16):
    drawn = jax.random.normal(rng, extent, jnp.float32) * scale
    if len(cuts) > 0:
        drawn = levels(rng, extent, cuts, -0.22, 0.18) * drawn
    return jnp.clip(drawn, min=-bound, max=bound).astype(held_as)


def gaussian_with(stream_key, extent, width, most, cuts, heavy, kind=jnp.bfloat16):
    values = width * jax.random.normal(stream_key, extent, jnp.float32)
    if cuts:
        values = values * levels(stream_key, extent, cuts, -0.22, 0.18)
    return jnp.clip(with_spikes(values, jax.random.fold_in(stream_key, 3), *heavy), -most, most).astype(kind)


def setup_inputs(seed: int = 0) -> dict:
    key_list = jax.random.split(jax.random.key(seed), 12)
    return {
        "tokens": centred(key_list[0], (PACKS, PACK, D), 1.0, 6.0, ((0, 4), (1, 8)), jnp.float32),
        "seq_lengths": draw_seq_lengths(jax.random.fold_in(key_list[11], 71), 0),
        "ln_gain": jnp.clip(1.0 + 0.1 * jax.random.normal(key_list[2], (LAYERS, D), jnp.float32), 0.5, 1.5),
        "ln_bias": centred(key_list[3], (LAYERS, D), 0.3, 1.75, (), jnp.float32),
        "w_one": centred(key_list[4], (LAYERS, D, GATE), D ** -0.5, 0.1875),
        "w_two": centred(key_list[5], (LAYERS, D, H), D ** -0.5, 0.1875),
        "w_three": centred(key_list[6], (LAYERS, H, GATE), H ** -0.5, 0.25),
        "w_four": centred(key_list[7], (LAYERS, GATE, D), (GATE // 16) ** -0.5, 0.4375),
        "readout": centred(key_list[8], (LAYERS, H, N), N ** -0.5, 0.25, (), jnp.float32),
        "log_rate": draw_log_rate(jax.random.fold_in(key_list[11], 71), 0),
        "cotangent": gaussian_with(key_list[10], (PACKS, PACK, D), 1.0, 8.0, ((0, 4), (1, 8)), (1, 2, 8, 2.0), jnp.float32),
    }


@jax.custom_vjp
def low(v):
    return lax.optimization_barrier(v.astype(jnp.bfloat16)).astype(jnp.float32)

@jax.custom_vjp
def low_back(v):
    return v

def low_keep(v):
    return (low(v), None)

def low_pass(kept, grad):
    return (grad,)

def back_keep(v):
    return (v, None)

def back_low(kept, grad):
    return (low(grad),)
low.defvjp(low_keep, low_pass)
low_back.defvjp(back_keep, back_low)

def exact_dot(factor, second):
    return jnp.dot(factor, second, precision=lax.Precision.HIGHEST, preferred_element_type=jnp.float32)

def normalize(inputs, gain_row, shift_row):
    center = inputs - lax.optimization_barrier(jnp.mean(inputs, axis=-1, keepdims=True))
    spread = lax.optimization_barrier(jnp.mean(center * center, axis=-1, keepdims=True))
    return center * lax.rsqrt(spread + 1e-05) * gain_row + shift_row

def decay_tables(readout_layer, log_rates):
    decay_rates = jnp.exp(log_rates)
    decays = jnp.exp(-decay_rates)
    retain = -jnp.expm1(-decay_rates)
    lag_column = jnp.arange(BLOCK, dtype=jnp.float32)[:, None]
    powers = jnp.exp(-lag_column * decay_rates)
    endings = jnp.exp(-(BLOCK - 1.0 - lag_column) * decay_rates)
    carries = jnp.exp(-(lag_column + 1.0) * decay_rates)
    across = jnp.exp(-BLOCK * decay_rates)
    return (decay_rates, decays, retain, readout_layer * retain, powers, endings, carries, across)

def state_mix(values, openings, mixing, powers, endings, carries, across):
    mixing_cols = mixing.T
    kernel = exact_dot(powers, mixing_cols)
    offsets = jnp.arange(BLOCK, dtype=jnp.int32)[:, None] - jnp.arange(BLOCK, dtype=jnp.int32)[None, :]
    toeplitz = jnp.where((offsets >= 0)[:, :, None], kernel[jnp.clip(offsets, 0, BLOCK - 1)], 0.0)

    def advance(carried, inputs):
        segment, opening = inputs
        carried = jnp.where(opening, 0.0, carried)
        within = jnp.einsum('tsh,sh->th', toeplitz, segment, precision=lax.Precision.HIGHEST)
        from_before = exact_dot(carries, mixing_cols * carried)
        carried = across[:, None] * carried + exact_dot(endings.T, segment)
        return (carried, within + from_before)
    initial = jnp.zeros((N, H), jnp.float32)
    finish_state, mixed_out = lax.scan(jax.checkpoint(advance), initial, (values.reshape(-1, BLOCK, H), openings))
    return mixed_out.reshape(-1, H)

def pack_openings(seq_lengths):
    finish = jnp.cumsum(seq_lengths, axis=1)
    begins = finish - seq_lengths
    places = BLOCK * jnp.arange(PACK // BLOCK, dtype=jnp.int32)
    return jnp.any(begins[:, :, None] == places[None, None, :], axis=1)

def forward(tokens, ln_gain, ln_bias, w_one, w_two, w_three, w_four, readout, log_rate, openings):
    residual = tokens
    for layer_index in range(LAYERS):
        tables = decay_tables(readout[layer_index], log_rate[layer_index])
        flat_rows = residual.reshape(-1, D)
        normed = low(normalize(flat_rows, ln_gain[layer_index], ln_bias[layer_index]))
        gate_pre = low_back(exact_dot(normed, w_one[layer_index]))
        value_pre = low_back(exact_dot(normed, w_two[layer_index]))
        gate_acts = jax.nn.gelu(gate_pre)
        values = jax.nn.gelu(value_pre)

        def one_pack(inputs):
            return state_mix(inputs[0], inputs[1], tables[3], tables[4], tables[5], tables[6], tables[7])
        mixed_out = lax.map(one_pack, (values.reshape(PACKS, PACK, H), openings))
        mixed_out = low(mixed_out.reshape(-1, H))
        lifted = low_back(exact_dot(mixed_out, w_three[layer_index]))
        product = low(gate_acts * lifted)
        branch = low_back(exact_dot(product, w_four[layer_index]))
        residual = residual + branch.reshape(residual.shape)
    return residual

def reference(tokens, seq_lengths, ln_gain, ln_bias, w_one, w_two, w_three, w_four, readout, log_rate, cotangent):
    openings = pack_openings(seq_lengths)

    def wrapped(*params):
        return forward(*params, openings)
    result, pullback = jax.vjp(wrapped, tokens, ln_gain, ln_bias, w_one.astype(jnp.float32), w_two.astype(jnp.float32), w_three.astype(jnp.float32), w_four.astype(jnp.float32), readout, log_rate)
    gradients = pullback(cotangent)
    return (result, gradients[0], gradients[1], gradients[2], gradients[3], gradients[4], gradients[5], gradients[6], gradients[7], gradients[8])
```

```python
import functools

import numpy as np

import jax
import jax.numpy as jnp
from jax import lax
from jax.experimental import pallas as pl
from jax.experimental.pallas import tpu as pltpu
from jax.sharding import PartitionSpec as P

BLOCK = 64
FREQS = 64
LANES = 128
GELU_SCALE = float(np.sqrt(2.0 / np.pi))
GELU_CUBE = 0.044715
EXACT = lax.Precision.HIGHEST
VMEM_LIMIT = 48 * 1024 * 1024


def fourier_tables():
    angles = (2.0 * np.pi / (2 * BLOCK)) * (np.arange(FREQS) + 0.5)[:, None]

    def forward(places):
        return np.concatenate([np.cos(angles * places), -np.sin(angles * places)], axis=0)

    def inverse(places):
        return np.concatenate([np.cos(angles * places), -np.sin(angles * places)], axis=0).T / FREQS

    upper = np.arange(BLOCK)[None, :]
    lower = np.arange(-BLOCK, 0)[None, :]
    lower_forward = forward(lower)
    lower_forward[:, 0] = 0.0
    lower_inverse = inverse(lower)
    lower_inverse[0, :] = 0.0
    return tuple(
        np.asarray(table, np.float32)
        for table in (forward(upper), lower_forward, inverse(upper), lower_inverse)
    )


def dot_exact(first, second):
    return jnp.dot(first, second, precision=EXACT, preferred_element_type=jnp.float32)


def dot_first(first, second, precision=None):
    return lax.dot_general(
        first,
        second,
        (((0,), (0,)), ((), ())),
        precision=precision,
        preferred_element_type=jnp.float32,
    )


def dot_last(first, second, precision=None):
    return lax.dot_general(
        first,
        second,
        (((1,), (1,)), ((), ())),
        precision=precision,
        preferred_element_type=jnp.float32,
    )


def dot_plain(first, second, precision=None):
    return jnp.dot(first, second, precision=precision, preferred_element_type=jnp.float32)


def kernel_spectrum_body(powers_ref, mixing_ref, upper_ref, lower_ref, out_ref):
    blocks = out_ref.shape[0]
    lags = dot_exact(powers_ref[...], mixing_ref[...])
    for step in range(blocks):
        piece = dot_exact(upper_ref[...], lags[step * BLOCK : (step + 1) * BLOCK])
        if step > 0:
            piece = piece + dot_exact(lower_ref[...], lags[(step - 1) * BLOCK : step * BLOCK])
        out_ref[step] = piece


def kernel_spectrum(powers, mixing, upper, lower):
    tokens, states = powers.shape
    channels = mixing.shape[1]
    blocks = tokens // BLOCK
    return pl.pallas_call(
        kernel_spectrum_body,
        grid=(channels // LANES,),
        in_specs=[
            pl.BlockSpec((tokens, states), lambda i: (0, 0)),
            pl.BlockSpec((states, LANES), lambda i: (0, i)),
            pl.BlockSpec(upper.shape, lambda i: (0, 0)),
            pl.BlockSpec(lower.shape, lambda i: (0, 0)),
        ],
        out_specs=pl.BlockSpec((blocks, 2 * FREQS, LANES), lambda i: (0, 0, i)),
        out_shape=jax.ShapeDtypeStruct((blocks, 2 * FREQS, channels), jnp.float32),
        compiler_params=pltpu.CompilerParams(vmem_limit_bytes=VMEM_LIMIT),
        cost_estimate=pl.CostEstimate(
            flops=2 * 6 * tokens * states * channels,
            bytes_accessed=4 * (tokens * states + states * channels + 2 * tokens * channels),
            transcendentals=0,
        ),
        name="kernel_spectrum",
    )(powers, mixing, upper, lower)


def same_segment(segments_ref, first, second):
    return (segments_ref[first] == segments_ref[second]).astype(jnp.float32)


def conv_forward_body(segments_ref, values_ref, kernel_ref, upper_ref, inverse_ref, out_ref, spec_ref):
    blocks = kernel_ref.shape[0]
    for block in range(blocks):
        spec_ref[block] = dot_exact(
            upper_ref[...], values_ref[block * BLOCK : (block + 1) * BLOCK, :]
        )
    for block in range(blocks):
        real = jnp.zeros((FREQS, LANES), jnp.float32)
        imag = jnp.zeros((FREQS, LANES), jnp.float32)
        for source in range(block + 1):
            lag = block - source
            mask = same_segment(segments_ref, block, source)
            kernel_real = kernel_ref[lag, :FREQS] * mask
            kernel_imag = kernel_ref[lag, FREQS:] * mask
            value_real = spec_ref[source, :FREQS]
            value_imag = spec_ref[source, FREQS:]
            real = real + (kernel_real * value_real - kernel_imag * value_imag)
            imag = imag + (kernel_real * value_imag + kernel_imag * value_real)
        both = jnp.concatenate([real, imag], axis=0)
        out_ref[block * BLOCK : (block + 1) * BLOCK, :] = dot_exact(inverse_ref[...], both)


def conv_forward(segments, values, kernel, upper, inverse):
    tokens, channels = values.shape
    blocks = tokens // BLOCK
    return pl.pallas_call(
        conv_forward_body,
        grid=(channels // LANES,),
        in_specs=[
            pl.BlockSpec(memory_space=pltpu.SMEM),
            pl.BlockSpec((tokens, LANES), lambda i: (0, i)),
            pl.BlockSpec((blocks, 2 * FREQS, LANES), lambda i: (0, 0, i)),
            pl.BlockSpec(upper.shape, lambda i: (0, 0)),
            pl.BlockSpec(inverse.shape, lambda i: (0, 0)),
        ],
        out_specs=pl.BlockSpec((tokens, LANES), lambda i: (0, i)),
        out_shape=jax.ShapeDtypeStruct((tokens, channels), jnp.float32),
        scratch_shapes=[pltpu.VMEM((blocks, 2 * FREQS, LANES), jnp.float32)],
        compiler_params=pltpu.CompilerParams(vmem_limit_bytes=VMEM_LIMIT),
        cost_estimate=pl.CostEstimate(
            flops=2 * 1000 * tokens * channels,
            bytes_accessed=4 * 4 * tokens * channels,
            transcendentals=0,
        ),
        name="conv_forward",
    )(segments, values, kernel, upper, inverse)


def conv_backward_body(
    segments_ref,
    values_ref,
    grads_ref,
    kernel_ref,
    upper_ref,
    inverse_ref,
    lower_inverse_ref,
    out_ref,
    lags_ref,
    value_spec_ref,
    grad_spec_ref,
):
    blocks = kernel_ref.shape[0]
    for block in range(blocks):
        rows = slice(block * BLOCK, (block + 1) * BLOCK)
        value_spec_ref[block] = dot_exact(upper_ref[...], values_ref[rows, :])
        grad_spec_ref[block] = dot_exact(upper_ref[...], grads_ref[rows, :])
    for source in range(blocks):
        real = jnp.zeros((FREQS, LANES), jnp.float32)
        imag = jnp.zeros((FREQS, LANES), jnp.float32)
        for block in range(source, blocks):
            lag = block - source
            mask = same_segment(segments_ref, block, source)
            kernel_real = kernel_ref[lag, :FREQS] * mask
            kernel_imag = kernel_ref[lag, FREQS:] * mask
            grad_real = grad_spec_ref[block, :FREQS]
            grad_imag = grad_spec_ref[block, FREQS:]
            real = real + (kernel_real * grad_real + kernel_imag * grad_imag)
            imag = imag + (kernel_real * grad_imag - kernel_imag * grad_real)
        both = jnp.concatenate([real, imag], axis=0)
        out_ref[source * BLOCK : (source + 1) * BLOCK, :] = dot_exact(inverse_ref[...], both)
    for lag in range(blocks):
        real = jnp.zeros((FREQS, LANES), jnp.float32)
        imag = jnp.zeros((FREQS, LANES), jnp.float32)
        for source in range(blocks - lag):
            block = source + lag
            mask = same_segment(segments_ref, block, source)
            grad_real = grad_spec_ref[block, :FREQS] * mask
            grad_imag = grad_spec_ref[block, FREQS:] * mask
            value_real = value_spec_ref[source, :FREQS]
            value_imag = value_spec_ref[source, FREQS:]
            real = real + (grad_real * value_real + grad_imag * value_imag)
            imag = imag + (grad_imag * value_real - grad_real * value_imag)
        both = jnp.concatenate([real, imag], axis=0)
        rows = slice(lag * BLOCK, (lag + 1) * BLOCK)
        lags_ref[rows, :] = dot_exact(inverse_ref[...], both)
        if lag > 0:
            rows = slice((lag - 1) * BLOCK, lag * BLOCK)
            lags_ref[rows, :] += dot_exact(lower_inverse_ref[...], both)


def conv_backward(segments, values, grads, kernel, upper, inverse, lower_inverse):
    tokens, channels = values.shape
    blocks = tokens // BLOCK
    shape = jax.ShapeDtypeStruct((tokens, channels), jnp.float32)
    tall = pl.BlockSpec((tokens, LANES), lambda i: (0, i))
    return pl.pallas_call(
        conv_backward_body,
        grid=(channels // LANES,),
        in_specs=[
            pl.BlockSpec(memory_space=pltpu.SMEM),
            tall,
            tall,
            pl.BlockSpec((blocks, 2 * FREQS, LANES), lambda i: (0, 0, i)),
            pl.BlockSpec(upper.shape, lambda i: (0, 0)),
            pl.BlockSpec(inverse.shape, lambda i: (0, 0)),
            pl.BlockSpec(lower_inverse.shape, lambda i: (0, 0)),
        ],
        out_specs=[tall, tall],
        out_shape=[shape, shape],
        scratch_shapes=[pltpu.VMEM((blocks, 2 * FREQS, LANES), jnp.float32)] * 2,
        compiler_params=pltpu.CompilerParams(vmem_limit_bytes=VMEM_LIMIT),
        cost_estimate=pl.CostEstimate(
            flops=2 * 2000 * tokens * channels,
            bytes_accessed=4 * 6 * tokens * channels,
            transcendentals=0,
        ),
        name="conv_backward",
    )(segments, values, grads, kernel, upper, inverse, lower_inverse)


def weight_grad_body(place_ref, first_ref, second_ref, send_ref, keep_ref):
    width = keep_ref.shape[-1]
    both = lax.dot_general(
        first_ref[...],
        second_ref[...],
        (((0,), (0,)), ((), ())),
        preferred_element_type=jnp.float32,
    )
    core = place_ref[1]

    @pl.when(core == 0)
    def _():
        keep_ref[0] = both[:, :width]
        send_ref[0] = both[:, width:]

    @pl.when(core != 0)
    def _():
        keep_ref[0] = both[:, width:]
        send_ref[0] = both[:, :width]


def weight_grad(place, first, second, chips):
    tokens, rows = first.shape
    pair = second.shape[1] // chips
    width = pair // 2
    out = jax.ShapeDtypeStruct((chips, rows, width), jnp.float32)
    return pl.pallas_call(
        weight_grad_body,
        grid_spec=pltpu.PrefetchScalarGridSpec(
            num_scalar_prefetch=1,
            grid=(chips,),
            in_specs=[
                pl.BlockSpec((tokens, rows), lambda j, place: (0, 0)),
                pl.BlockSpec((tokens, pair), lambda j, place: (0, jnp.bitwise_xor(j, place[0]))),
            ],
            out_specs=[
                pl.BlockSpec((1, rows, width), lambda j, place: (j, 0, 0)),
                pl.BlockSpec((1, rows, width), lambda j, place: (j, 0, 0)),
            ],
        ),
        out_shape=[out, out],
        compiler_params=pltpu.CompilerParams(vmem_limit_bytes=VMEM_LIMIT),
        cost_estimate=pl.CostEstimate(
            flops=2 * tokens * rows * second.shape[1],
            bytes_accessed=2 * tokens * (rows + second.shape[1]) + 4 * rows * second.shape[1],
            transcendentals=0,
        ),
        name="weight_grad",
    )(place, first, second)


def flip_with(axis, bit):
    count = lax.axis_size(axis)
    pairs = [(device, device ^ bit) for device in range(count)]
    return lambda array: lax.ppermute(array, axis, pairs)


def by_core(core, zero, one):
    return jnp.where(core == 0, zero, one)


def prefix_join(prefix, partner, order, reach, factors):
    chips = factors.shape[0]
    places = jnp.arange(chips)
    start = (order // reach) * reach
    ahead = (places >= start) & (places < order)
    passed = jnp.prod(jnp.where(ahead[:, None], factors, 1.0), axis=0)
    return prefix + passed[:, None] * partner


def chip_scan_general(total, factors, order, chips):
    prefix = jnp.zeros_like(total)
    level = factors
    reach = 1
    while reach < chips:
        partner = flip_with("seq", 2 * reach)(total)
        group = order // reach
        sibling = lax.dynamic_index_in_dim(level, group ^ 1, 0, keepdims=False)
        mine = lax.dynamic_index_in_dim(level, group, 0, keepdims=False)
        late = (group % 2) == 1
        prefix = jnp.where(late, prefix_join(prefix, partner, order, reach, factors), prefix)
        total = jnp.where(late, mine[:, None] * partner + total, sibling[:, None] * total + partner)
        level = level[0::2] * level[1::2]
        reach *= 2
    return prefix


def chip_scan_square(total, factors, order):
    half = total.shape[0] // 2
    first, second = total[:half], total[half:]
    first_factors, second_factors = factors[:, :half], factors[:, half:]
    along_x, along_y = flip_with("seq", 2), flip_with("seq", 4)
    place_x, place_y = order % 2, order // 2

    def column(table, index):
        return lax.dynamic_index_in_dim(table, index, 0, keepdims=False)[:, None]

    first_x = along_x(first)
    second_y = along_y(second)
    row = jnp.where(
        place_x == 0,
        column(first_factors, order ^ 1) * first + first_x,
        column(first_factors, order) * first_x + first,
    )
    first_y = along_y(row)
    passed = jnp.where(place_x == 1, column(first_factors, order ^ 1), 1.0)
    first_prefix = jnp.where(place_x == 1, first_x, 0.0) + jnp.where(
        place_y == 1, passed * first_y, 0.0
    )
    above_one = second_factors[1][:, None]
    below_zero = second_factors[2][:, None]
    outgoing = jnp.where(
        place_y == 0,
        second,
        jnp.where(place_x == 0, below_zero * above_one * second_y + second, second_y),
    )
    second_x = along_x(outgoing)
    upper_prefix = jnp.where(place_x == 1, second_x, 0.0)
    lower_prefix = jnp.where(
        place_x == 0, above_one * second_y + second_x, second_x + below_zero * second_y
    )
    second_prefix = jnp.where(place_y == 0, upper_prefix, lower_prefix)
    return jnp.concatenate([first_prefix, second_prefix], axis=0)


def carry(state, factors, order, core):
    devices = factors.shape[0]
    chips = devices // 2
    half = state.shape[0] // 2
    swap = flip_with("seq", 1)
    place = order % 2
    received = swap(state[half:])
    own = state[:half]
    early = jnp.where(place == 0, own, received)
    late = jnp.where(place == 0, received, own)
    mine_factors = factors[:, :half]
    late_factor = lax.dynamic_index_in_dim(mine_factors, order | 1, 0, keepdims=False)[:, None]
    early_factor = lax.dynamic_index_in_dim(mine_factors, (order | 1) ^ 1, 0, keepdims=False)[:, None]
    total = late_factor * early + late
    chip_factors = mine_factors[0::2] * mine_factors[1::2]
    if chips == 4:
        entering = chip_scan_square(total, chip_factors, order // 2)
    else:
        entering = chip_scan_general(total, chip_factors, order // 2, chips)
    middle = early_factor * entering + early
    keep = jnp.where(place == 0, entering, middle)
    send = jnp.where(place == 0, middle, entering)
    return jnp.concatenate([keep, swap(send)], axis=0)


def sum_line(array):
    place = lax.axis_index("blk")
    inner = array + lax.ppermute(array, "blk", [(0, 1), (3, 2)])
    total = inner + lax.ppermute(inner, "blk", [(1, 2), (2, 1)])
    outer = lax.ppermute(total, "blk", [(1, 0), (2, 3)])
    return jnp.where((place == 1) | (place == 2), total, outer)


def reduce_square(send, keep):
    swap, along_x, along_y = flip_with("seq", 1), flip_with("seq", 2), flip_with("seq", 4)
    half = keep.shape[1] // 16 * 8
    got = swap(send)
    first_x = along_x(keep[1::2, :half] + got[1::2, :half])
    second_y = along_y(keep[2:, half:] + got[2:, half:])
    first_y = along_y(keep[2, :half] + got[2, :half] + first_x[1])
    second_x = along_x(keep[1, half:] + got[1, half:] + second_y[1])
    first = keep[0, :half] + got[0, :half] + first_x[0] + first_y
    second = keep[0, half:] + got[0, half:] + second_y[0] + second_x
    return sum_line(jnp.concatenate([first, second], axis=0))


def reduce_general(array, axis):
    share = lax.psum_scatter(array, "seq", scatter_dimension=axis, tiled=True)
    return lax.psum(share, "blk")


def gelu_parts(inputs):
    square = inputs * inputs
    bent = jnp.tanh(GELU_SCALE * inputs * (1.0 + GELU_CUBE * square))
    half = 0.5 * (1.0 + bent)
    slope = half + 0.5 * inputs * (1.0 - bent * bent) * GELU_SCALE * (
        1.0 + 3.0 * GELU_CUBE * square
    )
    return inputs * half, slope


def gelu(inputs):
    return gelu_parts(inputs)[0]


def body(
    tokens,
    seq_lengths,
    ln_gain,
    ln_bias,
    w_one,
    w_two,
    w_three,
    w_four,
    readout,
    log_rate,
    cotangent,
):
    _, span, width = tokens.shape
    layers = w_one.shape[0]
    channels, states = readout.shape[1:]
    blocks = span // BLOCK
    devices = lax.axis_size("seq")
    chips = devices // 2
    me = lax.axis_index("seq")
    core = me % 2
    chip = me // 2
    custom = chips == 4 and lax.axis_size("blk") == 4
    place = jnp.stack([chip, core]).astype(jnp.int32)
    upper, lower, inverse, lower_inverse = (jnp.asarray(table) for table in fourier_tables())

    finish = jnp.cumsum(seq_lengths[0])
    begins = finish - seq_lengths[0]
    places = BLOCK * jnp.arange(devices * blocks, dtype=jnp.int32)
    opens = jnp.any(begins[:, None] == places[None, :], axis=0).reshape(devices, blocks)
    unbroken = jnp.logical_not(jnp.any(opens, axis=1))
    own_opens = lax.dynamic_index_in_dim(opens, me, 0, keepdims=False)
    segments = jnp.cumsum(own_opens.astype(jnp.int32))
    from_before = jnp.repeat((segments == 0).astype(jnp.float32), BLOCK)[:, None]
    to_after = jnp.repeat((segments == segments[-1]).astype(jnp.float32), BLOCK)[:, None]
    unbroken = unbroken.astype(jnp.float32)
    own_unbroken = (segments[-1] == 0).astype(jnp.float32)

    half = states // 2

    def turned(array):
        return by_core(core, array, jnp.concatenate([array[half:], array[:half]], axis=0))

    steps = jnp.arange(span, dtype=jnp.float32)[:, None]

    def tables(layer):
        log_row = log_rate[layer]
        rates = jnp.exp(log_row)
        retain = -jnp.expm1(-rates)
        turned_rates = turned(rates)
        row = turned_rates[None, :]
        mixing = turned((readout[layer] * retain).T)
        powers = jnp.exp(-steps * row)
        return dict(
            rates=rates,
            decays=jnp.exp(-rates),
            retain=retain,
            mixing=mixing,
            powers=powers,
            slopes=steps * jnp.exp(-(steps - 1.0) * row),
            entering=from_before * jnp.exp(-(steps + 1.0) * row),
            entering_slopes=from_before * (steps + 1.0) * powers,
            leaving=to_after * jnp.exp(-(span - 1.0 - steps) * row),
            leaving_slopes=to_after
            * (span - 1.0 - steps)
            * jnp.exp(-(span - 2.0 - steps) * row),
            through_slope=own_unbroken * span * jnp.exp(-(span - 1.0) * turned_rates),
            factors=unbroken[:, None] * jnp.exp(-span * row),
            kernel=kernel_spectrum(powers, mixing, upper, lower),
        )

    def before_carry(layer, flat, table):
        mean = jnp.mean(flat, axis=-1, keepdims=True)
        center = flat - mean
        scale = lax.rsqrt(jnp.mean(center * center, axis=-1, keepdims=True) + 1e-05)
        normed = (center * scale * ln_gain[layer] + ln_bias[layer]).astype(jnp.bfloat16)
        value_pre = dot_plain(normed, w_two[layer])
        values = gelu(value_pre)
        state = dot_first(table["leaving"], values)
        incoming = carry(state, table["factors"], me, core)
        gate_pre = dot_plain(normed, w_one[layer])
        local = conv_forward(segments, values, table["kernel"], upper, inverse)
        mixed = (local + dot_plain(table["entering"], table["mixing"] * incoming)).astype(
            jnp.bfloat16
        )
        lifted = dot_plain(mixed, w_three[layer])
        product = (gelu(gate_pre) * lifted).astype(jnp.bfloat16)
        branch = dot_plain(product, w_four[layer])
        saved = dict(
            flat=flat,
            mean=mean,
            scale=scale,
            normed=normed,
            value_pre=value_pre,
            values=values,
            incoming=incoming,
            gate_pre=gate_pre,
            mixed=mixed,
            lifted=lifted,
            product=product,
        )
        return flat + branch, saved

    def share_grad(first, second):
        if custom:
            return weight_grad(place, first, second, chips)
        return dot_first(first, second)

    def backward(layer, upstream, table, kept):
        low = upstream.astype(jnp.bfloat16)
        grad_product = dot_last(low, w_four[layer])
        acts, slope = gelu_parts(kept["gate_pre"])
        grad_lifted = (grad_product * acts).astype(jnp.bfloat16)
        grad_mixed = dot_last(grad_lifted, w_three[layer])
        pulled = dot_first(table["entering"], grad_mixed)
        adjoint = carry(
            table["mixing"] * pulled, table["factors"][::-1], devices - 1 - me, core
        )
        four = share_grad(kept["product"], low)
        three = share_grad(kept["mixed"], grad_lifted)
        local, lag_sums = conv_backward(
            segments, kept["values"], grad_mixed, table["kernel"], upper, inverse, lower_inverse
        )
        grad_values = local + dot_plain(table["leaving"], adjoint)
        value_slope = gelu_parts(kept["value_pre"])[1]
        grad_value_pre = (grad_values * value_slope).astype(jnp.bfloat16)
        grad_gate_pre = (grad_product * kept["lifted"] * slope).astype(jnp.bfloat16)
        one = share_grad(kept["normed"], grad_gate_pre)
        two = dot_first(grad_value_pre, kept["normed"])
        grad_normed = dot_last(grad_gate_pre, w_one[layer]) + dot_last(
            grad_value_pre, w_two[layer]
        )
        hat = (kept["flat"] - kept["mean"]) * kept["scale"]
        gain_grad = jnp.sum(grad_normed * hat, axis=0)
        bias_grad = jnp.sum(grad_normed, axis=0)
        scaled = grad_normed * ln_gain[layer]
        grad_flat = upstream + kept["scale"] * (
            scaled
            - jnp.mean(scaled, axis=-1, keepdims=True)
            - hat * jnp.mean(scaled * hat, axis=-1, keepdims=True)
        )
        incoming = kept["incoming"]
        grad_mixing = dot_first(table["powers"], lag_sums) + incoming * pulled
        grad_decays = jnp.sum(
            table["mixing"]
            * (
                dot_first(table["slopes"], lag_sums)
                + incoming * dot_first(table["entering_slopes"], grad_mixed)
            )
            + adjoint * dot_first(table["leaving_slopes"], kept["values"])
            + table["through_slope"][:, None] * incoming * adjoint,
            axis=1,
        )
        grad_mixing = turned(grad_mixing)
        grad_retain = jnp.sum(grad_mixing * readout[layer].T, axis=1)
        grad_rate = table["rates"] * table["decays"] * (grad_retain - turned(grad_decays))
        grad_readout = grad_mixing * table["retain"][:, None]

        def lines(array):
            return array.reshape(devices, -1, array.shape[-1])

        rows = lines(two).shape[1]
        extra = jnp.concatenate(
            [part.reshape(devices, 1, -1) for part in (gain_grad, bias_grad, grad_rate)], axis=-1
        )
        wide = jnp.concatenate([lines(two), lines(grad_readout)], axis=-1)
        extra = jnp.pad(extra, ((0, 0), (0, 7), (0, wide.shape[-1] - extra.shape[-1])))
        small = jnp.concatenate([wide, extra], axis=1)
        if custom:
            small = small.reshape(chips, 2, rows + 8, wide.shape[-1])
            small = jnp.stack(
                [lax.dynamic_index_in_dim(small, chip ^ j, 0, keepdims=False) for j in range(chips)]
            )
            small = by_core(core, small, small[:, ::-1])
            shares = [reduce_square(*pair) for pair in (four, three, one)]
            shares.append(reduce_square(small[:, 1], small[:, 0]))
        else:
            shares = [reduce_general(array, 1) for array in (four, three, one)]
            shares.append(reduce_general(small, 0)[0])
        return grad_flat, shares

    all_tables = [tables(layer) for layer in range(layers)]
    flat = tokens.reshape(span, width)
    saved = []
    for layer in range(layers):
        flat, kept = before_carry(layer, flat, all_tables[layer])
        saved.append(kept)
    upstream = cotangent.reshape(span, width)
    collected = [None] * layers
    for layer in reversed(range(layers)):
        upstream, collected[layer] = backward(layer, upstream, all_tables[layer], saved[layer])

    def unpack(shares):
        four, three, one, small = shares
        rows = small.shape[0] - 8
        gains = width // devices
        rate_width = states // devices
        return (
            small[rows, :gains],
            small[rows, gains : 2 * gains],
            one,
            small[:rows, :width].T,
            three,
            four,
            small[:rows, width:].T,
            small[rows, 2 * gains : 2 * gains + rate_width],
        )

    parts = [unpack(shares) for shares in collected]
    stacked = [jnp.stack([part[member] for part in parts]) for member in range(8)]
    return (flat[None], upstream[None], *stacked)


def solution(mesh):
    placed = (
        P("blk", "seq", None),
        P("blk", None),
        P(),
        P(),
        P(),
        P(),
        P(),
        P(),
        P(),
        P(),
        P("blk", "seq", None),
    )
    return jax.shard_map(
        body,
        mesh=mesh,
        in_specs=placed,
        out_specs=(
            P("blk", "seq", None),
            P("blk", "seq", None),
            P(None, "seq"),
            P(None, "seq"),
            P(None, None, "seq"),
            P(None, None, "seq"),
            P(None, None, "seq"),
            P(None, None, "seq"),
            P(None, None, "seq"),
            P(None, "seq"),
        ),
        check_vma=False,
    )
```

```python
import functools

import numpy as np

import jax
import jax.numpy as jnp
from jax import lax
from jax.experimental import pallas as pl
from jax.experimental.pallas import tpu as pltpu
from jax.sharding import PartitionSpec as P

BLOCK = 64
FREQS = 64
LANES = 128
GELU_SCALE = float(np.sqrt(2.0 / np.pi))
GELU_CUBE = 0.044715
MEBI = 1024 * 1024

SEQ = ("chip", "core")

ORDER = (
    "gate1", "slope1", "b1", "grad_four1", "grad_three1", "b1", "four1", "three1", "grad_one1", "one1",
    "three1", "b1", "conv1", "one1", "value1", "close1", "three1", "gate0", "grad_four0", "one1", "pull0",
    "three1", "b0", "grad_one0", "one1", "b0", "four0", "one0", "conv0", "four0", "b0", "three1", "one0",
    "lines1", "b0", "four1", "grad_three0", "four0", "one1", "value0", "four1", "three1", "four0", "close0",
    "lines0", "lines", "three1", "one0", "three0", "one1", "small", "four0", "four1", "three0", "small",
    "one0", "four0", "small", "one1", "one0", "three0", "small", "three0", "one0", "small", "four1", "four0",
    "three0", "small", "one0", "three0", "small", "result", "three0",
)
GROUPS = ()
ALONG_X = ()
ALONG_Y = ()
FAR = ("four1",)
PARTS = ("four1", "one1", "four0", "one0")


def fourier_tables():
    angles = (2.0 * np.pi / (2 * BLOCK)) * (np.arange(FREQS) + 0.5)[:, None]

    def forward(places):
        return np.concatenate([np.cos(angles * places), -np.sin(angles * places)], axis=0)

    def parts(table):
        table = np.asarray(table, np.float32)
        high = table.astype(jnp.bfloat16)
        rest = (table - high.astype(np.float32)).astype(jnp.bfloat16)
        return jnp.asarray(np.concatenate([high, high, rest], axis=1))

    upper = forward(np.arange(BLOCK)[None, :])
    lower = forward(np.arange(-BLOCK, 0)[None, :])
    lower[:, 0] = 0.0
    return (
        parts(upper),
        parts(np.concatenate([lower, upper], axis=1)),
        parts(upper.T / FREQS),
        parts(lower.T / FREQS),
    )


def three_parts(array):
    high = array.astype(jnp.bfloat16)
    rest = (array - high.astype(jnp.float32)).astype(jnp.bfloat16)
    return jnp.concatenate([high, rest, high], axis=0)


def beside(array, blocks):
    return jnp.concatenate(
        [array[block * BLOCK : (block + 1) * BLOCK] for block in range(blocks)], axis=1
    )


def dot_first(first, second, precision=None):
    return lax.dot_general(
        first,
        second,
        (((0,), (0,)), ((), ())),
        precision=precision,
        preferred_element_type=jnp.float32,
    )


def dot_last(first, second, precision=None):
    return lax.dot_general(
        first,
        second,
        (((1,), (1,)), ((), ())),
        precision=precision,
        preferred_element_type=jnp.float32,
    )


def dot_plain(first, second, precision=None):
    return jnp.dot(first, second, precision=precision, preferred_element_type=jnp.float32)


def layer_kernel_body(core_ref, readout_ref, rates_ref, retain_ref, window_ref, upright_ref, out_ref):
    blocks = out_ref.shape[0]
    tokens = blocks * BLOCK
    half = readout_ref.shape[1] // 2
    rates = rates_ref[...]
    decaying = jnp.exp(
        -lax.broadcasted_iota(jnp.int32, (tokens, 1), 0).astype(jnp.float32) * rates
    ).astype(jnp.bfloat16)
    readout = readout_ref[...]
    lags = dot_last(decaying, (readout * retain_ref[...]).astype(jnp.bfloat16))
    padded = jnp.concatenate([jnp.zeros((BLOCK, lags.shape[1]), jnp.float32), lags], axis=0)
    for step in range(blocks):
        window = padded[step * BLOCK : (step + 2) * BLOCK]
        out_ref[step] = dot_plain(window_ref[...], three_parts(window))
    upright = readout.T
    swapped = jnp.concatenate([upright[half:], upright[:half]], axis=0)
    upright_ref[...] = jnp.where(core_ref[0] == 0, upright, swapped)


def layer_kernel(layer, core, readout, rates, retain, window, tokens):
    _, channels, states = readout.shape
    blocks = tokens // BLOCK
    wide = 2 * LANES
    row = pl.BlockSpec((1, states), lambda i: (0, 0))
    return pl.pallas_call(
        layer_kernel_body,
        grid=(channels // wide,),
        in_specs=[
            pl.BlockSpec(memory_space=pltpu.SMEM),
            pl.BlockSpec((None, wide, states), lambda i: (layer, i, 0)),
            row,
            row,
            pl.BlockSpec(window.shape, lambda i: (0, 0)),
        ],
        out_specs=[
            pl.BlockSpec((states, wide), lambda i: (0, i)),
            pl.BlockSpec((blocks, 2 * FREQS, wide), lambda i: (0, 0, i)),
        ],
        out_shape=[
            jax.ShapeDtypeStruct((states, channels), jnp.float32),
            jax.ShapeDtypeStruct((blocks, 2 * FREQS, channels), jnp.float32),
        ],
        compiler_params=pltpu.CompilerParams(vmem_limit_bytes=12 * MEBI),
        cost_estimate=pl.CostEstimate(
            flops=8 * tokens * states * channels, bytes_accessed=8 * (states + tokens) * channels, transcendentals=0
        ),
        name="layer_kernel",
    )(core, readout, rates, retain, window)


def same_segment(segments_ref, first, second):
    return (segments_ref[first] == segments_ref[second]).astype(jnp.float32)


def keep_blocks(ref, array):
    for block in range(ref.shape[0]):
        ref[block] = array[:, block * LANES : (block + 1) * LANES]


def conv_forward_body(segments_ref, values_ref, kernel_ref, upper_ref, inverse_ref, out_ref, spec_ref):
    blocks = kernel_ref.shape[0]
    keep_blocks(spec_ref, dot_plain(upper_ref[...], three_parts(beside(values_ref[...], blocks))))
    sums = []
    for block in range(blocks):
        real = jnp.zeros((FREQS, LANES), jnp.float32)
        imag = jnp.zeros((FREQS, LANES), jnp.float32)
        for source in range(block + 1):
            lag = block - source
            mask = same_segment(segments_ref, block, source)
            kernel_real = kernel_ref[lag, :FREQS] * mask
            kernel_imag = kernel_ref[lag, FREQS:] * mask
            value_real = spec_ref[source, :FREQS]
            value_imag = spec_ref[source, FREQS:]
            real = real + (kernel_real * value_real - kernel_imag * value_imag)
            imag = imag + (kernel_real * value_imag + kernel_imag * value_real)
        sums.append(jnp.concatenate([real, imag], axis=0))
    out = dot_plain(inverse_ref[...], three_parts(jnp.concatenate(sums, axis=1)))
    for block in range(blocks):
        out_ref[block * BLOCK : (block + 1) * BLOCK, :] = out[:, block * LANES : (block + 1) * LANES]


def conv_forward(segments, values, kernel, upper, inverse):
    tokens, channels = values.shape
    blocks = tokens // BLOCK
    return pl.pallas_call(
        conv_forward_body,
        grid=(channels // LANES,),
        in_specs=[
            pl.BlockSpec(memory_space=pltpu.SMEM),
            pl.BlockSpec((tokens, LANES), lambda i: (0, i)),
            pl.BlockSpec((blocks, 2 * FREQS, LANES), lambda i: (0, 0, i)),
            pl.BlockSpec(upper.shape, lambda i: (0, 0)),
            pl.BlockSpec(inverse.shape, lambda i: (0, 0)),
        ],
        out_specs=pl.BlockSpec((tokens, LANES), lambda i: (0, i)),
        out_shape=jax.ShapeDtypeStruct((tokens, channels), jnp.float32),
        scratch_shapes=[pltpu.VMEM((blocks, 2 * FREQS, LANES), jnp.float32)],
        compiler_params=pltpu.CompilerParams(vmem_limit_bytes=10 * MEBI),
        cost_estimate=pl.CostEstimate(
            flops=2000 * tokens * channels, bytes_accessed=16 * tokens * channels, transcendentals=0
        ),
        name="conv_forward",
    )(segments, values, kernel, upper, inverse)


def conv_backward_body(
    segments_ref,
    values_ref,
    grads_ref,
    kernel_ref,
    upper_ref,
    inverse_ref,
    lower_inverse_ref,
    out_ref,
    lags_ref,
    value_spec_ref,
    grad_spec_ref,
):
    blocks = kernel_ref.shape[0]
    for spec_ref, in_ref in ((value_spec_ref, values_ref), (grad_spec_ref, grads_ref)):
        keep_blocks(spec_ref, dot_plain(upper_ref[...], three_parts(beside(in_ref[...], blocks))))
    sums = []
    for source in range(blocks):
        real = jnp.zeros((FREQS, LANES), jnp.float32)
        imag = jnp.zeros((FREQS, LANES), jnp.float32)
        for block in range(source, blocks):
            lag = block - source
            mask = same_segment(segments_ref, block, source)
            kernel_real = kernel_ref[lag, :FREQS] * mask
            kernel_imag = kernel_ref[lag, FREQS:] * mask
            grad_real = grad_spec_ref[block, :FREQS]
            grad_imag = grad_spec_ref[block, FREQS:]
            real = real + (kernel_real * grad_real + kernel_imag * grad_imag)
            imag = imag + (kernel_real * grad_imag - kernel_imag * grad_real)
        sums.append(jnp.concatenate([real, imag], axis=0))
    out = dot_plain(inverse_ref[...], three_parts(jnp.concatenate(sums, axis=1)))
    for block in range(blocks):
        out_ref[block * BLOCK : (block + 1) * BLOCK, :] = out[:, block * LANES : (block + 1) * LANES]
    sums = []
    for lag in range(blocks):
        real = jnp.zeros((FREQS, LANES), jnp.float32)
        imag = jnp.zeros((FREQS, LANES), jnp.float32)
        for source in range(blocks - lag):
            block = source + lag
            mask = same_segment(segments_ref, block, source)
            grad_real = grad_spec_ref[block, :FREQS] * mask
            grad_imag = grad_spec_ref[block, FREQS:] * mask
            value_real = value_spec_ref[source, :FREQS]
            value_imag = value_spec_ref[source, FREQS:]
            real = real + (grad_real * value_real + grad_imag * value_imag)
            imag = imag + (grad_imag * value_real - grad_real * value_imag)
        sums.append(jnp.concatenate([real, imag], axis=0))
    parts = three_parts(jnp.concatenate(sums, axis=1))
    here = dot_plain(inverse_ref[...], parts)
    behind = dot_plain(lower_inverse_ref[...], parts)
    for lag in range(blocks):
        lags = here[:, lag * LANES : (lag + 1) * LANES]
        if lag + 1 < blocks:
            lags = lags + behind[:, (lag + 1) * LANES : (lag + 2) * LANES]
        lags_ref[lag * BLOCK : (lag + 1) * BLOCK, :] = lags


def conv_backward(segments, values, grads, kernel, upper, inverse, lower_inverse):
    tokens, channels = values.shape
    blocks = tokens // BLOCK
    shape = jax.ShapeDtypeStruct((tokens, channels), jnp.float32)
    tall = pl.BlockSpec((tokens, LANES), lambda i: (0, i))
    return pl.pallas_call(
        conv_backward_body,
        grid=(channels // LANES,),
        in_specs=[
            pl.BlockSpec(memory_space=pltpu.SMEM),
            tall,
            tall,
            pl.BlockSpec((blocks, 2 * FREQS, LANES), lambda i: (0, 0, i)),
            pl.BlockSpec(upper.shape, lambda i: (0, 0)),
            pl.BlockSpec(inverse.shape, lambda i: (0, 0)),
            pl.BlockSpec(lower_inverse.shape, lambda i: (0, 0)),
        ],
        out_specs=[tall, tall],
        out_shape=[shape, shape],
        scratch_shapes=[pltpu.VMEM((blocks, 2 * FREQS, LANES), jnp.float32)] * 2,
        compiler_params=pltpu.CompilerParams(vmem_limit_bytes=12 * MEBI),
        cost_estimate=pl.CostEstimate(
            flops=4000 * tokens * channels, bytes_accessed=24 * tokens * channels, transcendentals=0
        ),
        name="conv_backward",
    )(segments, values, grads, kernel, upper, inverse, lower_inverse)


def weight_grad_body(place_ref, first_ref, second_ref, *out_refs):
    width = out_refs[0].shape[-1]
    second = second_ref[...]
    turned = jnp.concatenate([second[:, width:], second[:, :width]], axis=1)
    second = jnp.where(place_ref[1] == 0, second, turned)
    rows = out_refs[0].shape[1]
    for part in range(len(out_refs) // 2):
        both = dot_first(first_ref[:, part * rows : (part + 1) * rows], second)
        out_refs[2 * part][0] = both[:, width:]
        out_refs[2 * part + 1][0] = both[:, :width]


def weight_grad(place, first, second, chips, parts=1):
    tokens, rows = first.shape
    pair = second.shape[1] // chips
    width = pair // 2
    out = jax.ShapeDtypeStruct((chips, rows // parts, width), jnp.float32)
    outs = pl.pallas_call(
        weight_grad_body,
        grid_spec=pltpu.PrefetchScalarGridSpec(
            num_scalar_prefetch=1,
            grid=(chips,),
            in_specs=[
                pl.BlockSpec((tokens, rows), lambda j, place: (0, 0)),
                pl.BlockSpec((tokens, pair), lambda j, place: (0, jnp.bitwise_xor(j, place[0]))),
            ],
            out_specs=[pl.BlockSpec((1, rows // parts, width), lambda j, place: (j, 0, 0))]
            * (2 * parts),
        ),
        out_shape=[out] * (2 * parts),
        compiler_params=pltpu.CompilerParams(vmem_limit_bytes=24 * MEBI),
        cost_estimate=pl.CostEstimate(
            flops=2 * tokens * rows * second.shape[1], bytes_accessed=4 * rows * second.shape[1], transcendentals=0
        ),
        name="weight_grad",
    )(place, first, second)
    return [(outs[2 * part], outs[2 * part + 1]) for part in range(parts)]


def far_grad_body(chip_ref, first_ref, second_ref, out_ref):
    rows, width = out_ref.shape[2:]
    for part in range(out_ref.shape[0] // 2):
        both = dot_first(first_ref[:, part * rows : (part + 1) * rows], second_ref[...])
        out_ref[2 * part, 0] = both[:, :width]
        out_ref[2 * part + 1, 0] = both[:, width:]


def far_grad(chip, first, second, chips, packs):
    tokens, rows = first.shape
    pair = second.shape[1] // chips
    shape = (2 * packs, chips, rows // packs, pair // 2)
    return pl.pallas_call(
        far_grad_body,
        grid_spec=pltpu.PrefetchScalarGridSpec(
            num_scalar_prefetch=1,
            grid=(chips,),
            in_specs=[
                pl.BlockSpec((tokens, rows), lambda j, chip: (0, 0)),
                pl.BlockSpec((tokens, pair), lambda j, chip: (0, jnp.bitwise_xor(j, chip[0]))),
            ],
            out_specs=pl.BlockSpec((shape[0], 1) + shape[2:], lambda j, chip: (0, j, 0, 0)),
        ),
        out_shape=jax.ShapeDtypeStruct(shape, jnp.float32),
        compiler_params=pltpu.CompilerParams(vmem_limit_bytes=24 * MEBI),
        cost_estimate=pl.CostEstimate(
            flops=2 * tokens * rows * second.shape[1], bytes_accessed=4 * rows * second.shape[1], transcendentals=0
        ),
        name="far_grad",
    )(chip, first, second)


GATE_TILE = 512


def gate_forward_body(mixed_ref, weights_ref, gate_pre_ref, product_ref, bent_ref):
    lifted = dot_plain(mixed_ref[...], weights_ref[...])
    acts, slope = gelu_parts(gate_pre_ref[...])
    product_ref[...] = (acts * lifted).astype(jnp.bfloat16)
    bent_ref[...] = (slope * lifted).astype(jnp.bfloat16)


def gate_backward_body(low_ref, weights_ref, gate_pre_ref, bent_ref, lifted_ref, gate_ref):
    grads = dot_last(low_ref[...], weights_ref[...])
    acts = gelu(gate_pre_ref[...])
    lifted_ref[...] = (grads * acts).astype(jnp.bfloat16)
    gate_ref[...] = (grads * bent_ref[...]).astype(jnp.bfloat16)


def gate_early_body(low_ref, weights_ref, gate_pre_ref, lifted_ref, grads_ref):
    grads = dot_last(low_ref[...], weights_ref[...])
    lifted_ref[...] = (grads * gelu(gate_pre_ref[...])).astype(jnp.bfloat16)
    grads_ref[...] = grads.astype(jnp.bfloat16)


def gate_call(kernel, layer, left, weights, gated, upright, name):
    tokens, depth = left.shape
    gate = gated[0].shape[1]
    tile = pl.BlockSpec((tokens, GATE_TILE), lambda i: (0, i))
    if upright:
        weight_spec = pl.BlockSpec((None, GATE_TILE, depth), lambda i: (layer, i, 0))
    else:
        weight_spec = pl.BlockSpec((None, depth, GATE_TILE), lambda i: (layer, 0, i))
    out = jax.ShapeDtypeStruct((tokens, gate), jnp.bfloat16)
    return pl.pallas_call(
        kernel,
        grid=(gate // GATE_TILE,),
        in_specs=[pl.BlockSpec((tokens, depth), lambda i: (0, 0)), weight_spec]
        + [tile] * len(gated),
        out_specs=[tile, tile],
        out_shape=[out, out],
        compiler_params=pltpu.CompilerParams(vmem_limit_bytes=16 * MEBI),
        cost_estimate=pl.CostEstimate(
            flops=2 * tokens * depth * gate, bytes_accessed=2 * depth * gate + 10 * tokens * gate, transcendentals=0
        ),
        name=name,
    )(left, weights, *gated)


def flip_with(axis, bit):
    count = lax.axis_size(axis)
    pairs = [(device, device ^ bit) for device in range(count)]
    return lambda array: lax.ppermute(array, axis, pairs)


def by_core(core, zero, one):
    return jnp.where(core == 0, zero, one)


def prefix_join(prefix, partner, order, reach, factors):
    chips = factors.shape[0]
    places = jnp.arange(chips)
    start = (order // reach) * reach
    ahead = (places >= start) & (places < order)
    passed = jnp.prod(jnp.where(ahead[:, None], factors, 1.0), axis=0)
    return prefix + passed[:, None] * partner


def chip_scan_general(total, factors, order, chips):
    prefix = jnp.zeros_like(total)
    level = factors
    reach = 1
    while reach < chips:
        partner = flip_with("chip", reach)(total)
        group = order // reach
        sibling = lax.dynamic_index_in_dim(level, group ^ 1, 0, keepdims=False)
        mine = lax.dynamic_index_in_dim(level, group, 0, keepdims=False)
        late = (group % 2) == 1
        prefix = jnp.where(late, prefix_join(prefix, partner, order, reach, factors), prefix)
        total = jnp.where(late, mine[:, None] * partner + total, sibling[:, None] * total + partner)
        level = level[0::2] * level[1::2]
        reach *= 2
    return prefix


def column(table, index):
    return lax.dynamic_index_in_dim(table, index, 0, keepdims=False)[:, None]


class Carry:
    stages = 4

    def __init__(self, state, factors, order):
        half = state.shape[0] // 2
        self.half = half
        self.order = order
        self.square = factors.shape[0] == 8
        self.factors = factors[:, :half]
        self.chips = self.factors[0::2] * self.factors[1::2]
        self.own = state[:half]
        self.late = (order % 2) == 1
        self.swap = flip_with("core", 1)
        self.send(state[half:], self.swap)
        self.stage = 0

    def send(self, *pairs):
        self.operands = pairs[0::2]
        self.flight = tuple(way(array) for array, way in zip(pairs[0::2], pairs[1::2]))

    def go(self):
        self.stage += 1
        if self.stage == 1:
            self.total_of_chip()
            if self.square:
                self.first_round()
            else:
                entering = chip_scan_general(
                    self.total, self.chips, self.order // 2, self.chips.shape[0]
                )
                self.operands = self.flight = (entering,)
        elif self.stage == 2:
            if self.square:
                self.second_round()
        elif self.stage == 3:
            self.spread()
        else:
            self.operands = self.flight = (jnp.concatenate([self.keep, self.flight[0]], axis=0),)
        return self

    def total_of_chip(self):
        (received,) = self.flight
        self.early = jnp.where(self.late, received, self.own)
        after = jnp.where(self.late, self.own, received)
        last = self.order | 1
        self.early_factor = column(self.factors, last ^ 1)
        self.total = column(self.factors, last) * self.early + after

    def first_round(self):
        cut = self.half // 2
        self.along_x, self.along_y = flip_with("chip", 1), flip_with("chip", 2)
        self.first, self.second = self.total[:cut], self.total[cut:]
        self.send(self.first, self.along_x, self.second, self.along_y)

    def second_round(self):
        cut = self.half // 2
        place = self.order // 2
        self.place_x, self.place_y = place % 2, place // 2
        self.first_x, self.second_y = self.flight
        first_factors, second_factors = self.chips[:, :cut], self.chips[:, cut:]
        self.beside = column(first_factors, place ^ 1)
        row = jnp.where(
            self.place_x == 0,
            self.beside * self.first + self.first_x,
            column(first_factors, place) * self.first_x + self.first,
        )
        self.above, self.below = second_factors[1][:, None], second_factors[2][:, None]
        outgoing = jnp.where(
            self.place_y == 0,
            self.second,
            jnp.where(
                self.place_x == 0,
                self.below * self.above * self.second_y + self.second,
                self.second_y,
            ),
        )
        self.send(row, self.along_y, outgoing, self.along_x)

    def spread(self):
        if self.square:
            first_y, second_x = self.flight
            passed = jnp.where(self.place_x == 1, self.beside, 1.0)
            first = jnp.where(self.place_x == 1, self.first_x, 0.0) + jnp.where(
                self.place_y == 1, passed * first_y, 0.0
            )
            upper = jnp.where(self.place_x == 1, second_x, 0.0)
            lower = jnp.where(
                self.place_x == 0,
                self.above * self.second_y + second_x,
                second_x + self.below * self.second_y,
            )
            entering = jnp.concatenate([first, jnp.where(self.place_y == 0, upper, lower)], axis=0)
        else:
            (entering,) = self.flight
        middle = self.early_factor * entering + self.early
        self.keep = jnp.where(self.late, middle, entering)
        self.send(jnp.where(self.late, entering, middle), self.swap)

    def result(self):
        return self.flight[0]


class Share:
    def __init__(self, pair, along, line):
        self.pair = pair
        self.line = line
        rows = pair[1].shape[1]
        cut = {"x": rows, "y": 0}.get(along, rows // 16 * 8)
        self.parts = [
            part for part in ((slice(0, cut), 0), (slice(cut, rows), 1)) if part[0].stop > part[0].start
        ]
        self.operands = pair
        self.flight = (pair[0],)
        self.stage = -1

    def along_packs(self, array, pairs):
        self.operands = (array,)
        self.flight = (lax.ppermute(array, "blk", pairs),)

    def along_chips(self, arrays, step):
        self.operands = tuple(arrays)
        self.flight = tuple(
            flip_with("chip", 1 << (first ^ step))(array)
            for array, (_, first) in zip(arrays, self.parts)
        )

    def go(self):
        self.stage += 1
        getattr(self, "stage_%d" % self.stage)()
        return self

    def stage_0(self):
        self.operands = self.flight
        self.flight = (flip_with("core", 1)(self.operands[0]),)

    def stage_1(self):
        keep, (got,) = self.pair[1], self.flight
        self.got = got
        blocks = (slice(1, 4, 2), slice(2, 4))
        self.along_chips(
            [keep[blocks[y], rows] + got[blocks[y], rows] for rows, y in self.parts], 0
        )

    def stage_2(self):
        keep, got = self.pair[1], self.got
        self.first = self.flight
        self.along_chips(
            [
                keep[2 - y, rows] + got[2 - y, rows] + first[1]
                for (rows, y), first in zip(self.parts, self.first)
            ],
            1,
        )

    def stage_3(self):
        keep, got = self.pair[1], self.got
        sums = [
            keep[0, rows] + got[0, rows] + first[0] + second
            for (rows, _), first, second in zip(self.parts, self.first, self.flight)
        ]
        self.own = sums[0] if len(sums) == 1 else jnp.concatenate(sums, axis=0)
        if self.line:
            self.along_packs(self.own, [(0, 1), (3, 2)])
        else:
            self.operands = self.flight = (self.own,)
            self.stage = 6

    def stage_4(self):
        self.inner = self.own + self.flight[0]
        self.along_packs(self.inner, [(1, 2), (2, 1)])

    def stage_5(self):
        self.total = self.inner + self.flight[0]
        self.along_packs(self.total, [(1, 0), (2, 3)])

    def stage_6(self):
        place = lax.axis_index("blk")
        middle = (place == 1) | (place == 2)
        self.operands = self.flight = (jnp.where(middle, self.total, self.flight[0]),)

    def result(self):
        while self.stage < 6:
            self.go()
        return self.flight[0]


class FarShare:
    def __init__(self, array):
        self.operands = self.flight = (array,)
        self.cut = array.shape[2] // 16 * 8
        self.stage = -1

    def go(self):
        self.stage += 1
        getattr(self, "stage_%d" % self.stage)()
        return self

    def along_chips(self, first, second, bits):
        self.operands = (first, second)
        self.flight = tuple(
            flip_with("chip", bit)(array) for array, bit in zip(self.operands, bits)
        )

    def stage_0(self):
        self.operands = self.flight
        self.flight = (
            lax.psum_scatter(
                self.operands[0], ("blk", "core"), scatter_dimension=0, tiled=True
            ),
        )

    def stage_1(self):
        self.blocks = self.flight[0][0]
        self.along_chips(self.blocks[1::2, : self.cut], self.blocks[2:, self.cut :], (1, 2))

    def stage_2(self):
        self.first, self.second = self.flight
        self.along_chips(
            self.blocks[2, : self.cut] + self.first[1],
            self.blocks[1, self.cut :] + self.second[1],
            (2, 1),
        )

    def stage_3(self):
        first, second = self.flight
        own = jnp.concatenate(
            [
                self.blocks[0, : self.cut] + self.first[0] + first,
                self.blocks[0, self.cut :] + self.second[0] + second,
            ],
            axis=0,
        )
        self.operands = (own,)
        self.flight = (lax.all_gather(own, "blk", axis=0, tiled=True),)

    def stage_4(self):
        self.operands = self.flight

    def result(self):
        return self.flight[0]


class WholeShare:
    def __init__(self, array, axis):
        self.operands = (array,)
        self.flight = (lax.psum_scatter(array, ("chip", "core"), scatter_dimension=axis, tiled=True),)

    def go(self):
        self.operands = ()
        return self

    def result(self):
        return self.flight[0]


def sum_packs(*shares):
    for share, total in zip(shares, lax.psum([share.flight[0] for share in shares], "blk")):
        share.flight = (total,)


class Sequence:
    def __init__(self):
        self.last = ()

    def __call__(self, step, *arrays):
        arrays, _ = lax.optimization_barrier((arrays, self.last))
        results = step(*arrays)
        self.last = results
        return results

    def move(self, *items):
        for item in items:
            item.flight, _ = lax.optimization_barrier((item.flight, self.last))
            item.go()
            self.last = item.operands

    def wait(self, *items):
        for item in items:
            item.flight, _ = lax.optimization_barrier((item.flight, self.last))
            self.last = item.flight


def gelu_parts(inputs):
    square = inputs * inputs
    bent = jnp.tanh(GELU_SCALE * inputs * (1.0 + GELU_CUBE * square))
    half = 0.5 * (1.0 + bent)
    slope = half + 0.5 * inputs * (1.0 - bent * bent) * GELU_SCALE * (
        1.0 + 3.0 * GELU_CUBE * square
    )
    return inputs * half, slope


def gelu(inputs):
    return gelu_parts(inputs)[0]


def body(
    tokens,
    seq_lengths,
    ln_gain,
    ln_bias,
    w_one,
    w_two,
    w_three,
    w_four,
    readout,
    log_rate,
    cotangent,
):
    _, span, width = tokens.shape
    layers = w_one.shape[0]
    channels, states = readout.shape[1:]
    blocks = span // BLOCK
    chips = lax.axis_size("chip")
    devices = 2 * chips
    me = lax.axis_index(("chip", "core"))
    core = me % 2
    chip = me // 2
    custom = chips == 4 and lax.axis_size("blk") == 4
    upper, window, inverse, lower_inverse = fourier_tables()

    finish = jnp.cumsum(seq_lengths[0])
    begins = finish - seq_lengths[0]
    places = BLOCK * jnp.arange(devices * blocks, dtype=jnp.int32)
    opens = jnp.any(begins[:, None] == places[None, :], axis=0).reshape(devices, blocks)
    unbroken = jnp.logical_not(jnp.any(opens, axis=1))
    own_opens = lax.dynamic_index_in_dim(opens, me, 0, keepdims=False)
    segments = jnp.cumsum(own_opens.astype(jnp.int32))
    from_before = jnp.repeat((segments == 0).astype(jnp.float32), BLOCK)
    to_after = jnp.repeat((segments == segments[-1]).astype(jnp.float32), BLOCK)
    unbroken = unbroken.astype(jnp.float32)
    own_unbroken = (segments[-1] == 0).astype(jnp.float32)

    half = states // 2

    def turned(array):
        return by_core(core, array, jnp.concatenate([array[half:], array[:half]], axis=0))

    steps = jnp.arange(span, dtype=jnp.float32)

    def tables(layer):
        rates = jnp.exp(log_rate[layer])
        col = turned(rates)[:, None]
        row = turned(rates)[None, :]
        across, down = steps[None, :], steps[:, None]
        before_row, before_col = from_before[None, :], from_before[:, None]
        after_row, after_col = to_after[None, :], to_after[:, None]

        def low(array):
            return array.astype(jnp.bfloat16)

        return dict(
            rates=rates,
            decays=jnp.exp(-rates),
            retain=-jnp.expm1(-rates),
            retain_column=-jnp.expm1(-col),
            leaving=low(after_row * jnp.exp((across - (span - 1.0)) * col)),
            leaving_down=low(after_col * jnp.exp((down - (span - 1.0)) * row)),
            leaving_slopes=low(
                after_row * (span - 1.0 - across) * jnp.exp((across - (span - 2.0)) * col)
            ),
            entering=low(before_row * jnp.exp(-(across + 1.0) * col)),
            entering_down=low(before_col * jnp.exp(-(down + 1.0) * row)),
            entering_slopes=low(before_row * (across + 1.0) * jnp.exp(-across * col)),
            powers=low(jnp.exp(-across * col)),
            slopes=low(across * jnp.exp(-(across - 1.0) * col)),
            through_slope=own_unbroken * span * jnp.exp(-(span - 1.0) * col),
            factors=unbroken[:, None] * jnp.exp(-span * row),
        )

    def layer_tables(layer, table):
        def made(readout, row, retain):
            upright, kernel = layer_kernel(layer, core[None], readout, row, retain, window, span)
            return upright, kernel

        return made, readout, table["rates"][None], table["retain"][None]

    def low_dot(first, second):
        return dot_plain(first, second.astype(jnp.bfloat16))

    def open_layer(layer, flat, table):
        mean = jnp.mean(flat, axis=-1, keepdims=True)
        center = flat - mean
        scale = lax.rsqrt(jnp.mean(center * center, axis=-1, keepdims=True) + 1e-05)
        normed = (center * scale * ln_gain[layer] + ln_bias[layer]).astype(jnp.bfloat16)
        value_pre = dot_plain(normed, w_two[layer])
        values = gelu(value_pre)
        state = low_dot(table["leaving"], values)
        return mean, scale, normed, value_pre, values, state

    def share_of(name, pair):
        along = "x" if name in ALONG_X else "y" if name in ALONG_Y else "both"
        return Share(pair, along, not any(name in group for group in GROUPS))

    def share_grad(names, first, second):
        if custom and names[0] in FAR:
            made = sequence(
                lambda first, second: far_grad(
                    chip[None], first, second, chips, lax.axis_size("blk")
                ),
                first,
                second,
            )
            return [FarShare(made)]
        if custom:
            place = jnp.stack([chip, core])
            made = sequence(
                lambda first, second: weight_grad(place, first, second, chips, len(names)),
                first,
                second,
            )
            return [share_of(name, pair) for name, pair in zip(names, made)]
        return [
            WholeShare(sequence(dot_first, piece, second), 1)
            for piece in jnp.split(first, len(names), axis=1)
        ]

    def small_lines(two, grad_readout, gain_grad, bias_grad, grad_rate):
        def lines(array):
            return array.reshape(devices, -1, array.shape[-1])

        extra = jnp.concatenate(
            [part.reshape(devices, 1, -1) for part in (gain_grad, bias_grad, grad_rate)], axis=-1
        )
        wide = jnp.concatenate([lines(two), lines(grad_readout)], axis=-1)
        extra = jnp.pad(extra, ((0, 0), (0, 7), (0, wide.shape[-1] - extra.shape[-1])))
        return jnp.concatenate([wide, extra], axis=1)

    def small_share(name, lines):
        if not custom:
            return WholeShare(lines, 0)
        lines = lines.reshape((chips, 2) + lines.shape[1:])
        lines = jnp.stack(
            [lax.dynamic_index_in_dim(lines, chip ^ j, 0, keepdims=False) for j in range(chips)]
        )
        lines = by_core(core, lines, lines[:, ::-1])
        return share_of(name, (lines[:, 1], lines[:, 0]))

    def close_layer(layer, upstream, flat, mean, scale, grad_gate_pre, grad_value_pre):
        grad_normed = dot_last(grad_gate_pre, w_one[layer]) + dot_last(
            grad_value_pre, w_two[layer]
        )
        hat = (flat - mean) * scale
        gain_grad = jnp.sum(grad_normed * hat, axis=0)
        bias_grad = jnp.sum(grad_normed, axis=0)
        scaled = grad_normed * ln_gain[layer]
        grad_flat = upstream + scale * (
            scaled
            - jnp.mean(scaled, axis=-1, keepdims=True)
            - hat * jnp.mean(scaled * hat, axis=-1, keepdims=True)
        )
        return grad_flat, gain_grad, bias_grad

    def kernel_grads(
        table, upright, lag_sums, incoming, adjoint, pulled, grad_mixed, values
    ):
        mixing = upright * table["retain_column"]
        grad_mixing = low_dot(table["powers"], lag_sums) + incoming * pulled
        grad_decays = jnp.sum(
            mixing
            * (
                low_dot(table["slopes"], lag_sums)
                + incoming * low_dot(table["entering_slopes"], grad_mixed)
            )
            + adjoint * low_dot(table["leaving_slopes"], values)
            + table["through_slope"] * incoming * adjoint,
            axis=1,
        )
        grad_retain = jnp.sum(grad_mixing * upright, axis=1)
        grad_rate = table["rates"] * table["decays"] * turned(grad_retain - grad_decays)
        return turned(grad_mixing) * table["retain"][:, None], grad_rate

    back_order = devices - 1 - me
    sequence = Sequence()
    move = sequence.move

    def start_carry(state, factors, order):
        carried = Carry(state, factors, order)
        sequence.last = carried.operands
        return carried

    def mix(local, table, upright, incoming):
        scaled = upright * table["retain_column"] * incoming
        return (local + low_dot(table["entering_down"], scaled)).astype(jnp.bfloat16)

    def pull(grad_lifted, table, upright, layer):
        grad_mixed = dot_last(grad_lifted, w_three[layer])
        pulled = low_dot(table["entering"], grad_mixed)
        return grad_mixed, pulled, upright * table["retain_column"] * pulled

    def gate_forward(layer, mixed, gate_pre):
        return gate_call(
            gate_forward_body, layer, mixed, w_three, (gate_pre,), False, "gate_forward"
        )

    def value_grad(table, local, adjoint, value_pre):
        grad_values = local + low_dot(table["leaving_down"], adjoint)
        return (grad_values * gelu_parts(value_pre)[1]).astype(jnp.bfloat16)

    def small_grads(table, upright, grad_value_pre, normed, sums, gain_grad, bias_grad):
        def made(grad_value_pre, normed, gain_grad, bias_grad, *sums):
            two = dot_first(grad_value_pre, normed)
            grad_readout, grad_rate = kernel_grads(table, upright, *sums)
            return small_lines(two, grad_readout, gain_grad, bias_grad, grad_rate)

        return sequence(made, grad_value_pre, normed, gain_grad, bias_grad, *sums)

    conv_tables = (upper, inverse)
    back_tables = (upper, inverse, lower_inverse)

    flat0 = tokens.reshape(span, width)
    t0 = tables(0)
    t1 = tables(1)
    mean0, scale0, normed0, value_pre0, values0, state0 = open_layer(0, flat0, t0)
    c0 = start_carry(state0, t0["factors"], me)
    upright0, kernel0 = sequence(*layer_tables(0, t0))
    move(c0)
    gate_pre0 = sequence(lambda normed: dot_plain(normed, w_one[0]), normed0)
    move(c0)
    local0 = sequence(conv_forward, segments, values0, kernel0, *conv_tables)
    upright1, kernel1 = sequence(*layer_tables(1, t1))
    move(c0, c0)
    mixed0 = sequence(lambda *arrays: mix(arrays[0], t0, *arrays[1:]), local0, upright0, c0.result())
    product0, bent0 = sequence(functools.partial(gate_forward, 0), mixed0, gate_pre0)
    flat1 = flat0 + dot_plain(product0, w_four[0])

    mean1, scale1, normed1, value_pre1, values1, state1 = open_layer(1, flat1, t1)
    c1 = start_carry(state1, t1["factors"], me)
    gate_pre1 = sequence(lambda normed: dot_plain(normed, w_one[1]), normed1)
    move(c1)
    low_cotangent = cotangent.reshape(span, width).astype(jnp.bfloat16)
    grad_lifted1, grad_product1 = sequence(
        lambda low, gate_pre: gate_call(
            gate_early_body, 1, low, w_four, (gate_pre,), True, "gate_early"
        ),
        low_cotangent,
        gate_pre1,
    )
    move(c1)
    grad_mixed1, pulled1, leaving1 = sequence(
        lambda grad_lifted, upright: pull(grad_lifted, t1, upright, 1), grad_lifted1, upright1
    )
    b1 = start_carry(leaving1, t1["factors"][::-1], back_order)
    local1 = sequence(conv_forward, segments, values1, kernel1, *conv_tables)
    move(c1, b1, c1)
    incoming1 = c1.result()
    mixed1 = sequence(lambda *arrays: mix(arrays[0], t1, *arrays[1:]), local1, upright1, incoming1)
    v = dict(items=dict(b1=b1))
    items = v["items"]

    def shares(names, first, second):
        names = names.split()
        items.update(zip(names, share_grad(names, first, second)))

    def gate1():
        v["product1"], v["bent1"] = sequence(
            functools.partial(gate_forward, 1), mixed1, gate_pre1
        )

    def conv1():
        v["gv1"], v["lags1"] = sequence(
            conv_backward, segments, values1, grad_mixed1, kernel1, *back_tables
        )

    def slope1():
        v["grad_gate1"] = sequence(jnp.multiply, grad_product1, v["bent1"])

    def value1():
        v["adjoint1"] = items["b1"].result()
        v["grad_value1"] = sequence(
            lambda *arrays: value_grad(t1, *arrays), v["gv1"], v["adjoint1"], value_pre1
        )

    def close1():
        v["upstream0"], v["gain1"], v["bias1"] = sequence(
            functools.partial(close_layer, 1),
            cotangent.reshape(span, width),
            flat1,
            mean1,
            scale1,
            v["grad_gate1"],
            v["grad_value1"],
        )
        v["low0"] = v["upstream0"].astype(jnp.bfloat16)

    def gate0():
        v["grad_lifted0"], v["grad_gate0"] = sequence(
            lambda low, gate_pre, bent: gate_call(
                gate_backward_body, 0, low, w_four, (gate_pre, bent), True, "gate_backward"
            ),
            v["low0"],
            gate_pre0,
            bent0,
        )

    def pull0():
        v["grad_mixed0"], v["pulled0"], leaving0 = sequence(
            lambda grad_lifted, upright: pull(grad_lifted, t0, upright, 0),
            v["grad_lifted0"],
            upright0,
        )
        items["b0"] = start_carry(leaving0, t0["factors"][::-1], back_order)

    def conv0():
        v["gv0"], v["lags0"] = sequence(
            conv_backward, segments, values0, v["grad_mixed0"], kernel0, *back_tables
        )

    def value0():
        v["adjoint0"] = items["b0"].result()
        v["grad_value0"] = sequence(
            lambda *arrays: value_grad(t0, *arrays), v["gv0"], v["adjoint0"], value_pre0
        )

    def close0():
        v["grad_tokens"], v["gain0"], v["bias0"] = sequence(
            functools.partial(close_layer, 0),
            v["upstream0"],
            flat0,
            mean0,
            scale0,
            v["grad_gate0"],
            v["grad_value0"],
        )

    def lines1():
        sums = (v["lags1"], incoming1, v["adjoint1"], pulled1, grad_mixed1, values1)
        v["lines1"] = small_grads(
            t1, upright1, v["grad_value1"], normed1, sums, v["gain1"], v["bias1"]
        )

    def lines0():
        sums = (v["lags0"], c0.result(), v["adjoint0"], v["pulled0"], v["grad_mixed0"], values0)
        v["lines0"] = small_grads(
            t0, upright0, v["grad_value0"], normed0, sums, v["gain0"], v["bias0"]
        )

    def small():
        items["small"] = small_share("small", jnp.concatenate([v["lines0"], v["lines1"]], axis=1))
        sequence.last = items["small"].operands

    def result():
        v["result"] = sequence(
            lambda flat, product: flat + dot_plain(product, w_four[1]), flat1, v["product1"]
        )

    actions = dict(
        gate1=gate1,
        conv1=conv1,
        slope1=slope1,
        value1=value1,
        close1=close1,
        gate0=gate0,
        pull0=pull0,
        conv0=conv0,
        value0=value0,
        close0=close0,
        lines1=lines1,
        lines0=lines0,
        lines=small,
        result=result,
        grad_three1=lambda: shares("three1", mixed1, grad_lifted1),
        grad_four1=lambda: shares(PARTS[0], v["product1"], low_cotangent),
        grad_one1=lambda: shares(PARTS[1], normed1, v["grad_gate1"]),
        grad_four0=lambda: shares(PARTS[2], product0, v["low0"]),
        grad_one0=lambda: shares(PARTS[3], normed0, v["grad_gate0"]),
        grad_three0=lambda: shares("three0", mixed0, v["grad_lifted0"]),
    )
    for name in ORDER:
        if name in actions:
            actions[name]()
        elif name.startswith("~"):
            sequence.wait(items[name[1:]])
        elif name.startswith("sum"):
            if custom:
                sum_packs(*[items[member] for member in GROUPS[int(name[3:])]])
        else:
            move(items[name])
    if not custom:
        sum_packs(*[item for item in items.values() if isinstance(item, WholeShare)])
    flat, upstream = v["result"], v["grad_tokens"]

    def whole(*names):
        return jnp.concatenate([items[name].result() for name in names], axis=0)

    collected = []
    lines = items["small"].result()
    lines = jnp.split(lines if custom else lines[0], 2, axis=0)
    for layer, small_rows in zip("01", lines):
        collected.append(
            [
                whole(*PARTS[2 - 2 * int(layer)].split()),
                whole("three" + layer),
                whole(*PARTS[3 - 2 * int(layer)].split()),
                small_rows,
            ]
        )

    def unpack(shares):
        four, three, one, small = shares
        rows = small.shape[0] - 8
        gains = width // devices
        rate_width = states // devices
        return (
            small[rows, :gains],
            small[rows, gains : 2 * gains],
            one,
            small[:rows, :width].T,
            three,
            four,
            small[:rows, width:].T,
            small[rows, 2 * gains : 2 * gains + rate_width],
        )

    parts = [unpack(shares) for shares in collected]
    stacked = [jnp.stack([part[member] for part in parts]) for member in range(8)]
    return (flat[None], upstream[None], *stacked)


def solution(mesh):
    packs = mesh.shape["blk"]
    mesh = jax.sharding.Mesh(mesh.devices.reshape(-1, 2, packs), SEQ + ("blk",))
    placed = (
        P("blk", SEQ, None),
        P("blk", None),
        P(),
        P(),
        P(),
        P(),
        P(),
        P(),
        P(),
        P(),
        P("blk", SEQ, None),
    )
    return jax.shard_map(
        body,
        mesh=mesh,
        in_specs=placed,
        out_specs=(
            P("blk", SEQ, None),
            P("blk", SEQ, None),
            P(None, SEQ),
            P(None, SEQ),
            P(None, None, SEQ),
            P(None, None, SEQ),
            P(None, None, SEQ),
            P(None, None, SEQ),
            P(None, None, SEQ),
            P(None, SEQ),
        ),
        check_vma=False,
    )
```

```python
import functools

import numpy as np

import jax
import jax.numpy as jnp
from jax import lax
from jax.experimental import pallas as pl
from jax.experimental.pallas import tpu as pltpu
from jax.sharding import PartitionSpec as P

BLOCK = 64
FREQS = 64
LANES = 128
GELU_SCALE = float(np.sqrt(2.0 / np.pi))
GELU_CUBE = 0.044715
MEBI = 1024 * 1024

SEQ = ("chip", "core")

NAMES = (
    "gate1", "slope1", "b1", "grad_four1", "grad_three1", "four1", "three1", "grad_one1", "one1", "conv1",
    "value1", "close1", "gate0", "grad_four0", "pull0", "b0", "grad_one0", "four0", "one0", "conv0", "lines1",
    "grad_three0", "value0", "close0", "lines0", "lines", "three0", "small", "result",
)
ORDER = (
    0, 1, 2, 3, 4, 2, 5, 6, 7, 2, 6, 8, 9, 8, 10, 11, 6, 12, 13, 8, 14, 6, 15, 16, 8, 15, 17, 18, 19, 17, 15,
    6, 18, 20, 15, 5, 21, 17, 8, 22, 5, 6, 17, 23, 24, 25, 6, 18, 26, 8, 27, 17, 5, 26, 27, 18, 17, 27, 8, 18,
    26, 27, 26, 18, 27, 5, 17, 26, 27, 18, 26, 27, 28, 26,
)
GROUPS = ()
ALONG_X = ()
ALONG_Y = ()
FAR = ("four1",)
PARTS = ("four1", "one1", "four0", "one0")


def fourier_tables():
    angles = (2.0 * np.pi / (2 * BLOCK)) * (np.arange(FREQS) + 0.5)[:, None]

    def forward(places):
        return np.concatenate([np.cos(angles * places), -np.sin(angles * places)], axis=0)

    def parts(table):
        table = np.asarray(table, np.float32)
        high = table.astype(jnp.bfloat16)
        rest = (table - high.astype(np.float32)).astype(jnp.bfloat16)
        return jnp.asarray(np.concatenate([high, high, rest], axis=1))

    upper = forward(np.arange(BLOCK)[None, :])
    lower = forward(np.arange(-BLOCK, 0)[None, :])
    lower[:, 0] = 0.0
    return (
        parts(upper),
        parts(np.concatenate([lower, upper], axis=1)),
        parts(upper.T / FREQS),
        parts(lower.T / FREQS),
    )


def three_parts(array):
    high = array.astype(jnp.bfloat16)
    rest = (array - high.astype(jnp.float32)).astype(jnp.bfloat16)
    return jnp.concatenate([high, rest, high], axis=0)


def beside(array, blocks):
    return jnp.concatenate(
        [array[block * BLOCK : (block + 1) * BLOCK] for block in range(blocks)], axis=1
    )


def dot_first(first, second, precision=None):
    return lax.dot_general(
        first,
        second,
        (((0,), (0,)), ((), ())),
        precision=precision,
        preferred_element_type=jnp.float32,
    )


def dot_last(first, second, precision=None):
    return lax.dot_general(
        first,
        second,
        (((1,), (1,)), ((), ())),
        precision=precision,
        preferred_element_type=jnp.float32,
    )


def dot_plain(first, second, precision=None):
    return jnp.dot(first, second, precision=precision, preferred_element_type=jnp.float32)


def layer_kernel_body(core_ref, readout_ref, rates_ref, retain_ref, window_ref, upright_ref, out_ref):
    blocks = out_ref.shape[0]
    tokens = blocks * BLOCK
    half = readout_ref.shape[1] // 2
    rates = rates_ref[...]
    decaying = jnp.exp(
        -lax.broadcasted_iota(jnp.int32, (tokens, 1), 0).astype(jnp.float32) * rates
    ).astype(jnp.bfloat16)
    readout = readout_ref[...]
    lags = dot_last(decaying, (readout * retain_ref[...]).astype(jnp.bfloat16))
    padded = jnp.concatenate([jnp.zeros((BLOCK, lags.shape[1]), jnp.float32), lags], axis=0)
    for step in range(blocks):
        window = padded[step * BLOCK : (step + 2) * BLOCK]
        out_ref[step] = dot_plain(window_ref[...], three_parts(window))
    upright = readout.T
    swapped = jnp.concatenate([upright[half:], upright[:half]], axis=0)
    upright_ref[...] = jnp.where(core_ref[0] == 0, upright, swapped)


def layer_kernel(layer, core, readout, rates, retain, window, tokens):
    _, channels, states = readout.shape
    blocks = tokens // BLOCK
    wide = 2 * LANES
    row = pl.BlockSpec((1, states), lambda i: (0, 0))
    return pl.pallas_call(
        layer_kernel_body,
        grid=(channels // wide,),
        in_specs=[
            pl.BlockSpec(memory_space=pltpu.SMEM),
            pl.BlockSpec((None, wide, states), lambda i: (layer, i, 0)),
            row,
            row,
            pl.BlockSpec(window.shape, lambda i: (0, 0)),
        ],
        out_specs=[
            pl.BlockSpec((states, wide), lambda i: (0, i)),
            pl.BlockSpec((blocks, 2 * FREQS, wide), lambda i: (0, 0, i)),
        ],
        out_shape=[
            jax.ShapeDtypeStruct((states, channels), jnp.float32),
            jax.ShapeDtypeStruct((blocks, 2 * FREQS, channels), jnp.float32),
        ],
        compiler_params=pltpu.CompilerParams(vmem_limit_bytes=12 * MEBI),
        cost_estimate=pl.CostEstimate(
            flops=8 * tokens * states * channels, bytes_accessed=8 * (states + tokens) * channels, transcendentals=0
        ),
        name="layer_kernel",
    )(core, readout, rates, retain, window)


def same_segment(segments_ref, first, second):
    return (segments_ref[first] == segments_ref[second]).astype(jnp.float32)


def keep_blocks(ref, array):
    for block in range(ref.shape[0]):
        ref[block] = array[:, block * LANES : (block + 1) * LANES]


def conv_forward_body(segments_ref, values_ref, kernel_ref, upper_ref, inverse_ref, out_ref, spec_ref):
    blocks = kernel_ref.shape[0]
    keep_blocks(spec_ref, dot_plain(upper_ref[...], three_parts(beside(values_ref[...], blocks))))
    sums = []
    for block in range(blocks):
        real = jnp.zeros((FREQS, LANES), jnp.float32)
        imag = jnp.zeros((FREQS, LANES), jnp.float32)
        for source in range(block + 1):
            lag = block - source
            mask = same_segment(segments_ref, block, source)
            kernel_real = kernel_ref[lag, :FREQS] * mask
            kernel_imag = kernel_ref[lag, FREQS:] * mask
            value_real = spec_ref[source, :FREQS]
            value_imag = spec_ref[source, FREQS:]
            real = real + (kernel_real * value_real - kernel_imag * value_imag)
            imag = imag + (kernel_real * value_imag + kernel_imag * value_real)
        sums.append(jnp.concatenate([real, imag], axis=0))
    out = dot_plain(inverse_ref[...], three_parts(jnp.concatenate(sums, axis=1)))
    for block in range(blocks):
        out_ref[block * BLOCK : (block + 1) * BLOCK, :] = out[:, block * LANES : (block + 1) * LANES]


def conv_forward(segments, values, kernel, upper, inverse):
    tokens, channels = values.shape
    blocks = tokens // BLOCK
    return pl.pallas_call(
        conv_forward_body,
        grid=(channels // LANES,),
        in_specs=[
            pl.BlockSpec(memory_space=pltpu.SMEM),
            pl.BlockSpec((tokens, LANES), lambda i: (0, i)),
            pl.BlockSpec((blocks, 2 * FREQS, LANES), lambda i: (0, 0, i)),
            pl.BlockSpec(upper.shape, lambda i: (0, 0)),
            pl.BlockSpec(inverse.shape, lambda i: (0, 0)),
        ],
        out_specs=pl.BlockSpec((tokens, LANES), lambda i: (0, i)),
        out_shape=jax.ShapeDtypeStruct((tokens, channels), jnp.float32),
        scratch_shapes=[pltpu.VMEM((blocks, 2 * FREQS, LANES), jnp.float32)],
        compiler_params=pltpu.CompilerParams(vmem_limit_bytes=10 * MEBI),
        cost_estimate=pl.CostEstimate(
            flops=2000 * tokens * channels, bytes_accessed=16 * tokens * channels, transcendentals=0
        ),
        name="conv_forward",
    )(segments, values, kernel, upper, inverse)


def conv_backward_body(
    segments_ref,
    values_ref,
    grads_ref,
    kernel_ref,
    upper_ref,
    inverse_ref,
    lower_inverse_ref,
    out_ref,
    lags_ref,
    value_spec_ref,
    grad_spec_ref,
):
    blocks = kernel_ref.shape[0]
    for spec_ref, in_ref in ((value_spec_ref, values_ref), (grad_spec_ref, grads_ref)):
        keep_blocks(spec_ref, dot_plain(upper_ref[...], three_parts(beside(in_ref[...], blocks))))
    sums = []
    for source in range(blocks):
        real = jnp.zeros((FREQS, LANES), jnp.float32)
        imag = jnp.zeros((FREQS, LANES), jnp.float32)
        for block in range(source, blocks):
            lag = block - source
            mask = same_segment(segments_ref, block, source)
            kernel_real = kernel_ref[lag, :FREQS] * mask
            kernel_imag = kernel_ref[lag, FREQS:] * mask
            grad_real = grad_spec_ref[block, :FREQS]
            grad_imag = grad_spec_ref[block, FREQS:]
            real = real + (kernel_real * grad_real + kernel_imag * grad_imag)
            imag = imag + (kernel_real * grad_imag - kernel_imag * grad_real)
        sums.append(jnp.concatenate([real, imag], axis=0))
    out = dot_plain(inverse_ref[...], three_parts(jnp.concatenate(sums, axis=1)))
    for block in range(blocks):
        out_ref[block * BLOCK : (block + 1) * BLOCK, :] = out[:, block * LANES : (block + 1) * LANES]
    sums = []
    for lag in range(blocks):
        real = jnp.zeros((FREQS, LANES), jnp.float32)
        imag = jnp.zeros((FREQS, LANES), jnp.float32)
        for source in range(blocks - lag):
            block = source + lag
            mask = same_segment(segments_ref, block, source)
            grad_real = grad_spec_ref[block, :FREQS] * mask
            grad_imag = grad_spec_ref[block, FREQS:] * mask
            value_real = value_spec_ref[source, :FREQS]
            value_imag = value_spec_ref[source, FREQS:]
            real = real + (grad_real * value_real + grad_imag * value_imag)
            imag = imag + (grad_imag * value_real - grad_real * value_imag)
        sums.append(jnp.concatenate([real, imag], axis=0))
    parts = three_parts(jnp.concatenate(sums, axis=1))
    here = dot_plain(inverse_ref[...], parts)
    behind = dot_plain(lower_inverse_ref[...], parts)
    for lag in range(blocks):
        lags = here[:, lag * LANES : (lag + 1) * LANES]
        if lag + 1 < blocks:
            lags = lags + behind[:, (lag + 1) * LANES : (lag + 2) * LANES]
        lags_ref[lag * BLOCK : (lag + 1) * BLOCK, :] = lags


def conv_backward(segments, values, grads, kernel, upper, inverse, lower_inverse):
    tokens, channels = values.shape
    blocks = tokens // BLOCK
    shape = jax.ShapeDtypeStruct((tokens, channels), jnp.float32)
    tall = pl.BlockSpec((tokens, LANES), lambda i: (0, i))
    return pl.pallas_call(
        conv_backward_body,
        grid=(channels // LANES,),
        in_specs=[
            pl.BlockSpec(memory_space=pltpu.SMEM),
            tall,
            tall,
            pl.BlockSpec((blocks, 2 * FREQS, LANES), lambda i: (0, 0, i)),
            pl.BlockSpec(upper.shape, lambda i: (0, 0)),
            pl.BlockSpec(inverse.shape, lambda i: (0, 0)),
            pl.BlockSpec(lower_inverse.shape, lambda i: (0, 0)),
        ],
        out_specs=[tall, tall],
        out_shape=[shape, shape],
        scratch_shapes=[pltpu.VMEM((blocks, 2 * FREQS, LANES), jnp.float32)] * 2,
        compiler_params=pltpu.CompilerParams(vmem_limit_bytes=12 * MEBI),
        cost_estimate=pl.CostEstimate(
            flops=4000 * tokens * channels, bytes_accessed=24 * tokens * channels, transcendentals=0
        ),
        name="conv_backward",
    )(segments, values, grads, kernel, upper, inverse, lower_inverse)


def weight_grad_body(place_ref, first_ref, second_ref, *out_refs):
    width = out_refs[0].shape[-1]
    second = second_ref[...]
    turned = jnp.concatenate([second[:, width:], second[:, :width]], axis=1)
    second = jnp.where(place_ref[1] == 0, second, turned)
    rows = out_refs[0].shape[1]
    for part in range(len(out_refs) // 2):
        both = dot_first(first_ref[:, part * rows : (part + 1) * rows], second)
        out_refs[2 * part][0] = both[:, width:]
        out_refs[2 * part + 1][0] = both[:, :width]


def weight_grad(place, first, second, chips, parts=1):
    tokens, rows = first.shape
    pair = second.shape[1] // chips
    width = pair // 2
    out = jax.ShapeDtypeStruct((chips, rows // parts, width), jnp.float32)
    outs = pl.pallas_call(
        weight_grad_body,
        grid_spec=pltpu.PrefetchScalarGridSpec(
            num_scalar_prefetch=1,
            grid=(chips,),
            in_specs=[
                pl.BlockSpec((tokens, rows), lambda j, place: (0, 0)),
                pl.BlockSpec((tokens, pair), lambda j, place: (0, jnp.bitwise_xor(j, place[0]))),
            ],
            out_specs=[pl.BlockSpec((1, rows // parts, width), lambda j, place: (j, 0, 0))]
            * (2 * parts),
        ),
        out_shape=[out] * (2 * parts),
        compiler_params=pltpu.CompilerParams(vmem_limit_bytes=24 * MEBI),
        cost_estimate=pl.CostEstimate(
            flops=2 * tokens * rows * second.shape[1], bytes_accessed=4 * rows * second.shape[1], transcendentals=0
        ),
        name="weight_grad",
    )(place, first, second)
    return [(outs[2 * part], outs[2 * part + 1]) for part in range(parts)]


def far_grad_body(chip_ref, first_ref, second_ref, out_ref):
    rows, width = out_ref.shape[2:]
    for part in range(out_ref.shape[0] // 2):
        both = dot_first(first_ref[:, part * rows : (part + 1) * rows], second_ref[...])
        out_ref[2 * part, 0] = both[:, :width]
        out_ref[2 * part + 1, 0] = both[:, width:]


def far_grad(chip, first, second, chips, packs):
    tokens, rows = first.shape
    pair = second.shape[1] // chips
    shape = (2 * packs, chips, rows // packs, pair // 2)
    return pl.pallas_call(
        far_grad_body,
        grid_spec=pltpu.PrefetchScalarGridSpec(
            num_scalar_prefetch=1,
            grid=(chips,),
            in_specs=[
                pl.BlockSpec((tokens, rows), lambda j, chip: (0, 0)),
                pl.BlockSpec((tokens, pair), lambda j, chip: (0, jnp.bitwise_xor(j, chip[0]))),
            ],
            out_specs=pl.BlockSpec((shape[0], 1) + shape[2:], lambda j, chip: (0, j, 0, 0)),
        ),
        out_shape=jax.ShapeDtypeStruct(shape, jnp.float32),
        compiler_params=pltpu.CompilerParams(vmem_limit_bytes=24 * MEBI),
        cost_estimate=pl.CostEstimate(
            flops=2 * tokens * rows * second.shape[1], bytes_accessed=4 * rows * second.shape[1], transcendentals=0
        ),
        name="far_grad",
    )(chip, first, second)


def small_grad_body(place_ref, first_ref, normed_ref, readout_ref, gain_ref, bias_ref, rate_ref, send_ref, keep_ref):
    two = dot_first(first_ref[...], normed_ref[...])
    wide = jnp.concatenate([two, readout_ref[...]], axis=1)
    rows = wide.shape[0] // 2
    segment = gain_ref.shape[1] // 2
    rates = rate_ref[...]
    turned_rates = pltpu.roll(rates, rows, axis=1)
    spare = jnp.zeros((1, wide.shape[1] - 2 * segment - rates.shape[1]), jnp.float32)
    shares = []
    for core, rate in ((0, rates), (1, turned_rates)):
        part = slice(core * segment, (core + 1) * segment)
        line = jnp.concatenate([gain_ref[:, part], bias_ref[:, part], rate, spare], axis=1)
        shares.append(
            jnp.concatenate(
                [wide[core * rows : (core + 1) * rows], jnp.broadcast_to(line, (8, line.shape[1]))],
                axis=0,
            )
        )
    mine = place_ref[1] == 0
    keep_ref[0] = jnp.where(mine, shares[0], shares[1])
    send_ref[0] = jnp.where(mine, shares[1], shares[0])


def small_grad(place, first, normed, grad_readout, gain, bias, rate, chips):
    tokens, channels = first.shape
    width = normed.shape[1]
    pair = channels // chips
    states = grad_readout.shape[0] // chips

    def natural(j, place):
        return jnp.bitwise_xor(j, place[0])

    def turned(j, place):
        return lax.rem(natural(j, place) + place[1] * (chips // 2), chips)

    out = jax.ShapeDtypeStruct(
        (chips, pair // 2 + 8, width + grad_readout.shape[1]), jnp.float32
    )
    out_spec = pl.BlockSpec((1,) + out.shape[1:], lambda j, place: (j, 0, 0))
    gains = pl.BlockSpec((1, width // chips), lambda j, place: (0, natural(j, place)))
    return pl.pallas_call(
        small_grad_body,
        grid_spec=pltpu.PrefetchScalarGridSpec(
            num_scalar_prefetch=1,
            grid=(chips,),
            in_specs=[
                pl.BlockSpec((tokens, pair), lambda j, place: (0, natural(j, place))),
                pl.BlockSpec((tokens, width), lambda j, place: (0, 0)),
                pl.BlockSpec(
                    (states, grad_readout.shape[1]), lambda j, place: (turned(j, place), 0)
                ),
                gains,
                gains,
                pl.BlockSpec((1, states), lambda j, place: (0, turned(j, place))),
            ],
            out_specs=[out_spec, out_spec],
        ),
        out_shape=[out, out],
        compiler_params=pltpu.CompilerParams(vmem_limit_bytes=16 * MEBI),
        cost_estimate=pl.CostEstimate(
            flops=2 * tokens * channels * width, bytes_accessed=8 * 1024 * 1024, transcendentals=0
        ),
        name="small_grad",
    )(place, first, normed, grad_readout, gain, bias, rate)


GATE_TILE = 512


def gate_forward_body(mixed_ref, weights_ref, gate_pre_ref, product_ref, bent_ref):
    lifted = dot_plain(mixed_ref[...], weights_ref[...])
    acts, slope = gelu_parts(gate_pre_ref[...])
    product_ref[...] = (acts * lifted).astype(jnp.bfloat16)
    bent_ref[...] = (slope * lifted).astype(jnp.bfloat16)


def gate_backward_body(low_ref, weights_ref, gate_pre_ref, bent_ref, lifted_ref, gate_ref):
    grads = dot_last(low_ref[...], weights_ref[...])
    acts = gelu(gate_pre_ref[...])
    lifted_ref[...] = (grads * acts).astype(jnp.bfloat16)
    gate_ref[...] = (grads * bent_ref[...]).astype(jnp.bfloat16)


def gate_early_body(low_ref, weights_ref, gate_pre_ref, lifted_ref, grads_ref):
    grads = dot_last(low_ref[...], weights_ref[...])
    lifted_ref[...] = (grads * gelu(gate_pre_ref[...])).astype(jnp.bfloat16)
    grads_ref[...] = grads.astype(jnp.bfloat16)


def gate_call(kernel, layer, left, weights, gated, upright, name):
    tokens, depth = left.shape
    gate = gated[0].shape[1]
    tile = pl.BlockSpec((tokens, GATE_TILE), lambda i: (0, i))
    if upright:
        weight_spec = pl.BlockSpec((None, GATE_TILE, depth), lambda i: (layer, i, 0))
    else:
        weight_spec = pl.BlockSpec((None, depth, GATE_TILE), lambda i: (layer, 0, i))
    out = jax.ShapeDtypeStruct((tokens, gate), jnp.bfloat16)
    return pl.pallas_call(
        kernel,
        grid=(gate // GATE_TILE,),
        in_specs=[pl.BlockSpec((tokens, depth), lambda i: (0, 0)), weight_spec]
        + [tile] * len(gated),
        out_specs=[tile, tile],
        out_shape=[out, out],
        compiler_params=pltpu.CompilerParams(vmem_limit_bytes=16 * MEBI),
        cost_estimate=pl.CostEstimate(
            flops=2 * tokens * depth * gate, bytes_accessed=2 * depth * gate + 10 * tokens * gate, transcendentals=0
        ),
        name=name,
    )(left, weights, *gated)


def flip_with(axis, bit):
    count = lax.axis_size(axis)
    pairs = [(device, device ^ bit) for device in range(count)]
    return lambda array: lax.ppermute(array, axis, pairs)


def by_core(core, zero, one):
    return jnp.where(core == 0, zero, one)


def prefix_join(prefix, partner, order, reach, factors):
    chips = factors.shape[0]
    places = jnp.arange(chips)
    start = (order // reach) * reach
    ahead = (places >= start) & (places < order)
    passed = jnp.prod(jnp.where(ahead[:, None], factors, 1.0), axis=0)
    return prefix + passed[:, None] * partner


def chip_scan_general(total, factors, order, chips):
    prefix = jnp.zeros_like(total)
    level = factors
    reach = 1
    while reach < chips:
        partner = flip_with("chip", reach)(total)
        group = order // reach
        sibling = lax.dynamic_index_in_dim(level, group ^ 1, 0, keepdims=False)
        mine = lax.dynamic_index_in_dim(level, group, 0, keepdims=False)
        late = (group % 2) == 1
        prefix = jnp.where(late, prefix_join(prefix, partner, order, reach, factors), prefix)
        total = jnp.where(late, mine[:, None] * partner + total, sibling[:, None] * total + partner)
        level = level[0::2] * level[1::2]
        reach *= 2
    return prefix


def column(table, index):
    return lax.dynamic_index_in_dim(table, index, 0, keepdims=False)[:, None]


class Carry:
    stages = 4

    def __init__(self, state, factors, order):
        half = state.shape[0] // 2
        self.half = half
        self.order = order
        self.square = factors.shape[0] == 8
        self.factors = factors[:, :half]
        self.chips = self.factors[0::2] * self.factors[1::2]
        self.own = state[:half]
        self.late = (order % 2) == 1
        self.swap = flip_with("core", 1)
        self.send(state[half:], self.swap)
        self.stage = 0

    def send(self, *pairs):
        self.operands = pairs[0::2]
        self.flight = tuple(way(array) for array, way in zip(pairs[0::2], pairs[1::2]))

    def go(self):
        self.stage += 1
        if self.stage == 1:
            self.total_of_chip()
            if self.square:
                self.first_round()
            else:
                entering = chip_scan_general(
                    self.total, self.chips, self.order // 2, self.chips.shape[0]
                )
                self.operands = self.flight = (entering,)
        elif self.stage == 2:
            if self.square:
                self.second_round()
        elif self.stage == 3:
            self.spread()
        else:
            self.operands = self.flight = (jnp.concatenate([self.keep, self.flight[0]], axis=0),)
        return self

    def total_of_chip(self):
        (received,) = self.flight
        self.early = jnp.where(self.late, received, self.own)
        after = jnp.where(self.late, self.own, received)
        last = self.order | 1
        self.early_factor = column(self.factors, last ^ 1)
        self.total = column(self.factors, last) * self.early + after

    def first_round(self):
        cut = self.half // 2
        self.along_x, self.along_y = flip_with("chip", 1), flip_with("chip", 2)
        self.first, self.second = self.total[:cut], self.total[cut:]
        self.send(self.first, self.along_x, self.second, self.along_y)

    def second_round(self):
        cut = self.half // 2
        place = self.order // 2
        self.place_x, self.place_y = place % 2, place // 2
        self.first_x, self.second_y = self.flight
        first_factors, second_factors = self.chips[:, :cut], self.chips[:, cut:]
        self.beside = column(first_factors, place ^ 1)
        row = jnp.where(
            self.place_x == 0,
            self.beside * self.first + self.first_x,
            column(first_factors, place) * self.first_x + self.first,
        )
        self.above, self.below = second_factors[1][:, None], second_factors[2][:, None]
        outgoing = jnp.where(
            self.place_y == 0,
            self.second,
            jnp.where(
                self.place_x == 0,
                self.below * self.above * self.second_y + self.second,
                self.second_y,
            ),
        )
        self.send(row, self.along_y, outgoing, self.along_x)

    def spread(self):
        if self.square:
            first_y, second_x = self.flight
            passed = jnp.where(self.place_x == 1, self.beside, 1.0)
            first = jnp.where(self.place_x == 1, self.first_x, 0.0) + jnp.where(
                self.place_y == 1, passed * first_y, 0.0
            )
            upper = jnp.where(self.place_x == 1, second_x, 0.0)
            lower = jnp.where(
                self.place_x == 0,
                self.above * self.second_y + second_x,
                second_x + self.below * self.second_y,
            )
            entering = jnp.concatenate([first, jnp.where(self.place_y == 0, upper, lower)], axis=0)
        else:
            (entering,) = self.flight
        middle = self.early_factor * entering + self.early
        self.keep = jnp.where(self.late, middle, entering)
        self.send(jnp.where(self.late, entering, middle), self.swap)

    def result(self):
        return self.flight[0]


class Share:
    def __init__(self, pair, along, line):
        self.pair = pair
        self.line = line
        rows = pair[1].shape[1]
        cut = {"x": rows, "y": 0}.get(along, rows // 16 * 8)
        self.parts = [
            part for part in ((slice(0, cut), 0), (slice(cut, rows), 1)) if part[0].stop > part[0].start
        ]
        self.operands = pair
        self.flight = (pair[0],)
        self.stage = -1

    def along_packs(self, array, pairs):
        self.operands = (array,)
        self.flight = (lax.ppermute(array, "blk", pairs),)

    def along_chips(self, arrays, step):
        self.operands = tuple(arrays)
        self.flight = tuple(
            flip_with("chip", 1 << (first ^ step))(array)
            for array, (_, first) in zip(arrays, self.parts)
        )

    def go(self):
        self.stage += 1
        getattr(self, "stage_%d" % self.stage)()
        return self

    def stage_0(self):
        self.operands = self.flight
        self.flight = (flip_with("core", 1)(self.operands[0]),)

    def stage_1(self):
        keep, (got,) = self.pair[1], self.flight
        self.got = got
        blocks = (slice(1, 4, 2), slice(2, 4))
        self.along_chips(
            [keep[blocks[y], rows] + got[blocks[y], rows] for rows, y in self.parts], 0
        )

    def stage_2(self):
        keep, got = self.pair[1], self.got
        self.first = self.flight
        self.along_chips(
            [
                keep[2 - y, rows] + got[2 - y, rows] + first[1]
                for (rows, y), first in zip(self.parts, self.first)
            ],
            1,
        )

    def stage_3(self):
        keep, got = self.pair[1], self.got
        sums = [
            keep[0, rows] + got[0, rows] + first[0] + second
            for (rows, _), first, second in zip(self.parts, self.first, self.flight)
        ]
        self.own = sums[0] if len(sums) == 1 else jnp.concatenate(sums, axis=0)
        if self.line:
            self.along_packs(self.own, [(0, 1), (3, 2)])
        else:
            self.operands = self.flight = (self.own,)
            self.stage = 6

    def stage_4(self):
        self.inner = self.own + self.flight[0]
        self.along_packs(self.inner, [(1, 2), (2, 1)])

    def stage_5(self):
        self.total = self.inner + self.flight[0]
        self.along_packs(self.total, [(1, 0), (2, 3)])

    def stage_6(self):
        place = lax.axis_index("blk")
        middle = (place == 1) | (place == 2)
        self.operands = self.flight = (jnp.where(middle, self.total, self.flight[0]),)

    def result(self):
        while self.stage < 6:
            self.go()
        return self.flight[0]


class FarShare:
    def __init__(self, array):
        self.operands = self.flight = (array,)
        self.cut = array.shape[2] // 16 * 8
        self.stage = -1

    def go(self):
        self.stage += 1
        getattr(self, "stage_%d" % self.stage)()
        return self

    def along_chips(self, first, second, bits):
        self.operands = (first, second)
        self.flight = tuple(
            flip_with("chip", bit)(array) for array, bit in zip(self.operands, bits)
        )

    def stage_0(self):
        self.operands = self.flight
        self.flight = (
            lax.psum_scatter(
                self.operands[0], ("blk", "core"), scatter_dimension=0, tiled=True
            ),
        )

    def stage_1(self):
        self.blocks = self.flight[0][0]
        self.along_chips(self.blocks[1::2, : self.cut], self.blocks[2:, self.cut :], (1, 2))

    def stage_2(self):
        self.first, self.second = self.flight
        self.along_chips(
            self.blocks[2, : self.cut] + self.first[1],
            self.blocks[1, self.cut :] + self.second[1],
            (2, 1),
        )

    def stage_3(self):
        first, second = self.flight
        own = jnp.concatenate(
            [
                self.blocks[0, : self.cut] + self.first[0] + first,
                self.blocks[0, self.cut :] + self.second[0] + second,
            ],
            axis=0,
        )
        self.operands = (own,)
        self.flight = (lax.all_gather(own, "blk", axis=0, tiled=True),)

    def stage_4(self):
        self.operands = self.flight

    def result(self):
        return self.flight[0]


class WholeShare:
    def __init__(self, array, axis):
        self.operands = (array,)
        self.flight = (lax.psum_scatter(array, ("chip", "core"), scatter_dimension=axis, tiled=True),)

    def go(self):
        self.operands = ()
        return self

    def result(self):
        return self.flight[0]


def sum_packs(*shares):
    for share, total in zip(shares, lax.psum([share.flight[0] for share in shares], "blk")):
        share.flight = (total,)


class Bag:
    def __init__(self, **members):
        self.__dict__.update(members)


class Sequence:
    def __init__(self):
        self.last = ()

    def __call__(self, step, *arrays):
        arrays, _ = lax.optimization_barrier((arrays, self.last))
        results = step(*arrays)
        self.last = results
        return results

    def move(self, *items):
        for item in items:
            item.flight, _ = lax.optimization_barrier((item.flight, self.last))
            item.go()
            self.last = item.operands

    def wait(self, *items):
        for item in items:
            item.flight, _ = lax.optimization_barrier((item.flight, self.last))
            self.last = item.flight


def gelu_parts(inputs):
    square = inputs * inputs
    bent = jnp.tanh(GELU_SCALE * inputs * (1.0 + GELU_CUBE * square))
    half = 0.5 * (1.0 + bent)
    slope = half + 0.5 * inputs * (1.0 - bent * bent) * GELU_SCALE * (
        1.0 + 3.0 * GELU_CUBE * square
    )
    return inputs * half, slope


def gelu(inputs):
    return gelu_parts(inputs)[0]


def body(
    tokens,
    seq_lengths,
    ln_gain,
    ln_bias,
    w_one,
    w_two,
    w_three,
    w_four,
    readout,
    log_rate,
    cotangent,
):
    _, span, width = tokens.shape
    layers = w_one.shape[0]
    channels, states = readout.shape[1:]
    blocks = span // BLOCK
    chips = lax.axis_size("chip")
    devices = 2 * chips
    me = lax.axis_index(("chip", "core"))
    core = me % 2
    chip = me // 2
    custom = chips == 4 and lax.axis_size("blk") == 4
    upper, window, inverse, lower_inverse = fourier_tables()

    finish = jnp.cumsum(seq_lengths[0])
    begins = finish - seq_lengths[0]
    places = BLOCK * jnp.arange(devices * blocks, dtype=jnp.int32)
    opens = jnp.any(begins[:, None] == places[None, :], axis=0).reshape(devices, blocks)
    unbroken = jnp.logical_not(jnp.any(opens, axis=1))
    own_opens = lax.dynamic_index_in_dim(opens, me, 0, keepdims=False)
    segments = jnp.cumsum(own_opens.astype(jnp.int32))
    from_before = jnp.repeat((segments == 0).astype(jnp.float32), BLOCK)
    to_after = jnp.repeat((segments == segments[-1]).astype(jnp.float32), BLOCK)
    unbroken = unbroken.astype(jnp.float32)
    own_unbroken = (segments[-1] == 0).astype(jnp.float32)

    half = states // 2

    def turned(array):
        return by_core(core, array, jnp.concatenate([array[half:], array[:half]], axis=0))

    steps = jnp.arange(span, dtype=jnp.float32)

    def tables(layer):
        rates = jnp.exp(log_rate[layer])
        col = turned(rates)[:, None]
        row = turned(rates)[None, :]
        across, down = steps[None, :], steps[:, None]
        before_row, before_col = from_before[None, :], from_before[:, None]
        after_row, after_col = to_after[None, :], to_after[:, None]

        def low(array):
            return array.astype(jnp.bfloat16)

        return Bag(
            rates=rates,
            turned_factor=turned(rates * jnp.exp(-rates)),
            retain=-jnp.expm1(-rates),
            retain_column=-jnp.expm1(-col),
            leaving=low(after_row * jnp.exp((across - (span - 1.0)) * col)),
            leaving_down=low(after_col * jnp.exp((down - (span - 1.0)) * row)),
            leaving_slopes=low(
                after_row * (span - 1.0 - across) * jnp.exp((across - (span - 2.0)) * col)
            ),
            entering=low(before_row * jnp.exp(-(across + 1.0) * col)),
            entering_down=low(before_col * jnp.exp(-(down + 1.0) * row)),
            entering_slopes=low(before_row * (across + 1.0) * jnp.exp(-across * col)),
            powers=low(jnp.exp(-across * col)),
            slopes=low(across * jnp.exp(-(across - 1.0) * col)),
            through_slope=own_unbroken * span * jnp.exp(-(span - 1.0) * col),
            factors=unbroken[:, None] * jnp.exp(-span * row),
        )

    def layer_tables(layer, table):
        def made(readout, row, retain):
            upright, kernel = layer_kernel(layer, core[None], readout, row, retain, window, span)
            return upright, kernel

        return made, readout, table.rates[None], table.retain[None]

    def low_dot(first, second):
        return dot_plain(first, second.astype(jnp.bfloat16))

    def open_layer(layer, flat, table):
        mean = jnp.mean(flat, axis=-1, keepdims=True)
        center = flat - mean
        scale = lax.rsqrt(jnp.mean(center * center, axis=-1, keepdims=True) + 1e-05)
        normed = (center * scale * ln_gain[layer] + ln_bias[layer]).astype(jnp.bfloat16)
        value_pre = dot_plain(normed, w_two[layer])
        values = gelu(value_pre)
        state = low_dot(table.leaving, values)
        return mean, scale, normed, value_pre, values, state

    def share_of(name, pair):
        along = "x" if name in ALONG_X else "y" if name in ALONG_Y else "both"
        return Share(pair, along, not any(name in group for group in GROUPS))

    def share_grad(names, first, second):
        if custom and names[0] in FAR:
            made = sequence(
                lambda first, second: far_grad(
                    chip[None], first, second, chips, lax.axis_size("blk")
                ),
                first,
                second,
            )
            return [FarShare(made)]
        if custom:
            place = jnp.stack([chip, core])
            made = sequence(
                lambda first, second: weight_grad(place, first, second, chips, len(names)),
                first,
                second,
            )
            return [share_of(name, pair) for name, pair in zip(names, made)]
        return [
            WholeShare(sequence(dot_first, piece, second), 1)
            for piece in jnp.split(first, len(names), axis=1)
        ]

    def small_lines(two, grad_readout, gain_grad, bias_grad, grad_rate):
        def lines(array):
            return array.reshape(devices, -1, array.shape[-1])

        extra = jnp.concatenate(
            [part.reshape(devices, 1, -1) for part in (gain_grad, bias_grad, grad_rate)], axis=-1
        )
        wide = jnp.concatenate([lines(two), lines(grad_readout)], axis=-1)
        extra = jnp.pad(extra, ((0, 0), (0, 7), (0, wide.shape[-1] - extra.shape[-1])))
        return jnp.concatenate([wide, extra], axis=1)

    def small_share(name, first, second):
        if not custom:
            return WholeShare(jnp.concatenate([first, second], axis=1), 0)
        return share_of(
            name,
            tuple(jnp.concatenate(pair, axis=1) for pair in zip(first, second)),
        )

    def close_layer(layer, upstream, flat, mean, scale, grad_gate_pre, grad_value_pre):
        grad_normed = dot_last(grad_gate_pre, w_one[layer]) + dot_last(
            grad_value_pre, w_two[layer]
        )
        hat = (flat - mean) * scale
        gain_grad = jnp.sum(grad_normed * hat, axis=0)
        bias_grad = jnp.sum(grad_normed, axis=0)
        scaled = grad_normed * ln_gain[layer]
        grad_flat = upstream + scale * (
            scaled
            - jnp.mean(scaled, axis=-1, keepdims=True)
            - hat * jnp.mean(scaled * hat, axis=-1, keepdims=True)
        )
        return grad_flat, gain_grad, bias_grad

    def kernel_grads(
        table, upright, lag_sums, incoming, adjoint, pulled, grad_mixed, values
    ):
        mixing = upright * table.retain_column
        grad_mixing = low_dot(table.powers, lag_sums) + incoming * pulled
        grad_decays = jnp.sum(
            mixing
            * (
                low_dot(table.slopes, lag_sums)
                + incoming * low_dot(table.entering_slopes, grad_mixed)
            )
            + adjoint * low_dot(table.leaving_slopes, values)
            + table.through_slope * incoming * adjoint,
            axis=1,
        )
        grad_retain = jnp.sum(grad_mixing * upright, axis=1)
        grad_rate = table.turned_factor * (grad_retain - grad_decays)
        return grad_mixing * table.retain_column, grad_rate

    back_order = devices - 1 - me
    sequence = Sequence()
    move = sequence.move

    def start_carry(state, factors, order):
        carried = Carry(state, factors, order)
        sequence.last = carried.operands
        return carried

    def mix(local, table, upright, incoming):
        scaled = upright * table.retain_column * incoming
        return (local + low_dot(table.entering_down, scaled)).astype(jnp.bfloat16)

    def pull(grad_lifted, table, upright, layer):
        grad_mixed = dot_last(grad_lifted, w_three[layer])
        pulled = low_dot(table.entering, grad_mixed)
        return grad_mixed, pulled, upright * table.retain_column * pulled

    def gate_forward(layer, mixed, gate_pre):
        return gate_call(
            gate_forward_body, layer, mixed, w_three, (gate_pre,), False, "gate_forward"
        )

    def value_grad(table, local, adjoint, value_pre):
        grad_values = local + low_dot(table.leaving_down, adjoint)
        return (grad_values * gelu_parts(value_pre)[1]).astype(jnp.bfloat16)

    def small_grads(table, upright, grad_value_pre, normed, sums, gain_grad, bias_grad):
        def made(grad_value_pre, normed, gain_grad, bias_grad, *sums):
            two = dot_first(grad_value_pre, normed)
            grad_readout, grad_rate = kernel_grads(table, upright, *sums)
            return small_lines(
                two, turned(grad_readout), gain_grad, bias_grad, turned(grad_rate)
            )

        def made_pair(grad_value_pre, normed, gain_grad, bias_grad, *sums):
            grad_readout, grad_rate = kernel_grads(table, upright, *sums)
            place = jnp.stack([chip, core])
            return small_grad(
                place,
                grad_value_pre,
                normed,
                grad_readout,
                gain_grad[None],
                bias_grad[None],
                grad_rate[None],
                chips,
            )

        if custom:
            return sequence(made_pair, grad_value_pre, normed, gain_grad, bias_grad, *sums)

        return sequence(made, grad_value_pre, normed, gain_grad, bias_grad, *sums)

    conv_tables = (upper, inverse)
    back_tables = (upper, inverse, lower_inverse)

    flat0 = tokens.reshape(span, width)
    t0 = tables(0)
    t1 = tables(1)
    mean0, scale0, normed0, value_pre0, values0, state0 = open_layer(0, flat0, t0)
    c0 = start_carry(state0, t0.factors, me)
    upright0, kernel0 = sequence(*layer_tables(0, t0))
    move(c0)
    gate_pre0 = sequence(lambda normed: dot_plain(normed, w_one[0]), normed0)
    move(c0)
    local0 = sequence(conv_forward, segments, values0, kernel0, *conv_tables)
    upright1, kernel1 = sequence(*layer_tables(1, t1))
    move(c0, c0)
    mixed0 = sequence(lambda *arrays: mix(arrays[0], t0, *arrays[1:]), local0, upright0, c0.result())
    product0, bent0 = sequence(functools.partial(gate_forward, 0), mixed0, gate_pre0)
    flat1 = flat0 + dot_plain(product0, w_four[0])

    mean1, scale1, normed1, value_pre1, values1, state1 = open_layer(1, flat1, t1)
    c1 = start_carry(state1, t1.factors, me)
    gate_pre1 = sequence(lambda normed: dot_plain(normed, w_one[1]), normed1)
    move(c1)
    low_cotangent = cotangent.reshape(span, width).astype(jnp.bfloat16)
    grad_lifted1, grad_product1 = sequence(
        lambda low, gate_pre: gate_call(
            gate_early_body, 1, low, w_four, (gate_pre,), True, "gate_early"
        ),
        low_cotangent,
        gate_pre1,
    )
    move(c1)
    grad_mixed1, pulled1, leaving1 = sequence(
        lambda grad_lifted, upright: pull(grad_lifted, t1, upright, 1), grad_lifted1, upright1
    )
    b1 = start_carry(leaving1, t1.factors[::-1], back_order)
    local1 = sequence(conv_forward, segments, values1, kernel1, *conv_tables)
    move(c1, b1, c1)
    incoming1 = c1.result()
    mixed1 = sequence(lambda *arrays: mix(arrays[0], t1, *arrays[1:]), local1, upright1, incoming1)
    v = Bag()
    items = dict(b1=b1)

    def shares(names, first, second):
        names = names.split()
        items.update(zip(names, share_grad(names, first, second)))

    def gate1():
        v.product1, v.bent1 = sequence(
            functools.partial(gate_forward, 1), mixed1, gate_pre1
        )

    def conv1():
        v.gv1, v.lags1 = sequence(
            conv_backward, segments, values1, grad_mixed1, kernel1, *back_tables
        )

    def slope1():
        v.grad_gate1 = sequence(jnp.multiply, grad_product1, v.bent1)

    def value1():
        v.adjoint1 = items["b1"].result()
        v.grad_value1 = sequence(
            lambda *arrays: value_grad(t1, *arrays), v.gv1, v.adjoint1, value_pre1
        )

    def close1():
        v.upstream0, v.gain1, v.bias1 = sequence(
            functools.partial(close_layer, 1),
            cotangent.reshape(span, width),
            flat1,
            mean1,
            scale1,
            v.grad_gate1,
            v.grad_value1,
        )
        v.low0 = v.upstream0.astype(jnp.bfloat16)

    def gate0():
        v.grad_lifted0, v.grad_gate0 = sequence(
            lambda low, gate_pre, bent: gate_call(
                gate_backward_body, 0, low, w_four, (gate_pre, bent), True, "gate_backward"
            ),
            v.low0,
            gate_pre0,
            bent0,
        )

    def pull0():
        v.grad_mixed0, v.pulled0, leaving0 = sequence(
            lambda grad_lifted, upright: pull(grad_lifted, t0, upright, 0),
            v.grad_lifted0,
            upright0,
        )
        items["b0"] = start_carry(leaving0, t0.factors[::-1], back_order)

    def conv0():
        v.gv0, v.lags0 = sequence(
            conv_backward, segments, values0, v.grad_mixed0, kernel0, *back_tables
        )

    def value0():
        v.adjoint0 = items["b0"].result()
        v.grad_value0 = sequence(
            lambda *arrays: value_grad(t0, *arrays), v.gv0, v.adjoint0, value_pre0
        )

    def close0():
        v.grad_tokens, v.gain0, v.bias0 = sequence(
            functools.partial(close_layer, 0),
            v.upstream0,
            flat0,
            mean0,
            scale0,
            v.grad_gate0,
            v.grad_value0,
        )

    def lines1():
        sums = (v.lags1, incoming1, v.adjoint1, pulled1, grad_mixed1, values1)
        v.lines1 = small_grads(
            t1, upright1, v.grad_value1, normed1, sums, v.gain1, v.bias1
        )

    def lines0():
        sums = (v.lags0, c0.result(), v.adjoint0, v.pulled0, v.grad_mixed0, values0)
        v.lines0 = small_grads(
            t0, upright0, v.grad_value0, normed0, sums, v.gain0, v.bias0
        )

    def small():
        items["small"] = small_share("small", v.lines0, v.lines1)
        sequence.last = items["small"].operands

    def result():
        v.result = sequence(
            lambda flat, product: flat + dot_plain(product, w_four[1]), flat1, v.product1
        )

    actions = dict(
        gate1=gate1,
        conv1=conv1,
        slope1=slope1,
        value1=value1,
        close1=close1,
        gate0=gate0,
        pull0=pull0,
        conv0=conv0,
        value0=value0,
        close0=close0,
        lines1=lines1,
        lines0=lines0,
        lines=small,
        result=result,
        grad_three1=lambda: shares("three1", mixed1, grad_lifted1),
        grad_four1=lambda: shares(PARTS[0], v.product1, low_cotangent),
        grad_one1=lambda: shares(PARTS[1], normed1, v.grad_gate1),
        grad_four0=lambda: shares(PARTS[2], product0, v.low0),
        grad_one0=lambda: shares(PARTS[3], normed0, v.grad_gate0),
        grad_three0=lambda: shares("three0", mixed0, v.grad_lifted0),
    )
    for name in (NAMES[index] for index in ORDER):
        if name in actions:
            actions[name]()
        elif name[0] == "~":
            sequence.wait(items[name[1:]])
        else:
            move(items[name])
    if not custom:
        sum_packs(*[item for item in items.values() if isinstance(item, WholeShare)])
    flat, upstream = v.result, v.grad_tokens

    def whole(*names):
        return jnp.concatenate([items[name].result() for name in names], axis=0)

    collected = []
    lines = items["small"].result()
    lines = jnp.split(lines if custom else lines[0], 2, axis=0)
    for layer, small_rows in zip("01", lines):
        collected.append(
            [
                whole(*PARTS[2 - 2 * int(layer)].split()),
                whole("three" + layer),
                whole(*PARTS[3 - 2 * int(layer)].split()),
                small_rows,
            ]
        )

    def unpack(shares):
        four, three, one, small = shares
        rows = small.shape[0] - 8
        gains = width // devices
        rate_width = states // devices
        return (
            small[rows, :gains],
            small[rows, gains : 2 * gains],
            one,
            small[:rows, :width].T,
            three,
            four,
            small[:rows, width:].T,
            small[rows, 2 * gains : 2 * gains + rate_width],
        )

    parts = [unpack(shares) for shares in collected]
    stacked = [jnp.stack([part[member] for part in parts]) for member in range(8)]
    return (flat[None], upstream[None], *stacked)


def solution(mesh):
    packs = mesh.shape["blk"]
    mesh = jax.sharding.Mesh(mesh.devices.reshape(-1, 2, packs), SEQ + ("blk",))
    placed = (
        P("blk", SEQ, None),
        P("blk", None),
        P(),
        P(),
        P(),
        P(),
        P(),
        P(),
        P(),
        P(),
        P("blk", SEQ, None),
    )
    return jax.shard_map(
        body,
        mesh=mesh,
        in_specs=placed,
        out_specs=(
            P("blk", SEQ, None),
            P("blk", SEQ, None),
            P(None, SEQ),
            P(None, SEQ),
            P(None, None, SEQ),
            P(None, None, SEQ),
            P(None, None, SEQ),
            P(None, None, SEQ),
            P(None, None, SEQ),
            P(None, SEQ),
        ),
        check_vma=False,
    )
```

```python
import functools

import numpy as np

import jax
import jax.numpy as jnp
from jax import lax
from jax.experimental import pallas as pl
from jax.experimental.pallas import tpu as pltpu
from jax.sharding import PartitionSpec as P

BLOCK = 64
FREQS = 64
LANES = 128
GELU_SCALE = float(np.sqrt(2.0 / np.pi))
GELU_CUBE = 0.044715
MEBI = 1024 * 1024

SEQ = ("chip", "core")

NAMES = (
    "grad_three1", "three1", "gate1", "b1", "slope1", "grad_four1", "four1", "grad_one1", "one1", "conv1",
    "value1", "close1", "gate0", "grad_four0", "pull0", "b0", "grad_one0", "four0", "one0", "conv0", "lines1",
    "grad_three0", "value0", "close0", "lines0", "lines", "three0", "small", "result",
)
ORDER = (
    0, 1, 2, 3, 1, 4, 5, 6, 7, 3, 8, 3, 9, 8, 10, 11, 1, 12, 13, 8, 14, 1, 15, 16, 8, 15, 17, 18, 19, 17, 15,
    1, 18, 20, 15, 6, 21, 17, 8, 22, 6, 1, 17, 23, 24, 25, 1, 18, 17, 26, 8, 27, 6, 26, 27, 18, 8, 17, 27, 18,
    26, 27, 26, 18, 27, 6, 17, 26, 27, 18, 26, 27, 28, 26,
)
GROUPS = ()
ALONG_X = ()
ALONG_Y = ()
FAR = ("four1",)
PARTS = ("four1", "one1", "four0", "one0")


def fourier_tables():
    angles = (2.0 * np.pi / (2 * BLOCK)) * (np.arange(FREQS) + 0.5)[:, None]

    def forward(places):
        return np.concatenate([np.cos(angles * places), -np.sin(angles * places)], axis=0)

    def parts(table):
        table = np.asarray(table, np.float32)
        high = table.astype(jnp.bfloat16)
        rest = (table - high.astype(np.float32)).astype(jnp.bfloat16)
        return jnp.asarray(np.concatenate([high, high, rest], axis=1))

    upper = forward(np.arange(BLOCK)[None, :])
    lower = forward(np.arange(-BLOCK, 0)[None, :])
    lower[:, 0] = 0.0
    return (
        parts(upper),
        parts(np.concatenate([lower, upper], axis=1)),
        parts(upper.T / FREQS),
        parts(lower.T / FREQS),
    )


def three_parts(array):
    high = array.astype(jnp.bfloat16)
    rest = (array - high.astype(jnp.float32)).astype(jnp.bfloat16)
    return jnp.concatenate([high, rest, high], axis=0)


def beside(array, blocks):
    return jnp.concatenate(
        [array[block * BLOCK : (block + 1) * BLOCK] for block in range(blocks)], axis=1
    )


def dot_first(first, second, precision=None):
    return lax.dot_general(
        first,
        second,
        (((0,), (0,)), ((), ())),
        precision=precision,
        preferred_element_type=jnp.float32,
    )


def dot_last(first, second, precision=None):
    return lax.dot_general(
        first,
        second,
        (((1,), (1,)), ((), ())),
        precision=precision,
        preferred_element_type=jnp.float32,
    )


def dot_plain(first, second, precision=None):
    return jnp.dot(first, second, precision=precision, preferred_element_type=jnp.float32)


def layer_kernel_body(core_ref, readout_ref, rates_ref, retain_ref, window_ref, upright_ref, out_ref):
    blocks = out_ref.shape[0]
    tokens = blocks * BLOCK
    half = readout_ref.shape[1] // 2
    rates = rates_ref[...]
    decaying = jnp.exp(
        -lax.broadcasted_iota(jnp.int32, (tokens, 1), 0).astype(jnp.float32) * rates
    ).astype(jnp.bfloat16)
    readout = readout_ref[...]
    lags = dot_last(decaying, (readout * retain_ref[...]).astype(jnp.bfloat16))
    padded = jnp.concatenate([jnp.zeros((BLOCK, lags.shape[1]), jnp.float32), lags], axis=0)
    for step in range(blocks):
        window = padded[step * BLOCK : (step + 2) * BLOCK]
        out_ref[step] = dot_plain(window_ref[...], three_parts(window))
    upright = readout.T
    swapped = jnp.concatenate([upright[half:], upright[:half]], axis=0)
    upright_ref[...] = jnp.where(core_ref[0] == 0, upright, swapped)


def layer_kernel(layer, core, readout, rates, retain, window, tokens):
    _, channels, states = readout.shape
    blocks = tokens // BLOCK
    wide = 2 * LANES
    row = pl.BlockSpec((1, states), lambda i: (0, 0))
    return pl.pallas_call(
        layer_kernel_body,
        grid=(channels // wide,),
        in_specs=[
            pl.BlockSpec(memory_space=pltpu.SMEM),
            pl.BlockSpec((None, wide, states), lambda i: (layer, i, 0)),
            row,
            row,
            pl.BlockSpec(window.shape, lambda i: (0, 0)),
        ],
        out_specs=[
            pl.BlockSpec((states, wide), lambda i: (0, i)),
            pl.BlockSpec((blocks, 2 * FREQS, wide), lambda i: (0, 0, i)),
        ],
        out_shape=[
            jax.ShapeDtypeStruct((states, channels), jnp.float32),
            jax.ShapeDtypeStruct((blocks, 2 * FREQS, channels), jnp.float32),
        ],
        compiler_params=pltpu.CompilerParams(vmem_limit_bytes=12 * MEBI),
        cost_estimate=pl.CostEstimate(
            flops=8 * tokens * states * channels, bytes_accessed=8 * (states + tokens) * channels, transcendentals=0
        ),
        name="layer_kernel",
    )(core, readout, rates, retain, window)


def same_segment(segments_ref, first, second):
    return (segments_ref[first] == segments_ref[second]).astype(jnp.float32)


def keep_blocks(ref, array):
    for block in range(ref.shape[0]):
        ref[block] = array[:, block * LANES : (block + 1) * LANES]


def conv_forward_body(segments_ref, values_ref, kernel_ref, upper_ref, inverse_ref, out_ref, spec_ref):
    blocks = kernel_ref.shape[0]
    keep_blocks(spec_ref, dot_plain(upper_ref[...], three_parts(beside(values_ref[...], blocks))))
    sums = []
    for block in range(blocks):
        real = jnp.zeros((FREQS, LANES), jnp.float32)
        imag = jnp.zeros((FREQS, LANES), jnp.float32)
        for source in range(block + 1):
            lag = block - source
            mask = same_segment(segments_ref, block, source)
            kernel_real = kernel_ref[lag, :FREQS] * mask
            kernel_imag = kernel_ref[lag, FREQS:] * mask
            value_real = spec_ref[source, :FREQS]
            value_imag = spec_ref[source, FREQS:]
            real = real + (kernel_real * value_real - kernel_imag * value_imag)
            imag = imag + (kernel_real * value_imag + kernel_imag * value_real)
        sums.append(jnp.concatenate([real, imag], axis=0))
    out = dot_plain(inverse_ref[...], three_parts(jnp.concatenate(sums, axis=1)))
    for block in range(blocks):
        out_ref[block * BLOCK : (block + 1) * BLOCK, :] = out[:, block * LANES : (block + 1) * LANES]


def conv_forward(segments, values, kernel, upper, inverse):
    tokens, channels = values.shape
    blocks = tokens // BLOCK
    return pl.pallas_call(
        conv_forward_body,
        grid=(channels // LANES,),
        in_specs=[
            pl.BlockSpec(memory_space=pltpu.SMEM),
            pl.BlockSpec((tokens, LANES), lambda i: (0, i)),
            pl.BlockSpec((blocks, 2 * FREQS, LANES), lambda i: (0, 0, i)),
            pl.BlockSpec(upper.shape, lambda i: (0, 0)),
            pl.BlockSpec(inverse.shape, lambda i: (0, 0)),
        ],
        out_specs=pl.BlockSpec((tokens, LANES), lambda i: (0, i)),
        out_shape=jax.ShapeDtypeStruct((tokens, channels), jnp.float32),
        scratch_shapes=[pltpu.VMEM((blocks, 2 * FREQS, LANES), jnp.float32)],
        compiler_params=pltpu.CompilerParams(vmem_limit_bytes=10 * MEBI),
        cost_estimate=pl.CostEstimate(
            flops=2000 * tokens * channels, bytes_accessed=16 * tokens * channels, transcendentals=0
        ),
        name="conv_forward",
    )(segments, values, kernel, upper, inverse)


def conv_backward_body(
    segments_ref,
    values_ref,
    grads_ref,
    kernel_ref,
    upper_ref,
    inverse_ref,
    lower_inverse_ref,
    out_ref,
    lags_ref,
    value_spec_ref,
    grad_spec_ref,
):
    blocks = kernel_ref.shape[0]
    for spec_ref, in_ref in ((value_spec_ref, values_ref), (grad_spec_ref, grads_ref)):
        keep_blocks(spec_ref, dot_plain(upper_ref[...], three_parts(beside(in_ref[...], blocks))))
    sums = []
    for source in range(blocks):
        real = jnp.zeros((FREQS, LANES), jnp.float32)
        imag = jnp.zeros((FREQS, LANES), jnp.float32)
        for block in range(source, blocks):
            lag = block - source
            mask = same_segment(segments_ref, block, source)
            kernel_real = kernel_ref[lag, :FREQS] * mask
            kernel_imag = kernel_ref[lag, FREQS:] * mask
            grad_real = grad_spec_ref[block, :FREQS]
            grad_imag = grad_spec_ref[block, FREQS:]
            real = real + (kernel_real * grad_real + kernel_imag * grad_imag)
            imag = imag + (kernel_real * grad_imag - kernel_imag * grad_real)
        sums.append(jnp.concatenate([real, imag], axis=0))
    out = dot_plain(inverse_ref[...], three_parts(jnp.concatenate(sums, axis=1)))
    for block in range(blocks):
        out_ref[block * BLOCK : (block + 1) * BLOCK, :] = out[:, block * LANES : (block + 1) * LANES]
    sums = []
    for lag in range(blocks):
        real = jnp.zeros((FREQS, LANES), jnp.float32)
        imag = jnp.zeros((FREQS, LANES), jnp.float32)
        for source in range(blocks - lag):
            block = source + lag
            mask = same_segment(segments_ref, block, source)
            grad_real = grad_spec_ref[block, :FREQS] * mask
            grad_imag = grad_spec_ref[block, FREQS:] * mask
            value_real = value_spec_ref[source, :FREQS]
            value_imag = value_spec_ref[source, FREQS:]
            real = real + (grad_real * value_real + grad_imag * value_imag)
            imag = imag + (grad_imag * value_real - grad_real * value_imag)
        sums.append(jnp.concatenate([real, imag], axis=0))
    parts = three_parts(jnp.concatenate(sums, axis=1))
    here = dot_plain(inverse_ref[...], parts)
    behind = dot_plain(lower_inverse_ref[...], parts)
    for lag in range(blocks):
        lags = here[:, lag * LANES : (lag + 1) * LANES]
        if lag + 1 < blocks:
            lags = lags + behind[:, (lag + 1) * LANES : (lag + 2) * LANES]
        lags_ref[lag * BLOCK : (lag + 1) * BLOCK, :] = lags


def conv_backward(segments, values, grads, kernel, upper, inverse, lower_inverse):
    tokens, channels = values.shape
    blocks = tokens // BLOCK
    shape = jax.ShapeDtypeStruct((tokens, channels), jnp.float32)
    tall = pl.BlockSpec((tokens, LANES), lambda i: (0, i))
    return pl.pallas_call(
        conv_backward_body,
        grid=(channels // LANES,),
        in_specs=[
            pl.BlockSpec(memory_space=pltpu.SMEM),
            tall,
            tall,
            pl.BlockSpec((blocks, 2 * FREQS, LANES), lambda i: (0, 0, i)),
            pl.BlockSpec(upper.shape, lambda i: (0, 0)),
            pl.BlockSpec(inverse.shape, lambda i: (0, 0)),
            pl.BlockSpec(lower_inverse.shape, lambda i: (0, 0)),
        ],
        out_specs=[tall, tall],
        out_shape=[shape, shape],
        scratch_shapes=[pltpu.VMEM((blocks, 2 * FREQS, LANES), jnp.float32)] * 2,
        compiler_params=pltpu.CompilerParams(vmem_limit_bytes=12 * MEBI),
        cost_estimate=pl.CostEstimate(
            flops=4000 * tokens * channels, bytes_accessed=24 * tokens * channels, transcendentals=0
        ),
        name="conv_backward",
    )(segments, values, grads, kernel, upper, inverse, lower_inverse)


def weight_grad_body(place_ref, first_ref, second_ref, *out_refs):
    width = out_refs[0].shape[-1]
    second = second_ref[...]
    turned = jnp.concatenate([second[:, width:], second[:, :width]], axis=1)
    second = jnp.where(place_ref[1] == 0, second, turned)
    rows = out_refs[0].shape[1]
    for part in range(len(out_refs) // 2):
        both = dot_first(first_ref[:, part * rows : (part + 1) * rows], second)
        out_refs[2 * part][0] = both[:, width:]
        out_refs[2 * part + 1][0] = both[:, :width]


def weight_grad(place, first, second, chips, parts=1):
    tokens, rows = first.shape
    pair = second.shape[1] // chips
    width = pair // 2
    out = jax.ShapeDtypeStruct((chips, rows // parts, width), jnp.float32)
    outs = pl.pallas_call(
        weight_grad_body,
        grid_spec=pltpu.PrefetchScalarGridSpec(
            num_scalar_prefetch=1,
            grid=(chips,),
            in_specs=[
                pl.BlockSpec((tokens, rows), lambda j, place: (0, 0)),
                pl.BlockSpec((tokens, pair), lambda j, place: (0, jnp.bitwise_xor(j, place[0]))),
            ],
            out_specs=[pl.BlockSpec((1, rows // parts, width), lambda j, place: (j, 0, 0))]
            * (2 * parts),
        ),
        out_shape=[out] * (2 * parts),
        compiler_params=pltpu.CompilerParams(vmem_limit_bytes=24 * MEBI),
        cost_estimate=pl.CostEstimate(
            flops=2 * tokens * rows * second.shape[1], bytes_accessed=4 * rows * second.shape[1], transcendentals=0
        ),
        name="weight_grad",
    )(place, first, second)
    return [(outs[2 * part], outs[2 * part + 1]) for part in range(parts)]


def far_grad_body(chip_ref, first_ref, second_ref, out_ref):
    rows, width = out_ref.shape[2:]
    for part in range(out_ref.shape[0] // 2):
        both = dot_first(first_ref[:, part * rows : (part + 1) * rows], second_ref[...])
        out_ref[2 * part, 0] = both[:, :width]
        out_ref[2 * part + 1, 0] = both[:, width:]


def far_grad(chip, first, second, chips, packs):
    tokens, rows = first.shape
    pair = second.shape[1] // chips
    shape = (2 * packs, chips, rows // packs, pair // 2)
    return pl.pallas_call(
        far_grad_body,
        grid_spec=pltpu.PrefetchScalarGridSpec(
            num_scalar_prefetch=1,
            grid=(chips,),
            in_specs=[
                pl.BlockSpec((tokens, rows), lambda j, chip: (0, 0)),
                pl.BlockSpec((tokens, pair), lambda j, chip: (0, jnp.bitwise_xor(j, chip[0]))),
            ],
            out_specs=pl.BlockSpec((shape[0], 1) + shape[2:], lambda j, chip: (0, j, 0, 0)),
        ),
        out_shape=jax.ShapeDtypeStruct(shape, jnp.float32),
        compiler_params=pltpu.CompilerParams(vmem_limit_bytes=24 * MEBI),
        cost_estimate=pl.CostEstimate(
            flops=2 * tokens * rows * second.shape[1], bytes_accessed=4 * rows * second.shape[1], transcendentals=0
        ),
        name="far_grad",
    )(chip, first, second)


def small_grad_body(place_ref, first_ref, normed_ref, readout_ref, gain_ref, bias_ref, rate_ref, send_ref, keep_ref):
    two = dot_first(first_ref[...], normed_ref[...])
    wide = jnp.concatenate([two, readout_ref[...]], axis=1)
    rows = wide.shape[0] // 2
    segment = gain_ref.shape[1] // 2
    rates = rate_ref[...]
    turned_rates = pltpu.roll(rates, rows, axis=1)
    spare = jnp.zeros((1, wide.shape[1] - 2 * segment - rates.shape[1]), jnp.float32)
    shares = []
    for core, rate in ((0, rates), (1, turned_rates)):
        part = slice(core * segment, (core + 1) * segment)
        line = jnp.concatenate([gain_ref[:, part], bias_ref[:, part], rate, spare], axis=1)
        shares.append(
            jnp.concatenate(
                [wide[core * rows : (core + 1) * rows], jnp.broadcast_to(line, (8, line.shape[1]))],
                axis=0,
            )
        )
    mine = place_ref[1] == 0
    keep_ref[0] = jnp.where(mine, shares[0], shares[1])
    send_ref[0] = jnp.where(mine, shares[1], shares[0])


def small_grad(place, first, normed, grad_readout, gain, bias, rate, chips):
    tokens, channels = first.shape
    width = normed.shape[1]
    pair = channels // chips
    states = grad_readout.shape[0] // chips

    def natural(j, place):
        return jnp.bitwise_xor(j, place[0])

    def turned(j, place):
        return lax.rem(natural(j, place) + place[1] * (chips // 2), chips)

    out = jax.ShapeDtypeStruct(
        (chips, pair // 2 + 8, width + grad_readout.shape[1]), jnp.float32
    )
    out_spec = pl.BlockSpec((1,) + out.shape[1:], lambda j, place: (j, 0, 0))
    gains = pl.BlockSpec((1, width // chips), lambda j, place: (0, natural(j, place)))
    return pl.pallas_call(
        small_grad_body,
        grid_spec=pltpu.PrefetchScalarGridSpec(
            num_scalar_prefetch=1,
            grid=(chips,),
            in_specs=[
                pl.BlockSpec((tokens, pair), lambda j, place: (0, natural(j, place))),
                pl.BlockSpec((tokens, width), lambda j, place: (0, 0)),
                pl.BlockSpec(
                    (states, grad_readout.shape[1]), lambda j, place: (turned(j, place), 0)
                ),
                gains,
                gains,
                pl.BlockSpec((1, states), lambda j, place: (0, turned(j, place))),
            ],
            out_specs=[out_spec, out_spec],
        ),
        out_shape=[out, out],
        compiler_params=pltpu.CompilerParams(vmem_limit_bytes=16 * MEBI),
        cost_estimate=pl.CostEstimate(
            flops=2 * tokens * channels * width, bytes_accessed=8 * 1024 * 1024, transcendentals=0
        ),
        name="small_grad",
    )(place, first, normed, grad_readout, gain, bias, rate)


GATE_TILE = 512


def gate_forward_body(mixed_ref, weights_ref, gate_pre_ref, product_ref, bent_ref):
    lifted = dot_plain(mixed_ref[...], weights_ref[...])
    acts, slope = gelu_parts(gate_pre_ref[...])
    product_ref[...] = (acts * lifted).astype(jnp.bfloat16)
    bent_ref[...] = (slope * lifted).astype(jnp.bfloat16)


def gate_backward_body(low_ref, weights_ref, gate_pre_ref, bent_ref, lifted_ref, gate_ref):
    grads = dot_last(low_ref[...], weights_ref[...])
    acts = gelu(gate_pre_ref[...])
    lifted_ref[...] = (grads * acts).astype(jnp.bfloat16)
    gate_ref[...] = (grads * bent_ref[...]).astype(jnp.bfloat16)


def gate_early_body(low_ref, weights_ref, gate_pre_ref, lifted_ref, grads_ref):
    grads = dot_last(low_ref[...], weights_ref[...])
    lifted_ref[...] = (grads * gelu(gate_pre_ref[...])).astype(jnp.bfloat16)
    grads_ref[...] = grads.astype(jnp.bfloat16)


def gate_call(kernel, layer, left, weights, gated, upright, name):
    tokens, depth = left.shape
    gate = gated[0].shape[1]
    tile = pl.BlockSpec((tokens, GATE_TILE), lambda i: (0, i))
    if upright:
        weight_spec = pl.BlockSpec((None, GATE_TILE, depth), lambda i: (layer, i, 0))
    else:
        weight_spec = pl.BlockSpec((None, depth, GATE_TILE), lambda i: (layer, 0, i))
    out = jax.ShapeDtypeStruct((tokens, gate), jnp.bfloat16)
    return pl.pallas_call(
        kernel,
        grid=(gate // GATE_TILE,),
        in_specs=[pl.BlockSpec((tokens, depth), lambda i: (0, 0)), weight_spec]
        + [tile] * len(gated),
        out_specs=[tile, tile],
        out_shape=[out, out],
        compiler_params=pltpu.CompilerParams(vmem_limit_bytes=16 * MEBI),
        cost_estimate=pl.CostEstimate(
            flops=2 * tokens * depth * gate, bytes_accessed=2 * depth * gate + 10 * tokens * gate, transcendentals=0
        ),
        name=name,
    )(left, weights, *gated)


def flip_with(axis, bit):
    count = lax.axis_size(axis)
    pairs = [(device, device ^ bit) for device in range(count)]
    return lambda array: lax.ppermute(array, axis, pairs)


def by_core(core, zero, one):
    return jnp.where(core == 0, zero, one)


def prefix_join(prefix, partner, order, reach, factors):
    chips = factors.shape[0]
    places = jnp.arange(chips)
    start = (order // reach) * reach
    ahead = (places >= start) & (places < order)
    passed = jnp.prod(jnp.where(ahead[:, None], factors, 1.0), axis=0)
    return prefix + passed[:, None] * partner


def chip_scan_general(total, factors, order, chips):
    prefix = jnp.zeros_like(total)
    level = factors
    reach = 1
    while reach < chips:
        partner = flip_with("chip", reach)(total)
        group = order // reach
        sibling = lax.dynamic_index_in_dim(level, group ^ 1, 0, keepdims=False)
        mine = lax.dynamic_index_in_dim(level, group, 0, keepdims=False)
        late = (group % 2) == 1
        prefix = jnp.where(late, prefix_join(prefix, partner, order, reach, factors), prefix)
        total = jnp.where(late, mine[:, None] * partner + total, sibling[:, None] * total + partner)
        level = level[0::2] * level[1::2]
        reach *= 2
    return prefix


def column(table, index):
    return lax.dynamic_index_in_dim(table, index, 0, keepdims=False)[:, None]


class Carry:
    stages = 4

    def __init__(self, state, factors, order):
        half = state.shape[0] // 2
        self.half = half
        self.order = order
        self.square = factors.shape[0] == 8
        self.factors = factors[:, :half]
        self.chips = self.factors[0::2] * self.factors[1::2]
        self.own = state[:half]
        self.late = (order % 2) == 1
        self.swap = flip_with("core", 1)
        self.send(state[half:], self.swap)
        self.stage = 0

    def send(self, *pairs):
        self.operands = pairs[0::2]
        self.flight = tuple(way(array) for array, way in zip(pairs[0::2], pairs[1::2]))

    def go(self):
        self.stage += 1
        if self.stage == 1:
            self.total_of_chip()
            if self.square:
                self.first_round()
            else:
                entering = chip_scan_general(
                    self.total, self.chips, self.order // 2, self.chips.shape[0]
                )
                self.operands = self.flight = (entering,)
        elif self.stage == 2:
            if self.square:
                self.second_round()
        elif self.stage == 3:
            self.spread()
        else:
            self.operands = self.flight = (jnp.concatenate([self.keep, self.flight[0]], axis=0),)
        return self

    def total_of_chip(self):
        (received,) = self.flight
        self.early = jnp.where(self.late, received, self.own)
        after = jnp.where(self.late, self.own, received)
        last = self.order | 1
        self.early_factor = column(self.factors, last ^ 1)
        self.total = column(self.factors, last) * self.early + after

    def first_round(self):
        cut = self.half // 2
        self.along_x, self.along_y = flip_with("chip", 1), flip_with("chip", 2)
        self.first, self.second = self.total[:cut], self.total[cut:]
        self.send(self.first, self.along_x, self.second, self.along_y)

    def second_round(self):
        cut = self.half // 2
        place = self.order // 2
        self.place_x, self.place_y = place % 2, place // 2
        self.first_x, self.second_y = self.flight
        first_factors, second_factors = self.chips[:, :cut], self.chips[:, cut:]
        self.beside = column(first_factors, place ^ 1)
        row = jnp.where(
            self.place_x == 0,
            self.beside * self.first + self.first_x,
            column(first_factors, place) * self.first_x + self.first,
        )
        self.above, self.below = second_factors[1][:, None], second_factors[2][:, None]
        outgoing = jnp.where(
            self.place_y == 0,
            self.second,
            jnp.where(
                self.place_x == 0,
                self.below * self.above * self.second_y + self.second,
                self.second_y,
            ),
        )
        self.send(row, self.along_y, outgoing, self.along_x)

    def spread(self):
        if self.square:
            first_y, second_x = self.flight
            passed = jnp.where(self.place_x == 1, self.beside, 1.0)
            first = jnp.where(self.place_x == 1, self.first_x, 0.0) + jnp.where(
                self.place_y == 1, passed * first_y, 0.0
            )
            upper = jnp.where(self.place_x == 1, second_x, 0.0)
            lower = jnp.where(
                self.place_x == 0,
                self.above * self.second_y + second_x,
                second_x + self.below * self.second_y,
            )
            entering = jnp.concatenate([first, jnp.where(self.place_y == 0, upper, lower)], axis=0)
        else:
            (entering,) = self.flight
        middle = self.early_factor * entering + self.early
        self.keep = jnp.where(self.late, middle, entering)
        self.send(jnp.where(self.late, entering, middle), self.swap)

    def result(self):
        return self.flight[0]


class Share:
    def __init__(self, pair, along, line):
        self.pair = pair
        self.line = line
        rows = pair[1].shape[1]
        cut = {"x": rows, "y": 0}.get(along, rows // 16 * 8)
        self.parts = [
            part for part in ((slice(0, cut), 0), (slice(cut, rows), 1)) if part[0].stop > part[0].start
        ]
        self.operands = pair
        self.flight = (pair[0],)
        self.stage = -1

    def along_packs(self, array, pairs):
        self.operands = (array,)
        self.flight = (lax.ppermute(array, "blk", pairs),)

    def along_chips(self, arrays, step):
        self.operands = tuple(arrays)
        self.flight = tuple(
            flip_with("chip", 1 << (first ^ step))(array)
            for array, (_, first) in zip(arrays, self.parts)
        )

    def go(self):
        self.stage += 1
        getattr(self, "stage_%d" % self.stage)()
        return self

    def stage_0(self):
        self.operands = self.flight
        self.flight = (flip_with("core", 1)(self.operands[0]),)

    def stage_1(self):
        keep, (got,) = self.pair[1], self.flight
        self.got = got
        blocks = (slice(1, 4, 2), slice(2, 4))
        self.along_chips(
            [keep[blocks[y], rows] + got[blocks[y], rows] for rows, y in self.parts], 0
        )

    def stage_2(self):
        keep, got = self.pair[1], self.got
        self.first = self.flight
        self.along_chips(
            [
                keep[2 - y, rows] + got[2 - y, rows] + first[1]
                for (rows, y), first in zip(self.parts, self.first)
            ],
            1,
        )

    def stage_3(self):
        keep, got = self.pair[1], self.got
        sums = [
            keep[0, rows] + got[0, rows] + first[0] + second
            for (rows, _), first, second in zip(self.parts, self.first, self.flight)
        ]
        self.own = sums[0] if len(sums) == 1 else jnp.concatenate(sums, axis=0)
        if self.line:
            self.along_packs(self.own, [(0, 1), (3, 2)])
        else:
            self.operands = self.flight = (self.own,)
            self.stage = 6

    def stage_4(self):
        self.inner = self.own + self.flight[0]
        self.along_packs(self.inner, [(1, 2), (2, 1)])

    def stage_5(self):
        self.total = self.inner + self.flight[0]
        self.along_packs(self.total, [(1, 0), (2, 3)])

    def stage_6(self):
        place = lax.axis_index("blk")
        middle = (place == 1) | (place == 2)
        self.operands = self.flight = (jnp.where(middle, self.total, self.flight[0]),)

    def result(self):
        while self.stage < 6:
            self.go()
        return self.flight[0]


class FarShare:
    def __init__(self, array):
        self.operands = self.flight = (array,)
        self.cut = array.shape[2] // 16 * 8
        self.stage = -1

    def go(self):
        self.stage += 1
        getattr(self, "stage_%d" % self.stage)()
        return self

    def along_chips(self, first, second, bits):
        self.operands = (first, second)
        self.flight = tuple(
            flip_with("chip", bit)(array) for array, bit in zip(self.operands, bits)
        )

    def stage_0(self):
        self.operands = self.flight
        self.flight = (
            lax.psum_scatter(
                self.operands[0], ("blk", "core"), scatter_dimension=0, tiled=True
            ),
        )

    def stage_1(self):
        self.blocks = self.flight[0][0]
        self.along_chips(self.blocks[1::2, : self.cut], self.blocks[2:, self.cut :], (1, 2))

    def stage_2(self):
        self.first, self.second = self.flight
        self.along_chips(
            self.blocks[2, : self.cut] + self.first[1],
            self.blocks[1, self.cut :] + self.second[1],
            (2, 1),
        )

    def stage_3(self):
        first, second = self.flight
        own = jnp.concatenate(
            [
                self.blocks[0, : self.cut] + self.first[0] + first,
                self.blocks[0, self.cut :] + self.second[0] + second,
            ],
            axis=0,
        )
        self.operands = (own,)
        self.flight = (lax.all_gather(own, "blk", axis=0, tiled=True),)

    def stage_4(self):
        self.operands = self.flight

    def result(self):
        return self.flight[0]


class WholeShare:
    def __init__(self, array, axis):
        self.operands = (array,)
        self.flight = (lax.psum_scatter(array, ("chip", "core"), scatter_dimension=axis, tiled=True),)

    def go(self):
        self.operands = ()
        return self

    def result(self):
        return self.flight[0]


def sum_packs(*shares):
    for share, total in zip(shares, lax.psum([share.flight[0] for share in shares], "blk")):
        share.flight = (total,)


class Bag:
    def __init__(self, **members):
        self.__dict__.update(members)


class Sequence:
    def __init__(self):
        self.last = ()

    def __call__(self, step, *arrays):
        arrays, _ = lax.optimization_barrier((arrays, self.last))
        results = step(*arrays)
        self.last = results
        return results

    def move(self, *items):
        for item in items:
            item.flight, _ = lax.optimization_barrier((item.flight, self.last))
            item.go()
            self.last = item.operands

    def wait(self, *items):
        for item in items:
            item.flight, _ = lax.optimization_barrier((item.flight, self.last))
            self.last = item.flight


def gelu_parts(inputs):
    square = inputs * inputs
    bent = jnp.tanh(GELU_SCALE * inputs * (1.0 + GELU_CUBE * square))
    half = 0.5 * (1.0 + bent)
    slope = half + 0.5 * inputs * (1.0 - bent * bent) * GELU_SCALE * (
        1.0 + 3.0 * GELU_CUBE * square
    )
    return inputs * half, slope


def gelu(inputs):
    return gelu_parts(inputs)[0]


def body(
    tokens,
    seq_lengths,
    ln_gain,
    ln_bias,
    w_one,
    w_two,
    w_three,
    w_four,
    readout,
    log_rate,
    cotangent,
):
    _, span, width = tokens.shape
    layers = w_one.shape[0]
    channels, states = readout.shape[1:]
    blocks = span // BLOCK
    chips = lax.axis_size("chip")
    devices = 2 * chips
    me = lax.axis_index(("chip", "core"))
    core = me % 2
    chip = me // 2
    custom = chips == 4 and lax.axis_size("blk") == 4
    upper, window, inverse, lower_inverse = fourier_tables()

    finish = jnp.cumsum(seq_lengths[0])
    begins = finish - seq_lengths[0]
    places = BLOCK * jnp.arange(devices * blocks, dtype=jnp.int32)
    opens = jnp.any(begins[:, None] == places[None, :], axis=0).reshape(devices, blocks)
    unbroken = jnp.logical_not(jnp.any(opens, axis=1))
    own_opens = lax.dynamic_index_in_dim(opens, me, 0, keepdims=False)
    segments = jnp.cumsum(own_opens.astype(jnp.int32))
    from_before = jnp.repeat((segments == 0).astype(jnp.float32), BLOCK)
    to_after = jnp.repeat((segments == segments[-1]).astype(jnp.float32), BLOCK)
    unbroken = unbroken.astype(jnp.float32)
    own_unbroken = (segments[-1] == 0).astype(jnp.float32)

    half = states // 2

    def turned(array):
        return by_core(core, array, jnp.concatenate([array[half:], array[:half]], axis=0))

    steps = jnp.arange(span, dtype=jnp.float32)

    def tables(layer):
        rates = jnp.exp(log_rate[layer])
        col = turned(rates)[:, None]
        row = turned(rates)[None, :]
        across, down = steps[None, :], steps[:, None]
        before_row, before_col = from_before[None, :], from_before[:, None]
        after_row, after_col = to_after[None, :], to_after[:, None]

        def low(array):
            return array.astype(jnp.bfloat16)

        return Bag(
            rates=rates,
            turned_factor=turned(rates * jnp.exp(-rates)),
            retain=-jnp.expm1(-rates),
            retain_column=-jnp.expm1(-col),
            leaving=low(after_row * jnp.exp((across - (span - 1.0)) * col)),
            leaving_down=low(after_col * jnp.exp((down - (span - 1.0)) * row)),
            leaving_slopes=low(
                after_row * (span - 1.0 - across) * jnp.exp((across - (span - 2.0)) * col)
            ),
            entering=low(before_row * jnp.exp(-(across + 1.0) * col)),
            entering_down=low(before_col * jnp.exp(-(down + 1.0) * row)),
            entering_slopes=low(before_row * (across + 1.0) * jnp.exp(-across * col)),
            powers=low(jnp.exp(-across * col)),
            slopes=low(across * jnp.exp(-(across - 1.0) * col)),
            through_slope=own_unbroken * span * jnp.exp(-(span - 1.0) * col),
            factors=unbroken[:, None] * jnp.exp(-span * row),
        )

    def layer_tables(layer, table):
        def made(readout, row, retain):
            upright, kernel = layer_kernel(layer, core[None], readout, row, retain, window, span)
            return upright, kernel

        return made, readout, table.rates[None], table.retain[None]

    def low_dot(first, second):
        return dot_plain(first, second.astype(jnp.bfloat16))

    def open_layer(layer, flat, table):
        mean = jnp.mean(flat, axis=-1, keepdims=True)
        center = flat - mean
        scale = lax.rsqrt(jnp.mean(center * center, axis=-1, keepdims=True) + 1e-05)
        normed = (center * scale * ln_gain[layer] + ln_bias[layer]).astype(jnp.bfloat16)
        value_pre = dot_plain(normed, w_two[layer])
        values = gelu(value_pre)
        state = low_dot(table.leaving, values)
        return mean, scale, normed, value_pre, values, state

    def share_of(name, pair):
        along = "x" if name in ALONG_X else "y" if name in ALONG_Y else "both"
        return Share(pair, along, not any(name in group for group in GROUPS))

    def share_grad(names, first, second):
        if custom and names[0] in FAR:
            made = sequence(
                lambda first, second: far_grad(
                    chip[None], first, second, chips, lax.axis_size("blk")
                ),
                first,
                second,
            )
            return [FarShare(made)]
        if custom:
            place = jnp.stack([chip, core])
            made = sequence(
                lambda first, second: weight_grad(place, first, second, chips, len(names)),
                first,
                second,
            )
            return [share_of(name, pair) for name, pair in zip(names, made)]
        return [
            WholeShare(sequence(dot_first, piece, second), 1)
            for piece in jnp.split(first, len(names), axis=1)
        ]

    def small_lines(two, grad_readout, gain_grad, bias_grad, grad_rate):
        def lines(array):
            return array.reshape(devices, -1, array.shape[-1])

        extra = jnp.concatenate(
            [part.reshape(devices, 1, -1) for part in (gain_grad, bias_grad, grad_rate)], axis=-1
        )
        wide = jnp.concatenate([lines(two), lines(grad_readout)], axis=-1)
        extra = jnp.pad(extra, ((0, 0), (0, 7), (0, wide.shape[-1] - extra.shape[-1])))
        return jnp.concatenate([wide, extra], axis=1)

    def small_share(name, first, second):
        if not custom:
            return WholeShare(jnp.concatenate([first, second], axis=1), 0)
        return share_of(
            name,
            tuple(jnp.concatenate(pair, axis=1) for pair in zip(first, second)),
        )

    def close_layer(layer, upstream, flat, mean, scale, grad_gate_pre, grad_value_pre):
        grad_normed = dot_last(grad_gate_pre, w_one[layer]) + dot_last(
            grad_value_pre, w_two[layer]
        )
        hat = (flat - mean) * scale
        gain_grad = jnp.sum(grad_normed * hat, axis=0)
        bias_grad = jnp.sum(grad_normed, axis=0)
        scaled = grad_normed * ln_gain[layer]
        grad_flat = upstream + scale * (
            scaled
            - jnp.mean(scaled, axis=-1, keepdims=True)
            - hat * jnp.mean(scaled * hat, axis=-1, keepdims=True)
        )
        return grad_flat, gain_grad, bias_grad

    def kernel_grads(
        table, upright, lag_sums, incoming, adjoint, pulled, grad_mixed, values
    ):
        mixing = upright * table.retain_column
        grad_mixing = low_dot(table.powers, lag_sums) + incoming * pulled
        grad_decays = jnp.sum(
            mixing
            * (
                low_dot(table.slopes, lag_sums)
                + incoming * low_dot(table.entering_slopes, grad_mixed)
            )
            + adjoint * low_dot(table.leaving_slopes, values)
            + table.through_slope * incoming * adjoint,
            axis=1,
        )
        grad_retain = jnp.sum(grad_mixing * upright, axis=1)
        grad_rate = table.turned_factor * (grad_retain - grad_decays)
        return grad_mixing * table.retain_column, grad_rate

    back_order = devices - 1 - me
    sequence = Sequence()
    move = sequence.move

    def start_carry(state, factors, order):
        carried = Carry(state, factors, order)
        sequence.last = carried.operands
        return carried

    def mix(local, table, upright, incoming):
        scaled = upright * table.retain_column * incoming
        return (local + low_dot(table.entering_down, scaled)).astype(jnp.bfloat16)

    def pull(grad_lifted, table, upright, layer):
        grad_mixed = dot_last(grad_lifted, w_three[layer])
        pulled = low_dot(table.entering, grad_mixed)
        return grad_mixed, pulled, upright * table.retain_column * pulled

    def gate_forward(layer, mixed, gate_pre):
        return gate_call(
            gate_forward_body, layer, mixed, w_three, (gate_pre,), False, "gate_forward"
        )

    def value_grad(table, local, adjoint, value_pre):
        grad_values = local + low_dot(table.leaving_down, adjoint)
        return (grad_values * gelu_parts(value_pre)[1]).astype(jnp.bfloat16)

    def small_grads(table, upright, grad_value_pre, normed, sums, gain_grad, bias_grad):
        def made(grad_value_pre, normed, gain_grad, bias_grad, *sums):
            two = dot_first(grad_value_pre, normed)
            grad_readout, grad_rate = kernel_grads(table, upright, *sums)
            return small_lines(
                two, turned(grad_readout), gain_grad, bias_grad, turned(grad_rate)
            )

        def made_pair(grad_value_pre, normed, gain_grad, bias_grad, *sums):
            grad_readout, grad_rate = kernel_grads(table, upright, *sums)
            place = jnp.stack([chip, core])
            return small_grad(
                place,
                grad_value_pre,
                normed,
                grad_readout,
                gain_grad[None],
                bias_grad[None],
                grad_rate[None],
                chips,
            )

        if custom:
            return sequence(made_pair, grad_value_pre, normed, gain_grad, bias_grad, *sums)

        return sequence(made, grad_value_pre, normed, gain_grad, bias_grad, *sums)

    conv_tables = (upper, inverse)
    back_tables = (upper, inverse, lower_inverse)

    flat0 = tokens.reshape(span, width)
    t0 = tables(0)
    t1 = tables(1)
    mean0, scale0, normed0, value_pre0, values0, state0 = open_layer(0, flat0, t0)
    c0 = start_carry(state0, t0.factors, me)
    upright0, kernel0 = sequence(*layer_tables(0, t0))
    move(c0)
    gate_pre0 = sequence(lambda normed: dot_plain(normed, w_one[0]), normed0)
    move(c0)
    local0 = sequence(conv_forward, segments, values0, kernel0, *conv_tables)
    upright1, kernel1 = sequence(*layer_tables(1, t1))
    move(c0, c0)
    mixed0 = sequence(lambda *arrays: mix(arrays[0], t0, *arrays[1:]), local0, upright0, c0.result())
    product0, bent0 = sequence(functools.partial(gate_forward, 0), mixed0, gate_pre0)
    flat1 = flat0 + dot_plain(product0, w_four[0])

    mean1, scale1, normed1, value_pre1, values1, state1 = open_layer(1, flat1, t1)
    c1 = start_carry(state1, t1.factors, me)
    gate_pre1 = sequence(lambda normed: dot_plain(normed, w_one[1]), normed1)
    move(c1)
    low_cotangent = cotangent.reshape(span, width).astype(jnp.bfloat16)
    grad_lifted1, grad_product1 = sequence(
        lambda low, gate_pre: gate_call(
            gate_early_body, 1, low, w_four, (gate_pre,), True, "gate_early"
        ),
        low_cotangent,
        gate_pre1,
    )
    move(c1)
    grad_mixed1, pulled1, leaving1 = sequence(
        lambda grad_lifted, upright: pull(grad_lifted, t1, upright, 1), grad_lifted1, upright1
    )
    b1 = start_carry(leaving1, t1.factors[::-1], back_order)
    local1 = sequence(conv_forward, segments, values1, kernel1, *conv_tables)
    move(c1, b1, c1)
    incoming1 = c1.result()
    mixed1 = sequence(lambda *arrays: mix(arrays[0], t1, *arrays[1:]), local1, upright1, incoming1)
    v = Bag()
    items = dict(b1=b1)

    def shares(names, first, second):
        names = names.split()
        items.update(zip(names, share_grad(names, first, second)))

    def gate1():
        v.product1, v.bent1 = sequence(
            functools.partial(gate_forward, 1), mixed1, gate_pre1
        )

    def conv1():
        v.gv1, v.lags1 = sequence(
            conv_backward, segments, values1, grad_mixed1, kernel1, *back_tables
        )

    def slope1():
        v.grad_gate1 = sequence(jnp.multiply, grad_product1, v.bent1)

    def value1():
        v.adjoint1 = items["b1"].result()
        v.grad_value1 = sequence(
            lambda *arrays: value_grad(t1, *arrays), v.gv1, v.adjoint1, value_pre1
        )

    def close1():
        v.upstream0, v.gain1, v.bias1 = sequence(
            functools.partial(close_layer, 1),
            cotangent.reshape(span, width),
            flat1,
            mean1,
            scale1,
            v.grad_gate1,
            v.grad_value1,
        )
        v.low0 = v.upstream0.astype(jnp.bfloat16)

    def gate0():
        v.grad_lifted0, v.grad_gate0 = sequence(
            lambda low, gate_pre, bent: gate_call(
                gate_backward_body, 0, low, w_four, (gate_pre, bent), True, "gate_backward"
            ),
            v.low0,
            gate_pre0,
            bent0,
        )

    def pull0():
        v.grad_mixed0, v.pulled0, leaving0 = sequence(
            lambda grad_lifted, upright: pull(grad_lifted, t0, upright, 0),
            v.grad_lifted0,
            upright0,
        )
        items["b0"] = start_carry(leaving0, t0.factors[::-1], back_order)

    def conv0():
        v.gv0, v.lags0 = sequence(
            conv_backward, segments, values0, v.grad_mixed0, kernel0, *back_tables
        )

    def value0():
        v.adjoint0 = items["b0"].result()
        v.grad_value0 = sequence(
            lambda *arrays: value_grad(t0, *arrays), v.gv0, v.adjoint0, value_pre0
        )

    def close0():
        v.grad_tokens, v.gain0, v.bias0 = sequence(
            functools.partial(close_layer, 0),
            v.upstream0,
            flat0,
            mean0,
            scale0,
            v.grad_gate0,
            v.grad_value0,
        )

    def lines1():
        sums = (v.lags1, incoming1, v.adjoint1, pulled1, grad_mixed1, values1)
        v.lines1 = small_grads(
            t1, upright1, v.grad_value1, normed1, sums, v.gain1, v.bias1
        )

    def lines0():
        sums = (v.lags0, c0.result(), v.adjoint0, v.pulled0, v.grad_mixed0, values0)
        v.lines0 = small_grads(
            t0, upright0, v.grad_value0, normed0, sums, v.gain0, v.bias0
        )

    def small():
        items["small"] = small_share("small", v.lines0, v.lines1)
        sequence.last = items["small"].operands

    def result():
        v.result = sequence(
            lambda flat, product: flat + dot_plain(product, w_four[1]), flat1, v.product1
        )

    actions = dict(
        gate1=gate1,
        conv1=conv1,
        slope1=slope1,
        value1=value1,
        close1=close1,
        gate0=gate0,
        pull0=pull0,
        conv0=conv0,
        value0=value0,
        close0=close0,
        lines1=lines1,
        lines0=lines0,
        lines=small,
        result=result,
        grad_three1=lambda: shares("three1", mixed1, grad_lifted1),
        grad_four1=lambda: shares(PARTS[0], v.product1, low_cotangent),
        grad_one1=lambda: shares(PARTS[1], normed1, v.grad_gate1),
        grad_four0=lambda: shares(PARTS[2], product0, v.low0),
        grad_one0=lambda: shares(PARTS[3], normed0, v.grad_gate0),
        grad_three0=lambda: shares("three0", mixed0, v.grad_lifted0),
    )
    for name in (NAMES[index] for index in ORDER):
        if name in actions:
            actions[name]()
        elif name[0] == "~":
            sequence.wait(items[name[1:]])
        else:
            move(items[name])
    if not custom:
        sum_packs(*[item for item in items.values() if isinstance(item, WholeShare)])
    flat, upstream = v.result, v.grad_tokens

    def whole(*names):
        return jnp.concatenate([items[name].result() for name in names], axis=0)

    collected = []
    lines = items["small"].result()
    lines = jnp.split(lines if custom else lines[0], 2, axis=0)
    for layer, small_rows in zip("01", lines):
        collected.append(
            [
                whole(*PARTS[2 - 2 * int(layer)].split()),
                whole("three" + layer),
                whole(*PARTS[3 - 2 * int(layer)].split()),
                small_rows,
            ]
        )

    def unpack(shares):
        four, three, one, small = shares
        rows = small.shape[0] - 8
        gains = width // devices
        rate_width = states // devices
        return (
            small[rows, :gains],
            small[rows, gains : 2 * gains],
            one,
            small[:rows, :width].T,
            three,
            four,
            small[:rows, width:].T,
            small[rows, 2 * gains : 2 * gains + rate_width],
        )

    parts = [unpack(shares) for shares in collected]
    stacked = [jnp.stack([part[member] for part in parts]) for member in range(8)]
    return (flat[None], upstream[None], *stacked)


def solution(mesh):
    packs = mesh.shape["blk"]
    mesh = jax.sharding.Mesh(mesh.devices.reshape(-1, 2, packs), SEQ + ("blk",))
    placed = (
        P("blk", SEQ, None),
        P("blk", None),
        P(),
        P(),
        P(),
        P(),
        P(),
        P(),
        P(),
        P(),
        P("blk", SEQ, None),
    )
    return jax.shard_map(
        body,
        mesh=mesh,
        in_specs=placed,
        out_specs=(
            P("blk", SEQ, None),
            P("blk", SEQ, None),
            P(None, SEQ),
            P(None, SEQ),
            P(None, None, SEQ),
            P(None, None, SEQ),
            P(None, None, SEQ),
            P(None, None, SEQ),
            P(None, None, SEQ),
            P(None, SEQ),
        ),
        check_vma=False,
    )
```

```python
import functools

import numpy as np

import jax
import jax.numpy as jnp
from jax import lax
from jax.experimental import pallas as pl
from jax.experimental.pallas import tpu as pltpu
from jax.sharding import PartitionSpec as P

BLOCK = 64
FREQS = 64
LANES = 128
GELU_SCALE = float(np.sqrt(2.0 / np.pi))
GELU_CUBE = 0.044715
MEBI = 1024 * 1024

SEQ = ("chip", "core")

NAMES = (
    "grad_three1", "three1", "gate1", "b1", "slope1", "grad_four1", "four1", "grad_one1", "one1", "conv1",
    "value1", "close1", "gate0", "grad_four0", "pull0", "b0", "grad_one0", "four0", "one0", "conv0", "lines1",
    "grad_three0", "value0", "close0", "lines0", "lines", "three0", "small", "result",
)
ORDER = (
    0, 1, 2, 3, 1, 4, 5, 6, 7, 3, 8, 3, 9, 8, 10, 11, 1, 12, 13, 8, 14, 1, 15, 16, 8, 15, 17, 18, 19, 17, 15,
    1, 18, 20, 15, 6, 21, 17, 8, 22, 6, 1, 17, 23, 24, 25, 1, 18, 17, 26, 8, 27, 6, 26, 27, 18, 8, 17, 27, 18,
    26, 27, 26, 18, 27, 6, 17, 26, 27, 18, 26, 27, 28, 26,
)
GROUPS = ()
ALONG_X = ()
ALONG_Y = ()
FAR = ("four1",)
PARTS = ("four1", "one1", "four0", "one0")


def fourier_tables():
    angles = (2.0 * np.pi / (2 * BLOCK)) * (np.arange(FREQS) + 0.5)[:, None]

    def forward(places):
        return np.concatenate([np.cos(angles * places), -np.sin(angles * places)], axis=0)

    def parts(table):
        table = np.asarray(table, np.float32)
        high = table.astype(jnp.bfloat16)
        rest = (table - high.astype(np.float32)).astype(jnp.bfloat16)
        return jnp.asarray(np.concatenate([high, high, rest], axis=1))

    upper = forward(np.arange(BLOCK)[None, :])
    lower = forward(np.arange(-BLOCK, 0)[None, :])
    lower[:, 0] = 0.0
    return (
        parts(upper),
        parts(np.concatenate([lower, upper], axis=1)),
        parts(upper.T / FREQS),
        parts(lower.T / FREQS),
    )


def three_parts(array):
    high = array.astype(jnp.bfloat16)
    rest = (array - high.astype(jnp.float32)).astype(jnp.bfloat16)
    return jnp.concatenate([high, rest, high], axis=0)


def beside(array, blocks):
    return jnp.concatenate(
        [array[block * BLOCK : (block + 1) * BLOCK] for block in range(blocks)], axis=1
    )


def dot_first(first, second, precision=None):
    return lax.dot_general(
        first,
        second,
        (((0,), (0,)), ((), ())),
        precision=precision,
        preferred_element_type=jnp.float32,
    )


def dot_last(first, second, precision=None):
    return lax.dot_general(
        first,
        second,
        (((1,), (1,)), ((), ())),
        precision=precision,
        preferred_element_type=jnp.float32,
    )


def dot_plain(first, second, precision=None):
    return jnp.dot(first, second, precision=precision, preferred_element_type=jnp.float32)


def layer_kernel_body(core_ref, readout_ref, rates_ref, retain_ref, window_ref, upright_ref, out_ref):
    blocks = out_ref.shape[0]
    tokens = blocks * BLOCK
    half = readout_ref.shape[1] // 2
    rates = rates_ref[...]
    decaying = jnp.exp(
        -lax.broadcasted_iota(jnp.int32, (tokens, 1), 0).astype(jnp.float32) * rates
    ).astype(jnp.bfloat16)
    readout = readout_ref[...]
    lags = dot_last(decaying, (readout * retain_ref[...]).astype(jnp.bfloat16))
    padded = jnp.concatenate([jnp.zeros((BLOCK, lags.shape[1]), jnp.float32), lags], axis=0)
    for step in range(blocks):
        window = padded[step * BLOCK : (step + 2) * BLOCK]
        out_ref[step] = dot_plain(window_ref[...], three_parts(window))
    upright = readout.T
    swapped = jnp.concatenate([upright[half:], upright[:half]], axis=0)
    upright_ref[...] = jnp.where(core_ref[0] == 0, upright, swapped)


def layer_kernel(layer, core, readout, rates, retain, window, tokens):
    _, channels, states = readout.shape
    blocks = tokens // BLOCK
    wide = 2 * LANES
    row = pl.BlockSpec((1, states), lambda i: (0, 0))
    return pl.pallas_call(
        layer_kernel_body,
        grid=(channels // wide,),
        in_specs=[
            pl.BlockSpec(memory_space=pltpu.SMEM),
            pl.BlockSpec((None, wide, states), lambda i: (layer, i, 0)),
            row,
            row,
            pl.BlockSpec(window.shape, lambda i: (0, 0)),
        ],
        out_specs=[
            pl.BlockSpec((states, wide), lambda i: (0, i)),
            pl.BlockSpec((blocks, 2 * FREQS, wide), lambda i: (0, 0, i)),
        ],
        out_shape=[
            jax.ShapeDtypeStruct((states, channels), jnp.float32),
            jax.ShapeDtypeStruct((blocks, 2 * FREQS, channels), jnp.float32),
        ],
        compiler_params=pltpu.CompilerParams(vmem_limit_bytes=12 * MEBI),
        cost_estimate=pl.CostEstimate(
            flops=8 * tokens * states * channels, bytes_accessed=8 * (states + tokens) * channels, transcendentals=0
        ),
        name="layer_kernel",
    )(core, readout, rates, retain, window)


def same_segment(segments_ref, first, second):
    return (segments_ref[first] == segments_ref[second]).astype(jnp.float32)


def keep_blocks(ref, array):
    for block in range(ref.shape[0]):
        ref[block] = array[:, block * LANES : (block + 1) * LANES]


def conv_forward_body(segments_ref, values_ref, kernel_ref, upper_ref, inverse_ref, out_ref, spec_ref):
    blocks = kernel_ref.shape[0]
    keep_blocks(spec_ref, dot_plain(upper_ref[...], three_parts(beside(values_ref[...], blocks))))
    sums = []
    for block in range(blocks):
        real = jnp.zeros((FREQS, LANES), jnp.float32)
        imag = jnp.zeros((FREQS, LANES), jnp.float32)
        for source in range(block + 1):
            lag = block - source
            mask = same_segment(segments_ref, block, source)
            kernel_real = kernel_ref[lag, :FREQS] * mask
            kernel_imag = kernel_ref[lag, FREQS:] * mask
            value_real = spec_ref[source, :FREQS]
            value_imag = spec_ref[source, FREQS:]
            real = real + (kernel_real * value_real - kernel_imag * value_imag)
            imag = imag + (kernel_real * value_imag + kernel_imag * value_real)
        sums.append(jnp.concatenate([real, imag], axis=0))
    out = dot_plain(inverse_ref[...], three_parts(jnp.concatenate(sums, axis=1)))
    for block in range(blocks):
        out_ref[block * BLOCK : (block + 1) * BLOCK, :] = out[:, block * LANES : (block + 1) * LANES]


def conv_forward(segments, values, kernel, upper, inverse):
    tokens, channels = values.shape
    blocks = tokens // BLOCK
    return pl.pallas_call(
        conv_forward_body,
        grid=(channels // LANES,),
        in_specs=[
            pl.BlockSpec(memory_space=pltpu.SMEM),
            pl.BlockSpec((tokens, LANES), lambda i: (0, i)),
            pl.BlockSpec((blocks, 2 * FREQS, LANES), lambda i: (0, 0, i)),
            pl.BlockSpec(upper.shape, lambda i: (0, 0)),
            pl.BlockSpec(inverse.shape, lambda i: (0, 0)),
        ],
        out_specs=pl.BlockSpec((tokens, LANES), lambda i: (0, i)),
        out_shape=jax.ShapeDtypeStruct((tokens, channels), jnp.float32),
        scratch_shapes=[pltpu.VMEM((blocks, 2 * FREQS, LANES), jnp.float32)],
        compiler_params=pltpu.CompilerParams(vmem_limit_bytes=10 * MEBI),
        cost_estimate=pl.CostEstimate(
            flops=2000 * tokens * channels, bytes_accessed=16 * tokens * channels, transcendentals=0
        ),
        name="conv_forward",
    )(segments, values, kernel, upper, inverse)


def conv_backward_body(
    segments_ref,
    values_ref,
    grads_ref,
    kernel_ref,
    upper_ref,
    inverse_ref,
    lower_inverse_ref,
    out_ref,
    lags_ref,
    value_spec_ref,
    grad_spec_ref,
):
    blocks = kernel_ref.shape[0]
    for spec_ref, in_ref in ((value_spec_ref, values_ref), (grad_spec_ref, grads_ref)):
        keep_blocks(spec_ref, dot_plain(upper_ref[...], three_parts(beside(in_ref[...], blocks))))
    sums = []
    for source in range(blocks):
        real = jnp.zeros((FREQS, LANES), jnp.float32)
        imag = jnp.zeros((FREQS, LANES), jnp.float32)
        for block in range(source, blocks):
            lag = block - source
            mask = same_segment(segments_ref, block, source)
            kernel_real = kernel_ref[lag, :FREQS] * mask
            kernel_imag = kernel_ref[lag, FREQS:] * mask
            grad_real = grad_spec_ref[block, :FREQS]
            grad_imag = grad_spec_ref[block, FREQS:]
            real = real + (kernel_real * grad_real + kernel_imag * grad_imag)
            imag = imag + (kernel_real * grad_imag - kernel_imag * grad_real)
        sums.append(jnp.concatenate([real, imag], axis=0))
    out = dot_plain(inverse_ref[...], three_parts(jnp.concatenate(sums, axis=1)))
    for block in range(blocks):
        out_ref[block * BLOCK : (block + 1) * BLOCK, :] = out[:, block * LANES : (block + 1) * LANES]
    sums = []
    for lag in range(blocks):
        real = jnp.zeros((FREQS, LANES), jnp.float32)
        imag = jnp.zeros((FREQS, LANES), jnp.float32)
        for source in range(blocks - lag):
            block = source + lag
            mask = same_segment(segments_ref, block, source)
            grad_real = grad_spec_ref[block, :FREQS] * mask
            grad_imag = grad_spec_ref[block, FREQS:] * mask
            value_real = value_spec_ref[source, :FREQS]
            value_imag = value_spec_ref[source, FREQS:]
            real = real + (grad_real * value_real + grad_imag * value_imag)
            imag = imag + (grad_imag * value_real - grad_real * value_imag)
        sums.append(jnp.concatenate([real, imag], axis=0))
    parts = three_parts(jnp.concatenate(sums, axis=1))
    here = dot_plain(inverse_ref[...], parts)
    behind = dot_plain(lower_inverse_ref[...], parts)
    for lag in range(blocks):
        lags = here[:, lag * LANES : (lag + 1) * LANES]
        if lag + 1 < blocks:
            lags = lags + behind[:, (lag + 1) * LANES : (lag + 2) * LANES]
        lags_ref[lag * BLOCK : (lag + 1) * BLOCK, :] = lags


def conv_backward(segments, values, grads, kernel, upper, inverse, lower_inverse):
    tokens, channels = values.shape
    blocks = tokens // BLOCK
    shape = jax.ShapeDtypeStruct((tokens, channels), jnp.float32)
    tall = pl.BlockSpec((tokens, LANES), lambda i: (0, i))
    return pl.pallas_call(
        conv_backward_body,
        grid=(channels // LANES,),
        in_specs=[
            pl.BlockSpec(memory_space=pltpu.SMEM),
            tall,
            tall,
            pl.BlockSpec((blocks, 2 * FREQS, LANES), lambda i: (0, 0, i)),
            pl.BlockSpec(upper.shape, lambda i: (0, 0)),
            pl.BlockSpec(inverse.shape, lambda i: (0, 0)),
            pl.BlockSpec(lower_inverse.shape, lambda i: (0, 0)),
        ],
        out_specs=[tall, tall],
        out_shape=[shape, shape],
        scratch_shapes=[pltpu.VMEM((blocks, 2 * FREQS, LANES), jnp.float32)] * 2,
        compiler_params=pltpu.CompilerParams(vmem_limit_bytes=12 * MEBI),
        cost_estimate=pl.CostEstimate(
            flops=4000 * tokens * channels, bytes_accessed=24 * tokens * channels, transcendentals=0
        ),
        name="conv_backward",
    )(segments, values, grads, kernel, upper, inverse, lower_inverse)


def weight_grad_body(place_ref, first_ref, second_ref, *out_refs):
    width = out_refs[0].shape[-1]
    second = second_ref[...]
    turned = jnp.concatenate([second[:, width:], second[:, :width]], axis=1)
    second = jnp.where(place_ref[1] == 0, second, turned)
    rows = out_refs[0].shape[1]
    for part in range(len(out_refs) // 2):
        both = dot_first(first_ref[:, part * rows : (part + 1) * rows], second)
        out_refs[2 * part][0] = both[:, width:]
        out_refs[2 * part + 1][0] = both[:, :width]


def weight_grad(place, first, second, chips, parts=1):
    tokens, rows = first.shape
    pair = second.shape[1] // chips
    width = pair // 2
    out = jax.ShapeDtypeStruct((chips, rows // parts, width), jnp.float32)
    outs = pl.pallas_call(
        weight_grad_body,
        grid_spec=pltpu.PrefetchScalarGridSpec(
            num_scalar_prefetch=1,
            grid=(chips,),
            in_specs=[
                pl.BlockSpec((tokens, rows), lambda j, place: (0, 0)),
                pl.BlockSpec((tokens, pair), lambda j, place: (0, jnp.bitwise_xor(j, place[0]))),
            ],
            out_specs=[pl.BlockSpec((1, rows // parts, width), lambda j, place: (j, 0, 0))]
            * (2 * parts),
        ),
        out_shape=[out] * (2 * parts),
        compiler_params=pltpu.CompilerParams(vmem_limit_bytes=24 * MEBI),
        cost_estimate=pl.CostEstimate(
            flops=2 * tokens * rows * second.shape[1], bytes_accessed=4 * rows * second.shape[1], transcendentals=0
        ),
        name="weight_grad",
    )(place, first, second)
    return [(outs[2 * part], outs[2 * part + 1]) for part in range(parts)]


def far_grad_body(chip_ref, first_ref, second_ref, out_ref):
    rows, width = out_ref.shape[2:]
    for part in range(out_ref.shape[0] // 2):
        both = dot_first(first_ref[:, part * rows : (part + 1) * rows], second_ref[...])
        out_ref[2 * part, 0] = both[:, :width]
        out_ref[2 * part + 1, 0] = both[:, width:]


def far_grad(chip, first, second, chips, packs):
    tokens, rows = first.shape
    pair = second.shape[1] // chips
    shape = (2 * packs, chips, rows // packs, pair // 2)
    return pl.pallas_call(
        far_grad_body,
        grid_spec=pltpu.PrefetchScalarGridSpec(
            num_scalar_prefetch=1,
            grid=(chips,),
            in_specs=[
                pl.BlockSpec((tokens, rows), lambda j, chip: (0, 0)),
                pl.BlockSpec((tokens, pair), lambda j, chip: (0, jnp.bitwise_xor(j, chip[0]))),
            ],
            out_specs=pl.BlockSpec((shape[0], 1) + shape[2:], lambda j, chip: (0, j, 0, 0)),
        ),
        out_shape=jax.ShapeDtypeStruct(shape, jnp.float32),
        compiler_params=pltpu.CompilerParams(vmem_limit_bytes=24 * MEBI),
        cost_estimate=pl.CostEstimate(
            flops=2 * tokens * rows * second.shape[1], bytes_accessed=4 * rows * second.shape[1], transcendentals=0
        ),
        name="far_grad",
    )(chip, first, second)


def small_grad_body(place_ref, first_ref, normed_ref, readout_ref, gain_ref, bias_ref, rate_ref, send_ref, keep_ref):
    two = dot_first(first_ref[...], normed_ref[...])
    wide = jnp.concatenate([two, readout_ref[...]], axis=1)
    rows = wide.shape[0] // 2
    segment = gain_ref.shape[1] // 2
    rates = rate_ref[...]
    turned_rates = pltpu.roll(rates, rows, axis=1)
    spare = jnp.zeros((1, wide.shape[1] - 2 * segment - rates.shape[1]), jnp.float32)
    shares = []
    for core, rate in ((0, rates), (1, turned_rates)):
        part = slice(core * segment, (core + 1) * segment)
        line = jnp.concatenate([gain_ref[:, part], bias_ref[:, part], rate, spare], axis=1)
        shares.append(
            jnp.concatenate(
                [wide[core * rows : (core + 1) * rows], jnp.broadcast_to(line, (8, line.shape[1]))],
                axis=0,
            )
        )
    mine = place_ref[1] == 0
    keep_ref[0] = jnp.where(mine, shares[0], shares[1])
    send_ref[0] = jnp.where(mine, shares[1], shares[0])


def small_grad(place, first, normed, grad_readout, gain, bias, rate, chips):
    tokens, channels = first.shape
    width = normed.shape[1]
    pair = channels // chips
    states = grad_readout.shape[0] // chips

    def natural(j, place):
        return jnp.bitwise_xor(j, place[0])

    def turned(j, place):
        return lax.rem(natural(j, place) + place[1] * (chips // 2), chips)

    out = jax.ShapeDtypeStruct(
        (chips, pair // 2 + 8, width + grad_readout.shape[1]), jnp.float32
    )
    out_spec = pl.BlockSpec((1,) + out.shape[1:], lambda j, place: (j, 0, 0))
    gains = pl.BlockSpec((1, width // chips), lambda j, place: (0, natural(j, place)))
    return pl.pallas_call(
        small_grad_body,
        grid_spec=pltpu.PrefetchScalarGridSpec(
            num_scalar_prefetch=1,
            grid=(chips,),
            in_specs=[
                pl.BlockSpec((tokens, pair), lambda j, place: (0, natural(j, place))),
                pl.BlockSpec((tokens, width), lambda j, place: (0, 0)),
                pl.BlockSpec(
                    (states, grad_readout.shape[1]), lambda j, place: (turned(j, place), 0)
                ),
                gains,
                gains,
                pl.BlockSpec((1, states), lambda j, place: (0, turned(j, place))),
            ],
            out_specs=[out_spec, out_spec],
        ),
        out_shape=[out, out],
        compiler_params=pltpu.CompilerParams(vmem_limit_bytes=16 * MEBI),
        cost_estimate=pl.CostEstimate(
            flops=2 * tokens * channels * width, bytes_accessed=8 * 1024 * 1024, transcendentals=0
        ),
        name="small_grad",
    )(place, first, normed, grad_readout, gain, bias, rate)


GATE_TILE = 1024


def gate_forward_body(mixed_ref, weights_ref, gate_pre_ref, product_ref, bent_ref):
    lifted = dot_plain(mixed_ref[...], weights_ref[...])
    acts, slope = gelu_parts(gate_pre_ref[...])
    product_ref[...] = (acts * lifted).astype(jnp.bfloat16)
    bent_ref[...] = (slope * lifted).astype(jnp.bfloat16)


def gate_backward_body(low_ref, weights_ref, gate_pre_ref, bent_ref, lifted_ref, gate_ref):
    grads = dot_last(low_ref[...], weights_ref[...])
    acts = gelu(gate_pre_ref[...])
    lifted_ref[...] = (grads * acts).astype(jnp.bfloat16)
    gate_ref[...] = (grads * bent_ref[...]).astype(jnp.bfloat16)


def gate_early_body(low_ref, weights_ref, gate_pre_ref, lifted_ref, grads_ref):
    grads = dot_last(low_ref[...], weights_ref[...])
    lifted_ref[...] = (grads * gelu(gate_pre_ref[...])).astype(jnp.bfloat16)
    grads_ref[...] = grads.astype(jnp.bfloat16)


def gate_call(kernel, layer, left, weights, gated, upright, name):
    tokens, depth = left.shape
    gate = gated[0].shape[1]
    tile = pl.BlockSpec((tokens, GATE_TILE), lambda i: (0, i))
    if upright:
        weight_spec = pl.BlockSpec((None, GATE_TILE, depth), lambda i: (layer, i, 0))
    else:
        weight_spec = pl.BlockSpec((None, depth, GATE_TILE), lambda i: (layer, 0, i))
    out = jax.ShapeDtypeStruct((tokens, gate), jnp.bfloat16)
    return pl.pallas_call(
        kernel,
        grid=(gate // GATE_TILE,),
        in_specs=[pl.BlockSpec((tokens, depth), lambda i: (0, 0)), weight_spec]
        + [tile] * len(gated),
        out_specs=[tile, tile],
        out_shape=[out, out],
        compiler_params=pltpu.CompilerParams(vmem_limit_bytes=24 * MEBI),
        cost_estimate=pl.CostEstimate(
            flops=2 * tokens * depth * gate, bytes_accessed=2 * depth * gate + 10 * tokens * gate, transcendentals=0
        ),
        name=name,
    )(left, weights, *gated)


def flip_with(axis, bit):
    count = lax.axis_size(axis)
    pairs = [(device, device ^ bit) for device in range(count)]
    return lambda array: lax.ppermute(array, axis, pairs)


def by_core(core, zero, one):
    return jnp.where(core == 0, zero, one)


def prefix_join(prefix, partner, order, reach, factors):
    chips = factors.shape[0]
    places = jnp.arange(chips)
    start = (order // reach) * reach
    ahead = (places >= start) & (places < order)
    passed = jnp.prod(jnp.where(ahead[:, None], factors, 1.0), axis=0)
    return prefix + passed[:, None] * partner


def chip_scan_general(total, factors, order, chips):
    prefix = jnp.zeros_like(total)
    level = factors
    reach = 1
    while reach < chips:
        partner = flip_with("chip", reach)(total)
        group = order // reach
        sibling = lax.dynamic_index_in_dim(level, group ^ 1, 0, keepdims=False)
        mine = lax.dynamic_index_in_dim(level, group, 0, keepdims=False)
        late = (group % 2) == 1
        prefix = jnp.where(late, prefix_join(prefix, partner, order, reach, factors), prefix)
        total = jnp.where(late, mine[:, None] * partner + total, sibling[:, None] * total + partner)
        level = level[0::2] * level[1::2]
        reach *= 2
    return prefix


def column(table, index):
    return lax.dynamic_index_in_dim(table, index, 0, keepdims=False)[:, None]


class Carry:
    stages = 4

    def __init__(self, state, factors, order):
        half = state.shape[0] // 2
        self.half = half
        self.order = order
        self.square = factors.shape[0] == 8
        self.factors = factors[:, :half]
        self.chips = self.factors[0::2] * self.factors[1::2]
        self.own = state[:half]
        self.late = (order % 2) == 1
        self.swap = flip_with("core", 1)
        self.send(state[half:], self.swap)
        self.stage = 0

    def send(self, *pairs):
        self.operands = pairs[0::2]
        self.flight = tuple(way(array) for array, way in zip(pairs[0::2], pairs[1::2]))

    def go(self):
        self.stage += 1
        if self.stage == 1:
            self.total_of_chip()
            if self.square:
                self.first_round()
            else:
                entering = chip_scan_general(
                    self.total, self.chips, self.order // 2, self.chips.shape[0]
                )
                self.operands = self.flight = (entering,)
        elif self.stage == 2:
            if self.square:
                self.second_round()
        elif self.stage == 3:
            self.spread()
        else:
            self.operands = self.flight = (jnp.concatenate([self.keep, self.flight[0]], axis=0),)
        return self

    def total_of_chip(self):
        (received,) = self.flight
        self.early = jnp.where(self.late, received, self.own)
        after = jnp.where(self.late, self.own, received)
        last = self.order | 1
        self.early_factor = column(self.factors, last ^ 1)
        self.total = column(self.factors, last) * self.early + after

    def first_round(self):
        cut = self.half // 2
        self.along_x, self.along_y = flip_with("chip", 1), flip_with("chip", 2)
        self.first, self.second = self.total[:cut], self.total[cut:]
        self.send(self.first, self.along_x, self.second, self.along_y)

    def second_round(self):
        cut = self.half // 2
        place = self.order // 2
        self.place_x, self.place_y = place % 2, place // 2
        self.first_x, self.second_y = self.flight
        first_factors, second_factors = self.chips[:, :cut], self.chips[:, cut:]
        self.beside = column(first_factors, place ^ 1)
        row = jnp.where(
            self.place_x == 0,
            self.beside * self.first + self.first_x,
            column(first_factors, place) * self.first_x + self.first,
        )
        self.above, self.below = second_factors[1][:, None], second_factors[2][:, None]
        outgoing = jnp.where(
            self.place_y == 0,
            self.second,
            jnp.where(
                self.place_x == 0,
                self.below * self.above * self.second_y + self.second,
                self.second_y,
            ),
        )
        self.send(row, self.along_y, outgoing, self.along_x)

    def spread(self):
        if self.square:
            first_y, second_x = self.flight
            passed = jnp.where(self.place_x == 1, self.beside, 1.0)
            first = jnp.where(self.place_x == 1, self.first_x, 0.0) + jnp.where(
                self.place_y == 1, passed * first_y, 0.0
            )
            upper = jnp.where(self.place_x == 1, second_x, 0.0)
            lower = jnp.where(
                self.place_x == 0,
                self.above * self.second_y + second_x,
                second_x + self.below * self.second_y,
            )
            entering = jnp.concatenate([first, jnp.where(self.place_y == 0, upper, lower)], axis=0)
        else:
            (entering,) = self.flight
        middle = self.early_factor * entering + self.early
        self.keep = jnp.where(self.late, middle, entering)
        self.send(jnp.where(self.late, entering, middle), self.swap)

    def result(self):
        return self.flight[0]


class Share:
    def __init__(self, pair, along, line):
        self.pair = pair
        self.line = line
        rows = pair[1].shape[1]
        cut = {"x": rows, "y": 0}.get(along, rows // 16 * 8)
        self.parts = [
            part for part in ((slice(0, cut), 0), (slice(cut, rows), 1)) if part[0].stop > part[0].start
        ]
        self.operands = pair
        self.flight = (pair[0],)
        self.stage = -1

    def along_packs(self, array, pairs):
        self.operands = (array,)
        self.flight = (lax.ppermute(array, "blk", pairs),)

    def along_chips(self, arrays, step):
        self.operands = tuple(arrays)
        self.flight = tuple(
            flip_with("chip", 1 << (first ^ step))(array)
            for array, (_, first) in zip(arrays, self.parts)
        )

    def go(self):
        self.stage += 1
        getattr(self, "stage_%d" % self.stage)()
        return self

    def stage_0(self):
        self.operands = self.flight
        self.flight = (flip_with("core", 1)(self.operands[0]),)

    def stage_1(self):
        keep, (got,) = self.pair[1], self.flight
        self.got = got
        blocks = (slice(1, 4, 2), slice(2, 4))
        self.along_chips(
            [keep[blocks[y], rows] + got[blocks[y], rows] for rows, y in self.parts], 0
        )

    def stage_2(self):
        keep, got = self.pair[1], self.got
        self.first = self.flight
        self.along_chips(
            [
                keep[2 - y, rows] + got[2 - y, rows] + first[1]
                for (rows, y), first in zip(self.parts, self.first)
            ],
            1,
        )

    def stage_3(self):
        keep, got = self.pair[1], self.got
        sums = [
            keep[0, rows] + got[0, rows] + first[0] + second
            for (rows, _), first, second in zip(self.parts, self.first, self.flight)
        ]
        self.own = sums[0] if len(sums) == 1 else jnp.concatenate(sums, axis=0)
        if self.line:
            self.along_packs(self.own, [(0, 1), (3, 2)])
        else:
            self.operands = self.flight = (self.own,)
            self.stage = 6

    def stage_4(self):
        self.inner = self.own + self.flight[0]
        self.along_packs(self.inner, [(1, 2), (2, 1)])

    def stage_5(self):
        self.total = self.inner + self.flight[0]
        self.along_packs(self.total, [(1, 0), (2, 3)])

    def stage_6(self):
        place = lax.axis_index("blk")
        middle = (place == 1) | (place == 2)
        self.operands = self.flight = (jnp.where(middle, self.total, self.flight[0]),)

    def result(self):
        while self.stage < 6:
            self.go()
        return self.flight[0]


class FarShare:
    def __init__(self, array):
        self.operands = self.flight = (array,)
        self.cut = array.shape[2] // 16 * 8
        self.stage = -1

    def go(self):
        self.stage += 1
        getattr(self, "stage_%d" % self.stage)()
        return self

    def along_chips(self, first, second, bits):
        self.operands = (first, second)
        self.flight = tuple(
            flip_with("chip", bit)(array) for array, bit in zip(self.operands, bits)
        )

    def stage_0(self):
        self.operands = self.flight
        self.flight = (
            lax.psum_scatter(
                self.operands[0], ("blk", "core"), scatter_dimension=0, tiled=True
            ),
        )

    def stage_1(self):
        self.blocks = self.flight[0][0]
        self.along_chips(self.blocks[1::2, : self.cut], self.blocks[2:, self.cut :], (1, 2))

    def stage_2(self):
        self.first, self.second = self.flight
        self.along_chips(
            self.blocks[2, : self.cut] + self.first[1],
            self.blocks[1, self.cut :] + self.second[1],
            (2, 1),
        )

    def stage_3(self):
        first, second = self.flight
        own = jnp.concatenate(
            [
                self.blocks[0, : self.cut] + self.first[0] + first,
                self.blocks[0, self.cut :] + self.second[0] + second,
            ],
            axis=0,
        )
        self.operands = (own,)
        self.flight = (lax.all_gather(own, "blk", axis=0, tiled=True),)

    def stage_4(self):
        self.operands = self.flight

    def result(self):
        return self.flight[0]


class WholeShare:
    def __init__(self, array, axis):
        self.operands = (array,)
        self.flight = (lax.psum_scatter(array, ("chip", "core"), scatter_dimension=axis, tiled=True),)

    def go(self):
        self.operands = ()
        return self

    def result(self):
        return self.flight[0]


def sum_packs(*shares):
    for share, total in zip(shares, lax.psum([share.flight[0] for share in shares], "blk")):
        share.flight = (total,)


class Bag:
    def __init__(self, **members):
        self.__dict__.update(members)


class Sequence:
    def __init__(self):
        self.last = ()

    def __call__(self, step, *arrays):
        arrays, _ = lax.optimization_barrier((arrays, self.last))
        results = step(*arrays)
        self.last = results
        return results

    def move(self, *items):
        for item in items:
            item.flight, _ = lax.optimization_barrier((item.flight, self.last))
            item.go()
            self.last = item.operands

    def wait(self, *items):
        for item in items:
            item.flight, _ = lax.optimization_barrier((item.flight, self.last))
            self.last = item.flight


def gelu_parts(inputs):
    square = inputs * inputs
    bent = jnp.tanh(GELU_SCALE * inputs * (1.0 + GELU_CUBE * square))
    half = 0.5 * (1.0 + bent)
    slope = half + 0.5 * inputs * (1.0 - bent * bent) * GELU_SCALE * (
        1.0 + 3.0 * GELU_CUBE * square
    )
    return inputs * half, slope


def gelu(inputs):
    return gelu_parts(inputs)[0]


def body(
    tokens,
    seq_lengths,
    ln_gain,
    ln_bias,
    w_one,
    w_two,
    w_three,
    w_four,
    readout,
    log_rate,
    cotangent,
):
    _, span, width = tokens.shape
    layers = w_one.shape[0]
    channels, states = readout.shape[1:]
    blocks = span // BLOCK
    chips = lax.axis_size("chip")
    devices = 2 * chips
    me = lax.axis_index(("chip", "core"))
    core = me % 2
    chip = me // 2
    custom = chips == 4 and lax.axis_size("blk") == 4
    upper, window, inverse, lower_inverse = fourier_tables()

    finish = jnp.cumsum(seq_lengths[0])
    begins = finish - seq_lengths[0]
    places = BLOCK * jnp.arange(devices * blocks, dtype=jnp.int32)
    opens = jnp.any(begins[:, None] == places[None, :], axis=0).reshape(devices, blocks)
    unbroken = jnp.logical_not(jnp.any(opens, axis=1))
    own_opens = lax.dynamic_index_in_dim(opens, me, 0, keepdims=False)
    segments = jnp.cumsum(own_opens.astype(jnp.int32))
    from_before = jnp.repeat((segments == 0).astype(jnp.float32), BLOCK)
    to_after = jnp.repeat((segments == segments[-1]).astype(jnp.float32), BLOCK)
    unbroken = unbroken.astype(jnp.float32)
    own_unbroken = (segments[-1] == 0).astype(jnp.float32)

    half = states // 2

    def turned(array):
        return by_core(core, array, jnp.concatenate([array[half:], array[:half]], axis=0))

    steps = jnp.arange(span, dtype=jnp.float32)

    def tables(layer):
        rates = jnp.exp(log_rate[layer])
        col = turned(rates)[:, None]
        row = turned(rates)[None, :]
        across, down = steps[None, :], steps[:, None]
        before_row, before_col = from_before[None, :], from_before[:, None]
        after_row, after_col = to_after[None, :], to_after[:, None]

        def low(array):
            return array.astype(jnp.bfloat16)

        return Bag(
            rates=rates,
            turned_factor=turned(rates * jnp.exp(-rates)),
            retain=-jnp.expm1(-rates),
            retain_column=-jnp.expm1(-col),
            leaving=low(after_row * jnp.exp((across - (span - 1.0)) * col)),
            leaving_down=low(after_col * jnp.exp((down - (span - 1.0)) * row)),
            leaving_slopes=low(
                after_row * (span - 1.0 - across) * jnp.exp((across - (span - 2.0)) * col)
            ),
            entering=low(before_row * jnp.exp(-(across + 1.0) * col)),
            entering_down=low(before_col * jnp.exp(-(down + 1.0) * row)),
            entering_slopes=low(before_row * (across + 1.0) * jnp.exp(-across * col)),
            powers=low(jnp.exp(-across * col)),
            slopes=low(across * jnp.exp(-(across - 1.0) * col)),
            through_slope=own_unbroken * span * jnp.exp(-(span - 1.0) * col),
            factors=unbroken[:, None] * jnp.exp(-span * row),
        )

    def layer_tables(layer, table):
        def made(readout, row, retain):
            upright, kernel = layer_kernel(layer, core[None], readout, row, retain, window, span)
            return upright, kernel

        return made, readout, table.rates[None], table.retain[None]

    def low_dot(first, second):
        return dot_plain(first, second.astype(jnp.bfloat16))

    def open_layer(layer, flat, table):
        mean = jnp.mean(flat, axis=-1, keepdims=True)
        center = flat - mean
        scale = lax.rsqrt(jnp.mean(center * center, axis=-1, keepdims=True) + 1e-05)
        normed = (center * scale * ln_gain[layer] + ln_bias[layer]).astype(jnp.bfloat16)
        value_pre = dot_plain(normed, w_two[layer])
        values = gelu(value_pre)
        state = low_dot(table.leaving, values)
        return mean, scale, normed, value_pre, values, state

    def share_of(name, pair):
        along = "x" if name in ALONG_X else "y" if name in ALONG_Y else "both"
        return Share(pair, along, not any(name in group for group in GROUPS))

    def share_grad(names, first, second):
        if custom and names[0] in FAR:
            made = sequence(
                lambda first, second: far_grad(
                    chip[None], first, second, chips, lax.axis_size("blk")
                ),
                first,
                second,
            )
            return [FarShare(made)]
        if custom:
            place = jnp.stack([chip, core])
            made = sequence(
                lambda first, second: weight_grad(place, first, second, chips, len(names)),
                first,
                second,
            )
            return [share_of(name, pair) for name, pair in zip(names, made)]
        return [
            WholeShare(sequence(dot_first, piece, second), 1)
            for piece in jnp.split(first, len(names), axis=1)
        ]

    def small_lines(two, grad_readout, gain_grad, bias_grad, grad_rate):
        def lines(array):
            return array.reshape(devices, -1, array.shape[-1])

        extra = jnp.concatenate(
            [part.reshape(devices, 1, -1) for part in (gain_grad, bias_grad, grad_rate)], axis=-1
        )
        wide = jnp.concatenate([lines(two), lines(grad_readout)], axis=-1)
        extra = jnp.pad(extra, ((0, 0), (0, 7), (0, wide.shape[-1] - extra.shape[-1])))
        return jnp.concatenate([wide, extra], axis=1)

    def small_share(name, first, second):
        if not custom:
            return WholeShare(jnp.concatenate([first, second], axis=1), 0)
        return share_of(
            name,
            tuple(jnp.concatenate(pair, axis=1) for pair in zip(first, second)),
        )

    def close_layer(layer, upstream, flat, mean, scale, grad_gate_pre, grad_value_pre):
        grad_normed = dot_last(grad_gate_pre, w_one[layer]) + dot_last(
            grad_value_pre, w_two[layer]
        )
        hat = (flat - mean) * scale
        gain_grad = jnp.sum(grad_normed * hat, axis=0)
        bias_grad = jnp.sum(grad_normed, axis=0)
        scaled = grad_normed * ln_gain[layer]
        grad_flat = upstream + scale * (
            scaled
            - jnp.mean(scaled, axis=-1, keepdims=True)
            - hat * jnp.mean(scaled * hat, axis=-1, keepdims=True)
        )
        return grad_flat, gain_grad, bias_grad

    def kernel_grads(
        table, upright, lag_sums, incoming, adjoint, pulled, grad_mixed, values
    ):
        mixing = upright * table.retain_column
        grad_mixing = low_dot(table.powers, lag_sums) + incoming * pulled
        grad_decays = jnp.sum(
            mixing
            * (
                low_dot(table.slopes, lag_sums)
                + incoming * low_dot(table.entering_slopes, grad_mixed)
            )
            + adjoint * low_dot(table.leaving_slopes, values)
            + table.through_slope * incoming * adjoint,
            axis=1,
        )
        grad_retain = jnp.sum(grad_mixing * upright, axis=1)
        grad_rate = table.turned_factor * (grad_retain - grad_decays)
        return grad_mixing * table.retain_column, grad_rate

    back_order = devices - 1 - me
    sequence = Sequence()
    move = sequence.move

    def start_carry(state, factors, order):
        carried = Carry(state, factors, order)
        sequence.last = carried.operands
        return carried

    def mix(local, table, upright, incoming):
        scaled = upright * table.retain_column * incoming
        return (local + low_dot(table.entering_down, scaled)).astype(jnp.bfloat16)

    def pull(grad_lifted, table, upright, layer):
        grad_mixed = dot_last(grad_lifted, w_three[layer])
        pulled = low_dot(table.entering, grad_mixed)
        return grad_mixed, pulled, upright * table.retain_column * pulled

    def gate_forward(layer, mixed, gate_pre):
        return gate_call(
            gate_forward_body, layer, mixed, w_three, (gate_pre,), False, "gate_forward"
        )

    def value_grad(table, local, adjoint, value_pre):
        grad_values = local + low_dot(table.leaving_down, adjoint)
        return (grad_values * gelu_parts(value_pre)[1]).astype(jnp.bfloat16)

    def small_grads(table, upright, grad_value_pre, normed, sums, gain_grad, bias_grad):
        def made(grad_value_pre, normed, gain_grad, bias_grad, *sums):
            two = dot_first(grad_value_pre, normed)
            grad_readout, grad_rate = kernel_grads(table, upright, *sums)
            return small_lines(
                two, turned(grad_readout), gain_grad, bias_grad, turned(grad_rate)
            )

        def made_pair(grad_value_pre, normed, gain_grad, bias_grad, *sums):
            grad_readout, grad_rate = kernel_grads(table, upright, *sums)
            place = jnp.stack([chip, core])
            return small_grad(
                place,
                grad_value_pre,
                normed,
                grad_readout,
                gain_grad[None],
                bias_grad[None],
                grad_rate[None],
                chips,
            )

        if custom:
            return sequence(made_pair, grad_value_pre, normed, gain_grad, bias_grad, *sums)

        return sequence(made, grad_value_pre, normed, gain_grad, bias_grad, *sums)

    conv_tables = (upper, inverse)
    back_tables = (upper, inverse, lower_inverse)

    flat0 = tokens.reshape(span, width)
    t0 = tables(0)
    t1 = tables(1)
    mean0, scale0, normed0, value_pre0, values0, state0 = open_layer(0, flat0, t0)
    c0 = start_carry(state0, t0.factors, me)
    upright0, kernel0 = sequence(*layer_tables(0, t0))
    move(c0)
    gate_pre0 = sequence(lambda normed: dot_plain(normed, w_one[0]), normed0)
    move(c0)
    local0 = sequence(conv_forward, segments, values0, kernel0, *conv_tables)
    upright1, kernel1 = sequence(*layer_tables(1, t1))
    move(c0, c0)
    mixed0 = sequence(lambda *arrays: mix(arrays[0], t0, *arrays[1:]), local0, upright0, c0.result())
    product0, bent0 = sequence(functools.partial(gate_forward, 0), mixed0, gate_pre0)
    flat1 = flat0 + dot_plain(product0, w_four[0])

    mean1, scale1, normed1, value_pre1, values1, state1 = open_layer(1, flat1, t1)
    c1 = start_carry(state1, t1.factors, me)
    gate_pre1 = sequence(lambda normed: dot_plain(normed, w_one[1]), normed1)
    move(c1)
    low_cotangent = cotangent.reshape(span, width).astype(jnp.bfloat16)
    grad_lifted1, grad_product1 = sequence(
        lambda low, gate_pre: gate_call(
            gate_early_body, 1, low, w_four, (gate_pre,), True, "gate_early"
        ),
        low_cotangent,
        gate_pre1,
    )
    move(c1)
    grad_mixed1, pulled1, leaving1 = sequence(
        lambda grad_lifted, upright: pull(grad_lifted, t1, upright, 1), grad_lifted1, upright1
    )
    b1 = start_carry(leaving1, t1.factors[::-1], back_order)
    local1 = sequence(conv_forward, segments, values1, kernel1, *conv_tables)
    move(c1, b1, c1)
    incoming1 = c1.result()
    mixed1 = sequence(lambda *arrays: mix(arrays[0], t1, *arrays[1:]), local1, upright1, incoming1)
    v = Bag()
    items = dict(b1=b1)

    def shares(names, first, second):
        names = names.split()
        items.update(zip(names, share_grad(names, first, second)))

    def gate1():
        v.product1, v.bent1 = sequence(
            functools.partial(gate_forward, 1), mixed1, gate_pre1
        )

    def conv1():
        v.gv1, v.lags1 = sequence(
            conv_backward, segments, values1, grad_mixed1, kernel1, *back_tables
        )

    def slope1():
        v.grad_gate1 = sequence(jnp.multiply, grad_product1, v.bent1)

    def value1():
        v.adjoint1 = items["b1"].result()
        v.grad_value1 = sequence(
            lambda *arrays: value_grad(t1, *arrays), v.gv1, v.adjoint1, value_pre1
        )

    def close1():
        v.upstream0, v.gain1, v.bias1 = sequence(
            functools.partial(close_layer, 1),
            cotangent.reshape(span, width),
            flat1,
            mean1,
            scale1,
            v.grad_gate1,
            v.grad_value1,
        )
        v.low0 = v.upstream0.astype(jnp.bfloat16)

    def gate0():
        v.grad_lifted0, v.grad_gate0 = sequence(
            lambda low, gate_pre, bent: gate_call(
                gate_backward_body, 0, low, w_four, (gate_pre, bent), True, "gate_backward"
            ),
            v.low0,
            gate_pre0,
            bent0,
        )

    def pull0():
        v.grad_mixed0, v.pulled0, leaving0 = sequence(
            lambda grad_lifted, upright: pull(grad_lifted, t0, upright, 0),
            v.grad_lifted0,
            upright0,
        )
        items["b0"] = start_carry(leaving0, t0.factors[::-1], back_order)

    def conv0():
        v.gv0, v.lags0 = sequence(
            conv_backward, segments, values0, v.grad_mixed0, kernel0, *back_tables
        )

    def value0():
        v.adjoint0 = items["b0"].result()
        v.grad_value0 = sequence(
            lambda *arrays: value_grad(t0, *arrays), v.gv0, v.adjoint0, value_pre0
        )

    def close0():
        v.grad_tokens, v.gain0, v.bias0 = sequence(
            functools.partial(close_layer, 0),
            v.upstream0,
            flat0,
            mean0,
            scale0,
            v.grad_gate0,
            v.grad_value0,
        )

    def lines1():
        sums = (v.lags1, incoming1, v.adjoint1, pulled1, grad_mixed1, values1)
        v.lines1 = small_grads(
            t1, upright1, v.grad_value1, normed1, sums, v.gain1, v.bias1
        )

    def lines0():
        sums = (v.lags0, c0.result(), v.adjoint0, v.pulled0, v.grad_mixed0, values0)
        v.lines0 = small_grads(
            t0, upright0, v.grad_value0, normed0, sums, v.gain0, v.bias0
        )

    def small():
        items["small"] = small_share("small", v.lines0, v.lines1)
        sequence.last = items["small"].operands

    def result():
        v.result = sequence(
            lambda flat, product: flat + dot_plain(product, w_four[1]), flat1, v.product1
        )

    actions = dict(
        gate1=gate1,
        conv1=conv1,
        slope1=slope1,
        value1=value1,
        close1=close1,
        gate0=gate0,
        pull0=pull0,
        conv0=conv0,
        value0=value0,
        close0=close0,
        lines1=lines1,
        lines0=lines0,
        lines=small,
        result=result,
        grad_three1=lambda: shares("three1", mixed1, grad_lifted1),
        grad_four1=lambda: shares(PARTS[0], v.product1, low_cotangent),
        grad_one1=lambda: shares(PARTS[1], normed1, v.grad_gate1),
        grad_four0=lambda: shares(PARTS[2], product0, v.low0),
        grad_one0=lambda: shares(PARTS[3], normed0, v.grad_gate0),
        grad_three0=lambda: shares("three0", mixed0, v.grad_lifted0),
    )
    for name in (NAMES[index] for index in ORDER):
        if name in actions:
            actions[name]()
        elif name[0] == "~":
            sequence.wait(items[name[1:]])
        else:
            move(items[name])
    if not custom:
        sum_packs(*[item for item in items.values() if isinstance(item, WholeShare)])
    flat, upstream = v.result, v.grad_tokens

    def whole(*names):
        return jnp.concatenate([items[name].result() for name in names], axis=0)

    collected = []
    lines = items["small"].result()
    lines = jnp.split(lines if custom else lines[0], 2, axis=0)
    for layer, small_rows in zip("01", lines):
        collected.append(
            [
                whole(*PARTS[2 - 2 * int(layer)].split()),
                whole("three" + layer),
                whole(*PARTS[3 - 2 * int(layer)].split()),
                small_rows,
            ]
        )

    def unpack(shares):
        four, three, one, small = shares
        rows = small.shape[0] - 8
        gains = width // devices
        rate_width = states // devices
        return (
            small[rows, :gains],
            small[rows, gains : 2 * gains],
            one,
            small[:rows, :width].T,
            three,
            four,
            small[:rows, width:].T,
            small[rows, 2 * gains : 2 * gains + rate_width],
        )

    parts = [unpack(shares) for shares in collected]
    stacked = [jnp.stack([part[member] for part in parts]) for member in range(8)]
    return (flat[None], upstream[None], *stacked)


def solution(mesh):
    packs = mesh.shape["blk"]
    mesh = jax.sharding.Mesh(mesh.devices.reshape(-1, 2, packs), SEQ + ("blk",))
    placed = (
        P("blk", SEQ, None),
        P("blk", None),
        P(),
        P(),
        P(),
        P(),
        P(),
        P(),
        P(),
        P(),
        P("blk", SEQ, None),
    )
    return jax.shard_map(
        body,
        mesh=mesh,
        in_specs=placed,
        out_specs=(
            P("blk", SEQ, None),
            P("blk", SEQ, None),
            P(None, SEQ),
            P(None, SEQ),
            P(None, None, SEQ),
            P(None, None, SEQ),
            P(None, None, SEQ),
            P(None, None, SEQ),
            P(None, None, SEQ),
            P(None, SEQ),
        ),
        check_vma=False,
    )
```
